32 devices in a mesh: replica: 4 (over y, x), shard: 8 (over z, core).
Axes of the slice: x: 2, y: 2, z: 4, core: 2. Of those that a mesh axis runs over, the one named last changes fastest.
Arguments:
- master_weight: float32 [8, 1024, 4096], P(None, 'replica', 'shard'), may hold values from -0.1875 to 0.1875
- gradient: bfloat16 [8, 1024, 4096], P(None, 'replica', 'shard'), may hold values from -6 to 6
- first_moment: bfloat16 [8, 1024, 4096], P(None, 'replica', 'shard'), may hold values from -1.796875 to 1.796875
- second_moment: bfloat16 [8, 1024, 4096], P(None, 'replica', 'shard'), may hold values from 0.049804688 to 2
- hidden: bfloat16 [4, 8, 384, 1024], P('replica', 'shard'), may hold values from -6 to 6
- owner_of_expert: int32 [8], replicated, may hold values from 0 to 7, each once
- slab_order: int32 [4], replicated, may hold values from 0 to 3, each once
Outputs:
- new_master: float32 [8, 1024, 4096], P(None, 'replica', 'shard')
- new_first: bfloat16 [8, 1024, 4096], P(None, 'replica', 'shard')
- new_second: bfloat16 [8, 1024, 4096], P(None, 'replica', 'shard')
- expert_out: bfloat16 [4, 8, 384, 4096], P('replica', 'shard')
The draws below stay inside these ranges and needn't reach their ends.
Inputs may be any that keep to these rules, and one draw needn't show every extreme that they name: `owner_of_expert`: a permutation: every owner holds exactly one expert. A permutation: row slab j of the learner's arrays holds hidden units from slab_order[j] * 256 on.
All inputs are finite; a program needn't handle non-finite values.
Results may differ from the reference program's by a relative error of at most 0.0049.
Values may be sent and summed in bfloat16 or wider, within the bound.
No kernel may reach another device: no remote copies, remote signals or barrier semaphores. Data moves between devices by JAX's collectives and lax.ppermute only.
A program may use at most 128 MiB of HBM per device.

```python
import math
import jax
import jax.numpy as jnp
from jax import lax

D = 4096
FFW = 1024
QB = 128
TOK_DEV = 384
EXPERTS = 8
REPLICAS = 4


def block_levels(stream_key, shape, pieces, least, high):
    gain, own = 1.0, jax.random.fold_in(stream_key, 6)
    for axis_at, shards_of in pieces:
        steps = jnp.exp(jax.random.uniform(jax.random.fold_in(own, axis_at), (shards_of,), jnp.float32, least / len(pieces), high / len(pieces)))
        gain = gain * jnp.repeat(steps, shape[axis_at] // shards_of).reshape([-1 if axis == axis_at else 1 for axis in range(len(shape))])
    return gain


def gaussian(key, dims, spread, most, shards=(), held_as=jnp.bfloat16):
    factor_of = block_levels(key, dims, shards, -0.22, 0.18) if shards else 1.0
    array = jax.random.normal(key, dims, jnp.float32) * spread * factor_of
    return jnp.minimum(jnp.maximum(array, -most), most).astype(held_as)


def setup_inputs(seed: int = 0) -> dict:
    arg_keys = jax.random.split(jax.random.key(seed), 8)
    return {
        "master_weight": gaussian(arg_keys[0], (EXPERTS, FFW, D), FFW ** -0.5, 0.1875, ((1, 4), (2, 8)), jnp.float32),
        "gradient": gaussian(arg_keys[1], (EXPERTS, FFW, D), 1.0, 6.0, ((1, 4), (2, 8))),
        "first_moment": gaussian(arg_keys[2], (EXPERTS, FFW, D), 0.3, 1.796875, ((1, 4), (2, 8))),
        "second_moment": jnp.clip(jnp.exp(math.log(2.0) - 3.6927934 * jax.random.uniform(arg_keys[3], (EXPERTS, FFW, D), jnp.float32) ** block_levels(arg_keys[3], (EXPERTS, FFW, D), ((1, 4), (2, 8)), -0.2, 0.2)), 0.049804688, 2.0).astype(jnp.bfloat16),
        "hidden": gaussian(arg_keys[4], (REPLICAS, EXPERTS, TOK_DEV, FFW), 1.0, 6.0, ((0, 4), (1, 8))),
        "owner_of_expert": jax.random.permutation(arg_keys[5], EXPERTS).astype(jnp.int32),
        "slab_order": jax.random.permutation(arg_keys[6], REPLICAS).astype(jnp.int32),
    }


beta_one = 0.9
beta_two = 0.95
learn_rate = 0.004
adam_epsilon = 1e-08
step_count = 10.0
quant_limit = 448.0
scale_epsilon = 1e-06

def adam_step(master_weight, gradient, first_moment, second_moment):
    float_gradient = gradient.astype(jnp.float32)
    moment_one = beta_one * first_moment.astype(jnp.float32) + (1.0 - beta_one) * float_gradient
    moment_two = beta_two * second_moment.astype(jnp.float32) + (1.0 - beta_two) * float_gradient * float_gradient
    first_fix = 1.0 - beta_one ** step_count
    second_fix = 1.0 - beta_two ** step_count
    update = moment_one / first_fix / (jnp.sqrt(moment_two / second_fix) + adam_epsilon)
    return (master_weight - learn_rate * update, moment_one, moment_two)

def quantize(weights):
    number, height, breadth = weights.shape
    blocks = weights.reshape(number, height // QB, QB, breadth // QB, QB)
    largest = lax.optimization_barrier(jnp.max(jnp.abs(blocks), axis=(2, 4)))
    block_scale = ((largest + scale_epsilon) / quant_limit).astype(jnp.bfloat16)
    block_scale = lax.optimization_barrier(block_scale)
    divided = blocks / block_scale.astype(jnp.float32)[:, :, None, :, None]
    return (divided.astype(jnp.bfloat16).reshape(number, height, breadth), block_scale)

def scaled_product(summed, left_part, quant_rows, scale_rows):
    token_count = left_part.shape[0]
    breadth = quant_rows.shape[1]
    for row_block in range(scale_rows.shape[0]):
        partial_value = jnp.dot(left_part[:, row_block * QB:(row_block + 1) * QB], quant_rows[row_block * QB:(row_block + 1) * QB], preferred_element_type=jnp.float32)
        factor = scale_rows[row_block].astype(jnp.float32)
        summed = summed + (partial_value.reshape(token_count, breadth // QB, QB) * factor[None, :, None]).reshape(token_count, breadth)
    return summed

def reference(master_weight, gradient, first_moment, second_moment, hidden, owner_of_expert, slab_order):
    updated, moment_one, moment_two = adam_step(master_weight, gradient, first_moment, second_moment)
    quantized, block_scale = quantize(updated)
    experts = quantized.shape[0]
    replicas = slab_order.shape[0]
    unit_count = quantized.shape[1]
    slab_rows = unit_count // replicas
    tokens = hidden.shape[2]
    places = jnp.arange(experts, dtype=jnp.int32)
    held_expert = lax.optimization_barrier(jnp.sum(jnp.where(owner_of_expert[None, :] == places[:, None], places[None, :], 0), axis=1)).astype(jnp.int32)
    ordered = hidden.reshape(replicas, experts, tokens, replicas, slab_rows)[:, :, :, slab_order, :]
    ordered = ordered.reshape(replicas, experts, tokens, unit_count)

    def one_owner(owner_index):
        expert = held_expert[owner_index]
        expert_quant = quantized[expert]
        expert_scale = block_scale[expert]
        left_part = ordered[:, owner_index].reshape(replicas * tokens, unit_count)
        zero_sum = jnp.zeros((replicas * tokens, expert_quant.shape[1]), jnp.float32)
        return scaled_product(zero_sum, left_part, expert_quant, expert_scale).astype(jnp.bfloat16)
    results = lax.map(one_owner, places)
    expert_out = results.reshape(experts, replicas, tokens, results.shape[-1]).transpose(1, 0, 2, 3)
    return (updated, moment_one.astype(jnp.bfloat16), moment_two.astype(jnp.bfloat16), expert_out)
```

```python
import functools

import jax
import jax.numpy as jnp
from jax import lax
from jax.experimental import pallas as pl
from jax.experimental.pallas import tpu as pltpu
from jax.sharding import PartitionSpec as P

QB = 128

beta_one = 0.9
beta_two = 0.95
learn_rate = 0.004
adam_epsilon = 1e-08
step_count = 10.0
quant_limit = 448.0
scale_epsilon = 1e-06
first_fix = 1.0 - beta_one**step_count
second_fix = 1.0 - beta_two**step_count


def adam_kernel(experts, owner, master, gradient, first, second, *refs):
    new_master, new_first, new_second, send = refs[-4:]

    def one_expert(expert, carry):
        grad = gradient[expert].astype(jnp.float32)
        moment_one = beta_one * first[expert].astype(jnp.float32) + (1.0 - beta_one) * grad
        moment_two = beta_two * second[expert].astype(jnp.float32) + (1.0 - beta_two) * grad * grad
        scaled = moment_two * (1.0 / second_fix)
        root = scaled * lax.rsqrt(scaled)
        updated = master[expert] - (learn_rate / first_fix) * moment_one / (root + adam_epsilon)
        new_master[expert] = updated
        new_first[expert] = moment_one.astype(jnp.bfloat16)
        new_second[expert] = moment_two.astype(jnp.bfloat16)
        largest = jnp.max(jnp.abs(updated), axis=(0, 1), keepdims=True)
        scale = ((largest + scale_epsilon) * (1.0 / quant_limit)).astype(jnp.bfloat16)
        scale = jnp.broadcast_to(scale.astype(jnp.float32), (1, QB))
        quantized = (updated * (1.0 / scale)).astype(jnp.bfloat16)
        send[owner[expert]] = (quantized.astype(jnp.float32) * scale).astype(jnp.bfloat16)
        return carry

    lax.fori_loop(0, experts, one_expert, 0)


def adam_chunk(chunk, owner, arrays, carried):
    experts, rows, columns = arrays[0].shape
    block = (experts, QB, QB)
    here = pl.BlockSpec(block, lambda i, owner: (0, i, chunk))
    sent = pl.BlockSpec(block, lambda i, owner: (0, i, 0))
    whole = pl.BlockSpec(memory_space=pl.ANY)
    shapes = [
        jax.ShapeDtypeStruct(arrays[0].shape, jnp.float32),
        jax.ShapeDtypeStruct(arrays[0].shape, jnp.bfloat16),
        jax.ShapeDtypeStruct(arrays[0].shape, jnp.bfloat16),
        jax.ShapeDtypeStruct((experts, rows, QB), jnp.bfloat16),
    ]
    count = experts * rows * QB
    return pl.pallas_call(
        functools.partial(adam_kernel, experts),
        grid_spec=pltpu.PrefetchScalarGridSpec(
            num_scalar_prefetch=1,
            grid=(rows // QB,),
            in_specs=[here] * 4 + [whole] * len(carried),
            out_specs=[here] * 3 + [sent],
        ),
        out_shape=shapes,
        input_output_aliases={5 + i: i for i in range(len(carried))},
        compiler_params=pltpu.CompilerParams(vmem_limit_bytes=48 * 1024 * 1024),
        cost_estimate=pl.CostEstimate(flops=30 * count, bytes_accessed=20 * count, transcendentals=2 * count),
        name="adam_quantize",
    )(owner, *arrays, *carried)


def product_kernel(order, left, right, *refs):
    out = refs[-1]
    slabs, _, slab_rows, breadth = right.shape
    total = jnp.zeros(out.shape, jnp.float32)
    for slab in range(slabs):
        place = pl.multiple_of(order[slab] * slab_rows, QB)
        total += jnp.dot(
            left[:, pl.ds(place, slab_rows)], right[slab, 0], preferred_element_type=jnp.float32
        )
    out[...] = total.astype(out.dtype)


def product_chunk(chunk, chunks, order, token_rows, gathered, carried):
    slabs, sources, slab_rows, _ = gathered.shape
    tokens, units = token_rows.shape
    shape = (tokens, sources * chunks * QB)
    return pl.pallas_call(
        product_kernel,
        grid_spec=pltpu.PrefetchScalarGridSpec(
            num_scalar_prefetch=1,
            grid=(sources,),
            in_specs=[
                pl.BlockSpec((tokens, units), lambda s, order: (0, 0)),
                pl.BlockSpec((slabs, 1, slab_rows, QB), lambda s, order: (0, s, 0, 0)),
            ]
            + [pl.BlockSpec(memory_space=pl.ANY)] * len(carried),
            out_specs=pl.BlockSpec((tokens, QB), lambda s, order: (0, s * chunks + chunk)),
        ),
        out_shape=jax.ShapeDtypeStruct(shape, jnp.bfloat16),
        input_output_aliases={3: 0} if carried else {},
        compiler_params=pltpu.CompilerParams(vmem_limit_bytes=48 * 1024 * 1024),
        cost_estimate=pl.CostEstimate(
            flops=2 * tokens * units * sources * QB,
            bytes_accessed=2 * (units * sources * QB + tokens * units + tokens * sources * QB),
            transcendentals=0,
        ),
        name="expert_product",
    )(order, token_rows, gathered, *carried)


def body(master_weight, gradient, first_moment, second_moment, hidden, owner_of_expert, slab_order):
    arrays = (master_weight, gradient, first_moment, second_moment)
    chunks = master_weight.shape[2] // QB
    token_rows = hidden.reshape(hidden.shape[2:])
    carried = ()
    sends = []
    for chunk in range(chunks):
        *carried, send = adam_chunk(chunk, owner_of_expert, arrays, tuple(carried))
        sends.append(send)
    out = ()
    for chunk in range(chunks):
        received = lax.all_to_all(sends[chunk], "shard", split_axis=0, concat_axis=0, tiled=True)
        gathered = lax.all_gather(received, "replica", axis=0)
        out = (product_chunk(chunk, chunks, slab_order, token_rows, gathered, out),)
    return (*carried, out[0].reshape(hidden.shape[:2] + out[0].shape))


def solution(mesh):
    weights = P(None, "replica", "shard")
    tokens = P("replica", "shard", None, None)
    return jax.shard_map(
        body,
        mesh=mesh,
        in_specs=(weights, weights, weights, weights, tokens, P(), P()),
        out_specs=(weights, weights, weights, tokens),
        check_vma=False,
    )
```

```python
import functools

import jax
import jax.numpy as jnp
from jax import lax
from jax.experimental import pallas as pl
from jax.experimental.pallas import tpu as pltpu
from jax.sharding import PartitionSpec as P

QB = 128
VMEM_LIMIT = 48 * 1024 * 1024

beta_one = 0.9
beta_two = 0.95
learn_rate = 0.004
adam_epsilon = 1e-08
step_count = 10.0
quant_limit = 448.0
scale_epsilon = 1e-06
first_fix = 1.0 - beta_one**step_count
second_fix = 1.0 - beta_two**step_count


def adam_kernel(blocks, expert_of, master, gradient, first, second, *refs):
    new_master, new_first, new_second = refs[-3 - blocks : -blocks]
    sends = refs[-blocks:]
    rows, columns = sends[0].shape
    pieces = [
        (slice(i, i + QB), slice(j, j + QB)) for i in range(0, rows, QB) for j in range(0, columns, QB)
    ]
    scaled_out = []
    for piece in pieces:
        at = (0, *piece)
        grad = gradient[at].astype(jnp.float32)
        moment_one = beta_one * first[at].astype(jnp.float32) + (1.0 - beta_one) * grad
        moment_two = beta_two * second[at].astype(jnp.float32) + (1.0 - beta_two) * grad * grad
        new_first[at] = moment_one.astype(jnp.bfloat16)
        new_second[at] = moment_two.astype(jnp.bfloat16)
        scaled = moment_two * (1.0 / second_fix)
        root = scaled * lax.rsqrt(scaled)
        updated = master[at] - (learn_rate / first_fix) * moment_one / (root + adam_epsilon)
        new_master[at] = updated
        largest = jnp.max(jnp.abs(updated), axis=(0, 1), keepdims=True)
        scale = ((largest + scale_epsilon) * (1.0 / quant_limit)).astype(jnp.bfloat16)
        scale = jnp.broadcast_to(scale.astype(jnp.float32), (1, QB))
        quantized = (updated * (1.0 / scale)).astype(jnp.bfloat16)
        scaled_out.append((piece, (quantized.astype(jnp.float32) * scale).astype(jnp.bfloat16)))
    for number in range(blocks):

        @pl.when(pl.program_id(0) == number)
        def _():
            for piece, value in scaled_out:
                sends[number][piece] = value


def adam_blocks(expert_of, arrays, carried):
    _, rows, columns = arrays[0].shape
    blocks = expert_of.shape[0]
    here = pl.BlockSpec((1, rows, columns), lambda i, expert_of: (expert_of[i], 0, 0))
    sent = pl.BlockSpec((rows, columns), lambda i, expert_of: (0, 0))
    whole = pl.BlockSpec(memory_space=pl.ANY)
    shapes = [
        jax.ShapeDtypeStruct(arrays[0].shape, jnp.float32),
        jax.ShapeDtypeStruct(arrays[0].shape, jnp.bfloat16),
        jax.ShapeDtypeStruct(arrays[0].shape, jnp.bfloat16),
    ] + [jax.ShapeDtypeStruct((rows, columns), jnp.bfloat16)] * blocks
    count = blocks * rows * columns
    results = pl.pallas_call(
        functools.partial(adam_kernel, blocks),
        grid_spec=pltpu.PrefetchScalarGridSpec(
            num_scalar_prefetch=1,
            grid=(blocks,),
            in_specs=[here] * 4 + [whole] * len(carried),
            out_specs=[here] * 3 + [sent] * blocks,
        ),
        out_shape=shapes,
        input_output_aliases={5 + i: i for i in range(len(carried))},
        compiler_params=pltpu.CompilerParams(vmem_limit_bytes=VMEM_LIMIT),
        cost_estimate=pl.CostEstimate(
            flops=30 * count, bytes_accessed=20 * count, transcendentals=2 * count
        ),
        name="adam_quantize",
    )(expert_of, *arrays, *carried)
    return results[:3], results[3:]


def product_kernel(slabs, place, left, *refs):
    out = refs[-1]
    total = jnp.zeros(out.shape, jnp.float32)
    for slab in range(slabs):
        right = refs[slab]
        rows = right.shape[0]
        start = pl.multiple_of(place[1 + slab] * rows, QB)
        total += jnp.dot(
            left[:, pl.ds(start, rows)], right[...], preferred_element_type=jnp.float32
        )
    out[...] = total.astype(out.dtype)


def product(place, token_rows, weights, breadth, carried):
    slabs = len(weights)
    tokens, units = token_rows.shape
    rows, columns = weights[0].shape
    return pl.pallas_call(
        functools.partial(product_kernel, slabs),
        grid_spec=pltpu.PrefetchScalarGridSpec(
            num_scalar_prefetch=1,
            grid=(1,),
            in_specs=[pl.BlockSpec((tokens, units), lambda i, place: (0, 0))]
            + [pl.BlockSpec((rows, columns), lambda i, place: (0, 0))] * slabs
            + [pl.BlockSpec(memory_space=pl.ANY)] * len(carried),
            out_specs=pl.BlockSpec((tokens, columns), lambda i, place: (0, place[0])),
        ),
        out_shape=jax.ShapeDtypeStruct((tokens, breadth), jnp.bfloat16),
        input_output_aliases={2 + slabs: 0} if carried else {},
        compiler_params=pltpu.CompilerParams(vmem_limit_bytes=VMEM_LIMIT),
        cost_estimate=pl.CostEstimate(
            flops=2 * tokens * units * columns,
            bytes_accessed=2 * (units * columns + tokens * units + tokens * columns),
            transcendentals=0,
        ),
        name="expert_product",
    )(place, token_rows, *weights, *carried)


def swap(value, axis, size, mask):
    if not mask:
        return value
    return lax.ppermute(value, axis, [(i, i ^ mask) for i in range(size)])


def body(shards, replicas, *arguments):
    *arrays, hidden, owner_of_expert, slab_order = arguments
    shard, replica = lax.axis_index("shard"), lax.axis_index("replica")
    token_rows = hidden.reshape(hidden.shape[2:])
    columns = arrays[0].shape[2]
    bits = [1 << i for i in range((replicas - 1).bit_length())]
    experts = jnp.arange(shards, dtype=jnp.int32)
    sources = shard.astype(jnp.int32) ^ experts
    expert_of = jnp.sum(
        jnp.where(owner_of_expert[None, :] == sources[:, None], experts[None, :], 0), axis=1
    ).astype(jnp.int32)
    members = replica.astype(jnp.int32) ^ jnp.arange(replicas, dtype=jnp.int32)
    slabs = jnp.sum(
        jnp.where(members[:, None] == jnp.arange(replicas)[None, :], slab_order[None, :], 0), axis=1
    ).astype(jnp.int32)
    carried = ()
    weights = []
    for pair in range(0, shards, 2):
        carried, sends = adam_blocks(expert_of[pair : pair + 2], arrays, tuple(carried))
        weights += [swap(send, "shard", shards, pair + i) for i, send in enumerate(sends)]
    out = ()
    for number, weight in enumerate(weights):
        held = {0: weight}
        for step in range(len(bits)):
            bit = bits[(step + number) % len(bits)]
            held.update({m ^ bit: swap(w, "replica", replicas, bit) for m, w in list(held.items())})
        place = jnp.concatenate([sources[number : number + 1], slabs])
        ordered = [held[m] for m in range(replicas)]
        out = (product(place, token_rows, ordered, columns * shards, out),)
    return (*carried, out[0].reshape(hidden.shape[:2] + out[0].shape))


def solution(mesh):
    weights = P(None, "replica", "shard")
    tokens = P("replica", "shard", None, None)
    return jax.shard_map(
        functools.partial(body, mesh.shape["shard"], mesh.shape["replica"]),
        mesh=mesh,
        in_specs=(weights, weights, weights, weights, tokens, P(), P()),
        out_specs=(weights, weights, weights, tokens),
        check_vma=False,
    )
```

```python
import collections
import functools

import jax
import jax.numpy as jnp
from jax import lax
from jax.experimental import pallas as pl
from jax.experimental.pallas import tpu as pltpu
from jax.sharding import PartitionSpec as P

QB = 128
VMEM_LIMIT = 60 * 1024 * 1024
PRODUCT_LIMIT = 16 * 1024 * 1024

beta_one = 0.9
beta_two = 0.95
learn_rate = 0.004
adam_epsilon = 1e-08
step_count = 10.0
quant_limit = 448.0
scale_epsilon = 1e-06
first_fix = 1.0 - beta_one**step_count
second_fix = 1.0 - beta_two**step_count
second_root = second_fix**0.5
step_size = learn_rate / first_fix * second_root
root_epsilon = adam_epsilon * second_root

TOKEN = (132 * 1024, 128)
WHOLE = pl.BlockSpec(memory_space=pl.ANY)
SMALL_COST = pl.CostEstimate(flops=0, bytes_accessed=65536, transcendentals=0)


def like(array):
    return jax.ShapeDtypeStruct(array.shape, array.dtype)


def fence_kernel(*refs):
    pass


def fence(arrays):
    return pl.pallas_call(
        fence_kernel,
        in_specs=[WHOLE] * len(arrays),
        out_specs=[WHOLE] * len(arrays),
        out_shape=[like(array) for array in arrays],
        input_output_aliases={i: i for i in range(len(arrays))},
        compiler_params=pltpu.CompilerParams(vmem_limit_bytes=1024 * 1024),
        cost_estimate=SMALL_COST,
        name="arrival_order",
    )(*arrays)


def adam_kernel(blocks, passed, expert_of, master, gradient, first, second, *refs):
    new_master, new_first, new_second, *sends = refs[passed : passed + 3 + blocks]
    for number in range(blocks):

        @pl.when(pl.program_id(0) == number)
        def _():
            for start in range(0, master.shape[2], QB):
                at = (0, slice(None), slice(start, start + QB))
                grad = gradient[at].astype(jnp.float32)
                moment_one = beta_one * first[at].astype(jnp.float32) + (1.0 - beta_one) * grad
                moment_two = beta_two * second[at].astype(jnp.float32) + (
                    ((1.0 - beta_two) * grad) * grad
                )
                new_first[at] = moment_one.astype(jnp.bfloat16)
                new_second[at] = moment_two.astype(jnp.bfloat16)
                root = moment_two * lax.rsqrt(moment_two) + root_epsilon
                inverse = pl.reciprocal(root, approx=True)
                inverse = inverse * (2.0 - root * inverse)
                updated = master[at] - (step_size * moment_one) * inverse
                new_master[at] = updated
                largest = jnp.max(jnp.abs(updated), axis=0, keepdims=True)
                largest = jnp.max(largest, axis=1, keepdims=True)
                scale = ((largest + scale_epsilon) * (1.0 / quant_limit)).astype(jnp.bfloat16)
                scale = jnp.broadcast_to(scale.astype(jnp.float32), (1, QB))
                quantized = (updated * (1.0 / scale)).astype(jnp.bfloat16)
                value = quantized.astype(jnp.float32) * scale
                sends[number][:, start : start + QB] = value.astype(jnp.bfloat16)


def adam_blocks(expert_of, arrays, carried, token, fenced):
    _, rows, columns = arrays[0].shape
    blocks = expert_of.shape[0]
    passed = len(carried) + len(token)

    def sent(number):
        def place(e, i, expert_of):
            return jnp.where(e == number, i, jnp.where(e > number, rows // QB - 1, 0)), 0

        return pl.BlockSpec((QB, columns), place)

    here = pl.BlockSpec((1, QB, columns), lambda e, i, expert_of: (expert_of[e], i, 0))
    made = [like(arrays[0]), like(arrays[2]), like(arrays[3])]
    made += [jax.ShapeDtypeStruct((rows, columns), jnp.bfloat16)] * blocks
    aliases = {5 + i: i for i in range(len(carried))}
    if token:
        aliases[5 + len(carried)] = len(made)
    results = pl.pallas_call(
        functools.partial(adam_kernel, blocks, passed),
        grid_spec=pltpu.PrefetchScalarGridSpec(
            num_scalar_prefetch=1,
            grid=(blocks, rows // QB),
            in_specs=[here] * 4 + [WHOLE] * passed,
            out_specs=[here] * 3 + [sent(number) for number in range(blocks)] + [WHOLE] * fenced,
        ),
        out_shape=made + [jax.ShapeDtypeStruct(TOKEN, jnp.float32)] * fenced,
        input_output_aliases=aliases,
        compiler_params=pltpu.CompilerParams(vmem_limit_bytes=VMEM_LIMIT),
        cost_estimate=SMALL_COST,
        name="adam_quantize",
    )(expert_of, *arrays, *carried, *token)
    return results[:3], results[3 : 3 + blocks], tuple(results[3 + blocks :])


def product_kernel(number, slabs, sources, places, left, *refs):
    out = refs[-1]
    total = jnp.zeros(out.shape, jnp.float32)
    for slab in range(slabs):
        right = refs[slab]
        rows = right.shape[0]
        start = pl.multiple_of(places[slab] * rows, QB)
        total += jnp.dot(
            left[:, pl.ds(start, rows)], right[...], preferred_element_type=jnp.float32
        )
    out[...] = total.astype(out.dtype)


def product(number, sources, places, token_rows, weights, breadth, carried, token):
    slabs = len(weights)
    tokens, units = token_rows.shape
    rows, columns = weights[0].shape
    passed = len(token) + len(carried)
    *token, out = pl.pallas_call(
        functools.partial(product_kernel, number, slabs),
        grid_spec=pltpu.PrefetchScalarGridSpec(
            num_scalar_prefetch=2,
            grid=(1,),
            in_specs=[pl.BlockSpec((tokens, units), lambda i, sources, places: (0, 0))]
            + [pl.BlockSpec((rows, columns), lambda i, sources, places: (0, 0))] * slabs
            + [WHOLE] * passed,
            out_specs=[WHOLE] * len(token)
            + [pl.BlockSpec((tokens, columns), lambda i, sources, places: (0, sources[number]))],
        ),
        out_shape=[like(array) for array in token]
            + [jax.ShapeDtypeStruct((tokens, breadth), jnp.bfloat16)],
        input_output_aliases={3 + slabs + i: i for i in range(passed)},
        compiler_params=pltpu.CompilerParams(vmem_limit_bytes=PRODUCT_LIMIT),
        cost_estimate=SMALL_COST,
        name="expert_product",
    )(sources, places, token_rows, *weights, *token, *carried)
    return (out,), tuple(token)


def swap(value, axis, size, mask):
    return lax.ppermute(value, axis, [(i, i ^ mask) for i in range(size)])


def body(shards, replicas, *arguments):
    *arrays, hidden, owner_of_expert, slab_order = arguments
    shard = lax.axis_index("shard").astype(jnp.int32)
    replica = lax.axis_index("replica").astype(jnp.int32)
    token_rows = hidden.reshape(hidden.shape[2:])
    breadth = arrays[0].shape[2] * shards
    bits = [1 << i for i in range((replicas - 1).bit_length())]
    experts = jnp.arange(shards, dtype=jnp.int32)
    members = jnp.arange(replicas, dtype=jnp.int32)
    sources = shard ^ experts
    expert_of = jnp.sum(
        jnp.where(owner_of_expert[None, :] == sources[:, None], experts[None, :], 0), axis=1
    ).astype(jnp.int32)
    places = jnp.sum(
        jnp.where((replica ^ members)[:, None] == members[None, :], slab_order[None, :], 0), axis=1
    ).astype(jnp.int32)

    pairs = shards // 2
    fenced = len(bits) == 2 and pairs > 1
    held = [{} for _ in range(shards)]
    made, due, ready = {}, collections.defaultdict(list), set()
    state = {"adam": (), "token": (), "out": ()}

    def adam(pair):
        picked = expert_of[2 * pair : 2 * pair + 2]
        state["adam"], sends, state["token"] = adam_blocks(
            picked, arrays, tuple(state["adam"]), state["token"], fenced
        )
        made[2 * pair], made[2 * pair + 1] = sends

    def deliver(block):
        held[block][0] = swap(made[block], "shard", shards, block) if block else made[block]

    def send(block, member, bit):
        held[block][member ^ bit] = swap(held[block][member], "replica", replicas, bit)

    def arrived(keys):
        token, *passed = fence([*state["token"], *[held[b][m] for b, m in keys]])
        state["token"] = (token,)
        for (block, member), array in zip(keys, passed):
            held[block][member] = array
        ready.update(keys)

    def multiply(block):
        ordered = [held[block][member] for member in range(replicas)]
        state["out"], state["token"] = product(
            block, sources, places, token_rows, ordered, breadth, state["out"], state["token"]
        )

    waiting = list(range(shards))
    if fenced:
        steps, moves = collections.defaultdict(list), collections.defaultdict(list)
        steps[-1], steps[0], steps[1], steps[2] = (
            [(0, 0, 1), (0, 0, 2)],
            [(1, 0, 1), (1, 0, 2)],
            [(0, 1, 2)],
            [(1, 2, 1)],
        )
        for pair in range(1, pairs):
            even, odd = 2 * pair, 2 * pair + 1
            steps[3 * pair] = [(even, 0, 1), (odd, 0, 2)]
            steps[3 * pair + 1] = [(even, 0, 2), (odd, 0, 1)]
            steps[3 * pair + 2] = [(even, 1, 2), (odd, 2, 1)]
        for block in range(2, shards):
            moves[max(block - 2, min(2 * block - 7, 3 * (block // 2) - 2))].append(block)

        def start(step):
            for block in moves[step]:
                deliver(block)
                due[step + 2].append((block, 0))
            for block, member, bit in steps[step]:
                send(block, member, bit)
                due[step + 2].append((block, member ^ bit))

        adam(0)
        deliver(0)
        deliver(1)
        ready.add((0, 0))
        due[0].append((1, 0))
        start(-1)
        adam(1)
        for step in range(3 * pairs + 2):
            arrived(due[step])
            start(step)
            if step + 2 < pairs:
                adam(step + 2)
            for block in list(waiting):
                if all((block, member) in ready for member in range(replicas)):
                    multiply(block)
                    waiting.remove(block)
    else:
        for pair in range(pairs):
            adam(pair)
        for block in range(shards):
            deliver(block)
            for number in range(len(bits)):
                bit = bits[(number + block) % len(bits)]
                for member in list(held[block]):
                    send(block, member, bit)
            multiply(block)
    out = state["out"][0]
    return (*state["adam"], out.reshape(hidden.shape[:2] + out.shape))


def solution(mesh):
    weights = P(None, "replica", "shard")
    tokens = P("replica", "shard", None, None)
    return jax.shard_map(
        functools.partial(body, mesh.shape["shard"], mesh.shape["replica"]),
        mesh=mesh,
        in_specs=(weights, weights, weights, weights, tokens, P(), P()),
        out_specs=(weights, weights, weights, tokens),
        check_vma=False,
    )
```

```python
import collections
import functools

import jax
import jax.numpy as jnp
from jax import lax
from jax.experimental import pallas as pl
from jax.experimental.pallas import tpu as pltpu
from jax.sharding import PartitionSpec as P

QB = 128
VMEM_LIMIT = 60 * 1024 * 1024
PRODUCT_LIMIT = 16 * 1024 * 1024

beta_one = 0.9
beta_two = 0.95
learn_rate = 0.004
adam_epsilon = 1e-08
step_count = 10.0
quant_limit = 448.0
scale_epsilon = 1e-06
first_fix = 1.0 - beta_one**step_count
second_fix = 1.0 - beta_two**step_count
second_root = second_fix**0.5
step_size = learn_rate / first_fix * second_root
root_epsilon = adam_epsilon * second_root

TOKEN = (132 * 1024, 128)
WHOLE = pl.BlockSpec(memory_space=pl.ANY)
SMALL_COST = pl.CostEstimate(flops=0, bytes_accessed=65536, transcendentals=0)


def like(array):
    return jax.ShapeDtypeStruct(array.shape, array.dtype)


def fence_kernel(*refs):
    pass


def fence(arrays):
    return pl.pallas_call(
        fence_kernel,
        in_specs=[WHOLE] * len(arrays),
        out_specs=[WHOLE] * len(arrays),
        out_shape=[like(array) for array in arrays],
        input_output_aliases={i: i for i in range(len(arrays))},
        compiler_params=pltpu.CompilerParams(vmem_limit_bytes=1024 * 1024),
        cost_estimate=SMALL_COST,
        name="arrival_order",
    )(*arrays)


def adam_kernel(blocks, passed, expert_of, master, gradient, first, second, *refs):
    new_master, new_first, new_second, *sends = refs[passed : passed + 3 + blocks]
    _, rows, columns = master.shape
    places = [
        (slice(i, i + QB), slice(j, j + QB)) for i in range(0, rows, QB) for j in range(0, columns, QB)
    ]
    peaks = []
    for place in places:
        at = (0, *place)
        grad = gradient[at].astype(jnp.float32)
        moment_one = beta_one * first[at].astype(jnp.float32) + (1.0 - beta_one) * grad
        moment_two = beta_two * second[at].astype(jnp.float32) + ((1.0 - beta_two) * grad) * grad
        new_first[at] = moment_one.astype(jnp.bfloat16)
        new_second[at] = moment_two.astype(jnp.bfloat16)
        root = moment_two * lax.rsqrt(moment_two) + root_epsilon
        inverse = pl.reciprocal(root, approx=True)
        inverse = inverse * (2.0 - root * inverse)
        updated = master[at] - (step_size * moment_one) * inverse
        new_master[at] = updated
        peaks.append(jnp.max(jnp.abs(updated), axis=0, keepdims=True))
    largest = jnp.max(jnp.concatenate(peaks, axis=0), axis=1, keepdims=True)
    scale = ((largest + scale_epsilon) * (1.0 / quant_limit)).astype(jnp.bfloat16)
    scale = jnp.broadcast_to(scale.astype(jnp.float32), (len(places), QB))
    inverse_scale = 1.0 / scale
    for number in range(blocks):

        @pl.when(pl.program_id(0) == number)
        def _():
            for row, place in enumerate(places):
                one = slice(row, row + 1)
                quantized = (new_master[(0, *place)] * inverse_scale[one]).astype(jnp.bfloat16)
                value = quantized.astype(jnp.float32) * scale[one]
                sends[number][place] = value.astype(jnp.bfloat16)


def adam_blocks(base, blocks, expert_of, arrays, carried, token, fenced):
    _, rows, columns = arrays[0].shape
    passed = len(carried) + len(token)
    here = pl.BlockSpec((1, rows, columns), lambda i, expert_of: (expert_of[base + i], 0, 0))
    sent = pl.BlockSpec((rows, columns), lambda i, expert_of: (0, 0))
    made = [like(arrays[0]), like(arrays[2]), like(arrays[3])]
    made += [jax.ShapeDtypeStruct((rows, columns), jnp.bfloat16)] * blocks
    aliases = {5 + i: i for i in range(len(carried))}
    if token:
        aliases[5 + len(carried)] = len(made)
    results = pl.pallas_call(
        functools.partial(adam_kernel, blocks, passed),
        grid_spec=pltpu.PrefetchScalarGridSpec(
            num_scalar_prefetch=1,
            grid=(blocks,),
            in_specs=[here] * 4 + [WHOLE] * passed,
            out_specs=[here] * 3 + [sent] * blocks + [WHOLE] * fenced,
        ),
        out_shape=made + [jax.ShapeDtypeStruct(TOKEN, jnp.float32)] * fenced,
        input_output_aliases=aliases,
        compiler_params=pltpu.CompilerParams(vmem_limit_bytes=VMEM_LIMIT),
        cost_estimate=SMALL_COST,
        name="adam_quantize",
    )(expert_of, *arrays, *carried, *token)
    return results[:3], results[3 : 3 + blocks], tuple(results[3 + blocks :])


def product_kernel(number, slabs, sources, places, left, *refs):
    out = refs[-1]
    total = jnp.zeros(out.shape, jnp.float32)
    for slab in range(slabs):
        right = refs[slab]
        rows = right.shape[0]
        start = pl.multiple_of(places[slab] * rows, QB)
        total += jnp.dot(
            left[:, pl.ds(start, rows)], right[...], preferred_element_type=jnp.float32
        )
    out[...] = total.astype(out.dtype)


def product(number, sources, places, token_rows, weights, breadth, carried, token):
    slabs = len(weights)
    tokens, units = token_rows.shape
    rows, columns = weights[0].shape
    passed = len(token) + len(carried)
    *token, out = pl.pallas_call(
        functools.partial(product_kernel, number, slabs),
        grid_spec=pltpu.PrefetchScalarGridSpec(
            num_scalar_prefetch=2,
            grid=(1,),
            in_specs=[pl.BlockSpec((tokens, units), lambda i, sources, places: (0, 0))]
            + [pl.BlockSpec((rows, columns), lambda i, sources, places: (0, 0))] * slabs
            + [WHOLE] * passed,
            out_specs=[WHOLE] * len(token)
            + [pl.BlockSpec((tokens, columns), lambda i, sources, places: (0, sources[number]))],
        ),
        out_shape=[like(array) for array in token]
            + [jax.ShapeDtypeStruct((tokens, breadth), jnp.bfloat16)],
        input_output_aliases={3 + slabs + i: i for i in range(passed)},
        compiler_params=pltpu.CompilerParams(vmem_limit_bytes=PRODUCT_LIMIT),
        cost_estimate=SMALL_COST,
        name="expert_product",
    )(sources, places, token_rows, *weights, *token, *carried)
    return (out,), tuple(token)


def swap(value, axis, size, mask):
    return lax.ppermute(value, axis, [(i, i ^ mask) for i in range(size)])


def body(shards, replicas, *arguments):
    *arrays, hidden, owner_of_expert, slab_order = arguments
    shard = lax.axis_index("shard").astype(jnp.int32)
    replica = lax.axis_index("replica").astype(jnp.int32)
    token_rows = hidden.reshape(hidden.shape[2:])
    breadth = arrays[0].shape[2] * shards
    bits = [1 << i for i in range((replicas - 1).bit_length())]
    experts = jnp.arange(shards, dtype=jnp.int32)
    members = jnp.arange(replicas, dtype=jnp.int32)
    sources = shard ^ experts
    expert_of = jnp.sum(
        jnp.where(owner_of_expert[None, :] == sources[:, None], experts[None, :], 0), axis=1
    ).astype(jnp.int32)
    places = jnp.sum(
        jnp.where((replica ^ members)[:, None] == members[None, :], slab_order[None, :], 0), axis=1
    ).astype(jnp.int32)

    pairs = shards // 2
    fenced = len(bits) == 2 and pairs > 1
    held = [{} for _ in range(shards)]
    made, due, ready = {}, collections.defaultdict(list), set()
    state = {"adam": (), "token": (), "out": ()}

    def adam(first, blocks):
        state["adam"], sends, state["token"] = adam_blocks(
            first, blocks, expert_of, arrays, tuple(state["adam"]), state["token"], fenced
        )
        made.update(zip(range(first, first + blocks), sends))

    def deliver(block):
        held[block][0] = swap(made[block], "shard", shards, block) if block else made[block]

    def send(block, member, bit):
        held[block][member ^ bit] = swap(held[block][member], "replica", replicas, bit)

    def arrived(keys):
        token, *passed = fence([*state["token"], *[held[b][m] for b, m in keys]])
        state["token"] = (token,)
        for (block, member), array in zip(keys, passed):
            held[block][member] = array
        ready.update(keys)

    def multiply(block):
        ordered = [held[block][member] for member in range(replicas)]
        state["out"], state["token"] = product(
            block, sources, places, token_rows, ordered, breadth, state["out"], state["token"]
        )

    waiting = list(range(shards))
    if fenced:
        steps, moves = collections.defaultdict(list), collections.defaultdict(list)
        steps[-1], steps[0], steps[1], steps[2] = (
            [(0, 0, 1), (0, 0, 2)],
            [(1, 0, 1), (1, 0, 2)],
            [(0, 1, 2)],
            [(1, 2, 1)],
        )
        for pair in range(1, pairs):
            even, odd = 2 * pair, 2 * pair + 1
            steps[3 * pair] = [(even, 0, 1), (odd, 0, 2)]
            steps[3 * pair + 1] = [(even, 0, 2), (odd, 0, 1)]
            steps[3 * pair + 2] = [(even, 1, 2), (odd, 2, 1)]
        for block in range(2, shards):
            moves[max((block - 1) // 2, min(2 * block - 7, 3 * (block // 2) - 2))].append(block)

        def start(step):
            for block in moves[step]:
                deliver(block)
                due[step + 2].append((block, 0))
            for block, member, bit in steps[step]:
                send(block, member, bit)
                due[step + 2].append((block, member ^ bit))

        adam(0, 2)
        deliver(0)
        deliver(1)
        ready.add((0, 0))
        due[0].append((1, 0))
        start(-1)
        adam(2, 2)
        for step in range(3 * pairs + 2):
            arrived(due[step])
            start(step)
            if step + 2 < pairs:
                adam(2 * step + 4, 2)
            for block in list(waiting):
                if all((block, member) in ready for member in range(replicas)):
                    multiply(block)
                    waiting.remove(block)
    else:
        for pair in range(pairs):
            adam(2 * pair, 2)
        for block in range(shards):
            deliver(block)
            for number in range(len(bits)):
                bit = bits[(number + block) % len(bits)]
                for member in list(held[block]):
                    send(block, member, bit)
            multiply(block)
    out = state["out"][0]
    return (*state["adam"], out.reshape(hidden.shape[:2] + out.shape))


def solution(mesh):
    weights = P(None, "replica", "shard")
    tokens = P("replica", "shard", None, None)
    return jax.shard_map(
        functools.partial(body, mesh.shape["shard"], mesh.shape["replica"]),
        mesh=mesh,
        in_specs=(weights, weights, weights, weights, tokens, P(), P()),
        out_specs=(weights, weights, weights, tokens),
        check_vma=False,
    )
```

```python
import collections
import functools

import jax
import jax.numpy as jnp
from jax import lax
from jax.experimental import pallas as pl
from jax.experimental.pallas import tpu as pltpu
from jax.sharding import PartitionSpec as P

QB = 128
VMEM_LIMIT = 60 * 1024 * 1024
PRODUCT_LIMIT = 16 * 1024 * 1024

beta_one = 0.9
beta_two = 0.95
learn_rate = 0.004
adam_epsilon = 1e-08
step_count = 10.0
quant_limit = 448.0
scale_epsilon = 1e-06
first_fix = 1.0 - beta_one**step_count
second_fix = 1.0 - beta_two**step_count
second_root = second_fix**0.5
step_size = learn_rate / first_fix * second_root
root_epsilon = adam_epsilon * second_root

TOKEN = (132 * 1024, 128)
WHOLE = pl.BlockSpec(memory_space=pl.ANY)
SMALL_COST = pl.CostEstimate(flops=0, bytes_accessed=65536, transcendentals=0)


def like(array):
    return jax.ShapeDtypeStruct(array.shape, array.dtype)


def fence_kernel(*refs):
    pass


def fence(arrays):
    return pl.pallas_call(
        fence_kernel,
        in_specs=[WHOLE] * len(arrays),
        out_specs=[WHOLE] * len(arrays),
        out_shape=[like(array) for array in arrays],
        input_output_aliases={i: i for i in range(len(arrays))},
        compiler_params=pltpu.CompilerParams(vmem_limit_bytes=1024 * 1024),
        cost_estimate=SMALL_COST,
        name="arrival_order",
    )(*arrays)


def adam_kernel(numbers, passed, owner, *refs):
    arrays, outs = refs[:4], refs[4 + passed : 7 + passed]
    sends = refs[7 + passed : 7 + passed + len(numbers)]
    *buffers, semaphores = refs[-9:]
    experts, rows, columns = arrays[0].shape
    shard = lax.axis_index("shard")
    chunks = [(n, i) for n in range(len(numbers)) for i in range(rows // QB)]
    held = []
    for number in numbers:
        expert = jnp.int32(0)
        for candidate in range(experts):
            expert = jnp.where(owner[candidate] == shard ^ number, candidate, expert)
        held.append(expert)

    def copies(chunk, inward):
        n, i = chunk
        span = pl.ds(i * QB, QB)
        outer = arrays if inward else (*outs, sends[n])
        for k, ref in enumerate(outer):
            far = ref.at[span] if ref is sends[n] else ref.at[held[n], span]
            near = buffers[k if inward else 4 + k].at[n, span]
            pair = (far, near) if inward else (near, far)
            yield pltpu.make_async_copy(*pair, semaphores.at[n, i, k if inward else 4 + k])

    def update(chunk):
        n, i = chunk
        master, gradient, first, second, new_master, new_first, new_second, _ = buffers
        peaks = []
        for start in range(0, columns, QB):
            at = (n, slice(i * QB, (i + 1) * QB), slice(start, start + QB))
            grad = gradient[at].astype(jnp.float32)
            moment_one = beta_one * first[at].astype(jnp.float32) + (1.0 - beta_one) * grad
            moment_two = beta_two * second[at].astype(jnp.float32) + (
                ((1.0 - beta_two) * grad) * grad
            )
            new_first[at] = moment_one.astype(jnp.bfloat16)
            new_second[at] = moment_two.astype(jnp.bfloat16)
            guess = lax.rsqrt(moment_two)
            root = moment_two * guess + root_epsilon
            inverse = guess * (2.0 - root * guess)
            updated = master[at] - (step_size * moment_one) * inverse
            new_master[at] = updated
            peaks.append(jnp.max(jnp.abs(updated), axis=0, keepdims=True))
        largest = jnp.max(jnp.concatenate(peaks, axis=0), axis=1, keepdims=True)
        scale = ((largest + scale_epsilon) * (1.0 / quant_limit)).astype(jnp.bfloat16)
        scale = jnp.broadcast_to(scale.astype(jnp.float32), (len(peaks), QB))
        return scale, 1.0 / scale

    def quantize(chunk, scale, inverse_scale):
        n, i = chunk
        for block, start in enumerate(range(0, columns, QB)):
            at = (n, slice(i * QB, (i + 1) * QB), slice(start, start + QB))
            one = slice(block, block + 1)
            quantized = (buffers[4][at] * inverse_scale[one]).astype(jnp.bfloat16)
            buffers[7][at] = (quantized.astype(jnp.float32) * scale[one]).astype(jnp.bfloat16)
        for copy in copies(chunk, False):
            copy.start()

    for chunk in chunks:
        for copy in copies(chunk, True):
            copy.start()
    pending = None
    for chunk in chunks:
        for copy in copies(chunk, True):
            copy.wait()
        scales = update(chunk)
        if pending:
            quantize(*pending)
        pending = (chunk, *scales)
    quantize(*pending)
    for chunk in chunks:
        for copy in copies(chunk, False):
            copy.wait()


def adam_blocks(numbers, owner, arrays, carried, token, fenced):
    _, rows, columns = arrays[0].shape
    blocks = len(numbers)
    passed = len(carried) + len(token)
    made = [like(arrays[0]), like(arrays[2]), like(arrays[3])]
    made += [jax.ShapeDtypeStruct((rows, columns), jnp.bfloat16)] * blocks
    aliases = {5 + i: i for i in range(len(carried))}
    if token:
        aliases[5 + len(carried)] = len(made)
    made += [jax.ShapeDtypeStruct(TOKEN, jnp.float32)] * fenced
    kinds = [jnp.float32, jnp.bfloat16, jnp.bfloat16, jnp.bfloat16] * 2
    results = pl.pallas_call(
        functools.partial(adam_kernel, numbers, passed),
        in_specs=[pl.BlockSpec(memory_space=pltpu.SMEM)] + [WHOLE] * (4 + passed),
        out_specs=[WHOLE] * len(made),
        out_shape=made,
        scratch_shapes=[pltpu.VMEM((blocks, rows, columns), kind) for kind in kinds]
        + [pltpu.SemaphoreType.DMA((blocks, rows // QB, 8))],
        input_output_aliases=aliases,
        compiler_params=pltpu.CompilerParams(vmem_limit_bytes=VMEM_LIMIT),
        cost_estimate=SMALL_COST,
        name="adam_quantize",
    )(owner, *arrays, *carried, *token)
    return results[:3], results[3 : 3 + blocks], tuple(results[3 + blocks :])


def product_kernel(number, slabs, sources, places, left, *refs):
    out = refs[-1]
    total = jnp.zeros(out.shape, jnp.float32)
    for slab in range(slabs):
        right = refs[slab]
        rows = right.shape[0]
        start = pl.multiple_of(places[slab] * rows, QB)
        total += jnp.dot(
            left[:, pl.ds(start, rows)], right[...], preferred_element_type=jnp.float32
        )
    out[...] = total.astype(out.dtype)


def product(number, sources, places, token_rows, weights, breadth, carried, token):
    slabs = len(weights)
    tokens, units = token_rows.shape
    rows, columns = weights[0].shape
    passed = len(token) + len(carried)
    *token, out = pl.pallas_call(
        functools.partial(product_kernel, number, slabs),
        grid_spec=pltpu.PrefetchScalarGridSpec(
            num_scalar_prefetch=2,
            grid=(1,),
            in_specs=[pl.BlockSpec(memory_space=pltpu.VMEM)] * (1 + slabs) + [WHOLE] * passed,
            out_specs=[WHOLE] * len(token)
            + [pl.BlockSpec((tokens, columns), lambda i, sources, places: (0, sources[number]))],
        ),
        out_shape=[like(array) for array in token]
            + [jax.ShapeDtypeStruct((tokens, breadth), jnp.bfloat16)],
        input_output_aliases={3 + slabs + i: i for i in range(passed)},
        compiler_params=pltpu.CompilerParams(vmem_limit_bytes=PRODUCT_LIMIT),
        cost_estimate=SMALL_COST,
        name="expert_product",
    )(sources, places, token_rows, *weights, *token, *carried)
    return (out,), tuple(token)


def swap(value, axis, size, mask):
    return lax.ppermute(value, axis, [(i, i ^ mask) for i in range(size)])


def body(shards, replicas, *arguments):
    *arrays, hidden, owner_of_expert, slab_order = arguments
    shard = lax.axis_index("shard").astype(jnp.int32)
    replica = lax.axis_index("replica").astype(jnp.int32)
    token_rows = hidden.reshape(hidden.shape[2:])
    breadth = arrays[0].shape[2] * shards
    bits = [1 << i for i in range((replicas - 1).bit_length())]
    members = jnp.arange(replicas, dtype=jnp.int32)
    sources = shard ^ jnp.arange(shards, dtype=jnp.int32)
    places = jnp.sum(
        jnp.where((replica ^ members)[:, None] == members[None, :], slab_order[None, :], 0), axis=1
    ).astype(jnp.int32)

    pairs = shards // 2
    fenced = len(bits) == 2 and pairs > 1
    held = [{} for _ in range(shards)]
    made, due, ready = {}, collections.defaultdict(list), set()
    state = {"adam": (), "token": (), "out": ()}

    def adam(*numbers):
        state["adam"], sends, state["token"] = adam_blocks(
            numbers, owner_of_expert, arrays, tuple(state["adam"]), state["token"], fenced
        )
        made.update(zip(numbers, sends))

    def deliver(block):
        held[block][0] = swap(made[block], "shard", shards, block) if block else made[block]

    def send(block, member, bit):
        held[block][member ^ bit] = swap(held[block][member], "replica", replicas, bit)

    def arrived(keys, leaving):
        waiting = [held[b][m] for b, m in keys] + [made[b] for b in leaving]
        token, *passed = fence([*state["token"], *waiting])
        state["token"] = (token,)
        made.update(zip(leaving, passed[len(keys) :]))
        for (block, member), array in zip(keys, passed):
            held[block][member] = array
        ready.update(keys)

    def multiply(block):
        ordered = [held[block][member] for member in range(replicas)]
        state["out"], state["token"] = product(
            block, sources, places, token_rows, ordered, breadth, state["out"], state["token"]
        )

    waiting = list(range(shards))
    if fenced:
        steps, moves = collections.defaultdict(list), collections.defaultdict(list)
        steps[-1], steps[0], steps[1], steps[2] = (
            [(0, 0, 1), (0, 0, 2)],
            [(1, 0, 1), (1, 0, 2)],
            [(0, 1, 2)],
            [(1, 2, 1)],
        )
        for pair in range(1, pairs):
            even, odd = 2 * pair, 2 * pair + 1
            steps[3 * pair] = [(even, 0, 1), (odd, 0, 2)]
            steps[3 * pair + 1] = [(even, 0, 2), (odd, 0, 1)]
            steps[3 * pair + 2] = [(even, 1, 2), (odd, 2, 1)]
        for block in range(2, shards):
            moves[max((block - 1) // 2, min(2 * block - 7, 3 * (block // 2) - 2))].append(block)

        def start(step):
            for block in moves[step]:
                deliver(block)
                due[step + 2].append((block, 0))
            for block, member, bit in steps[step]:
                send(block, member, bit)
                due[step + 2].append((block, member ^ bit))

        half = shards // 2
        rest = [half, 2, 3, *range(half + 1, shards), *range(4, half)]
        adam(0, 1)
        deliver(0)
        deliver(1)
        ready.add((0, 0))
        due[0].append((1, 0))
        start(-1)
        adam(*rest[:2])
        for step in range(3 * pairs + 2):
            arrived(due[step], moves[step])
            start(step)
            if 2 * step + 2 < len(rest):
                adam(*rest[2 * step + 2 : 2 * step + 4])
            for block in list(waiting):
                if all((block, member) in ready for member in range(replicas)):
                    multiply(block)
                    waiting.remove(block)
    else:
        for pair in range(pairs):
            adam(2 * pair, 2 * pair + 1)
        for block in range(shards):
            deliver(block)
            for number in range(len(bits)):
                bit = bits[(number + block) % len(bits)]
                for member in list(held[block]):
                    send(block, member, bit)
            multiply(block)
    out = state["out"][0]
    return (*state["adam"], out.reshape(hidden.shape[:2] + out.shape))


def solution(mesh):
    weights = P(None, "replica", "shard")
    tokens = P("replica", "shard", None, None)
    return jax.shard_map(
        functools.partial(body, mesh.shape["shard"], mesh.shape["replica"]),
        mesh=mesh,
        in_specs=(weights, weights, weights, weights, tokens, P(), P()),
        out_specs=(weights, weights, weights, tokens),
        check_vma=False,
    )
```

```python
import collections
import functools

import jax
import jax.numpy as jnp
from jax import lax
from jax.experimental import pallas as pl
from jax.experimental.pallas import tpu as pltpu
from jax.sharding import PartitionSpec as P

QB = 128
VMEM_LIMIT = 60 * 1024 * 1024
PRODUCT_LIMIT = 16 * 1024 * 1024

beta_one = 0.9
beta_two = 0.95
learn_rate = 0.004
adam_epsilon = 1e-08
step_count = 10.0
quant_limit = 448.0
scale_epsilon = 1e-06
first_fix = 1.0 - beta_one**step_count
second_fix = 1.0 - beta_two**step_count
second_root = second_fix**0.5
step_size = learn_rate / first_fix * second_root
root_epsilon = adam_epsilon * second_root

TOKEN = (132 * 1024, 128)
WHOLE = pl.BlockSpec(memory_space=pl.ANY)
SMALL_COST = pl.CostEstimate(flops=0, bytes_accessed=65536, transcendentals=0)


def like(array):
    return jax.ShapeDtypeStruct(array.shape, array.dtype)


def fence_kernel(*refs):
    pass


def fence(arrays):
    return pl.pallas_call(
        fence_kernel,
        in_specs=[WHOLE] * len(arrays),
        out_specs=[WHOLE] * len(arrays),
        out_shape=[like(array) for array in arrays],
        input_output_aliases={i: i for i in range(len(arrays))},
        compiler_params=pltpu.CompilerParams(vmem_limit_bytes=1024 * 1024),
        cost_estimate=SMALL_COST,
        name="arrival_order",
    )(*arrays)


def adam_kernel(numbers, passed, owner, *refs):
    arrays, outs = refs[:4], refs[4 + passed : 7 + passed]
    sends = refs[7 + passed : 7 + passed + len(numbers)]
    *buffers, semaphores = refs[-9:]
    experts, rows, columns = arrays[0].shape
    shard = lax.axis_index("shard")
    chunks = [(n, i) for n in range(len(numbers)) for i in range(rows // QB)]
    held = []
    for number in numbers:
        expert = jnp.int32(0)
        for candidate in range(experts):
            expert = jnp.where(owner[candidate] == shard ^ number, candidate, expert)
        held.append(expert)

    def copies(chunk, inward):
        n, i = chunk
        span = pl.ds(i * QB, QB)
        outer = arrays if inward else (*outs, sends[n])
        for k, ref in enumerate(outer):
            far = ref.at[span] if ref is sends[n] else ref.at[held[n], span]
            near = buffers[k if inward else 4 + k].at[n, span]
            pair = (far, near) if inward else (near, far)
            yield pltpu.make_async_copy(*pair, semaphores.at[n, i, k if inward else 4 + k])

    def update(chunk):
        n, i = chunk
        master, gradient, first, second, new_master, new_first, new_second, _ = buffers
        peaks = []
        for start in range(0, columns, QB):
            at = (n, slice(i * QB, (i + 1) * QB), slice(start, start + QB))
            grad = gradient[at].astype(jnp.float32)
            moment_one = beta_one * first[at].astype(jnp.float32) + (1.0 - beta_one) * grad
            moment_two = beta_two * second[at].astype(jnp.float32) + (
                ((1.0 - beta_two) * grad) * grad
            )
            new_first[at] = moment_one.astype(jnp.bfloat16)
            new_second[at] = moment_two.astype(jnp.bfloat16)
            guess = lax.rsqrt(moment_two)
            root = moment_two * guess + root_epsilon
            inverse = guess * (2.0 - root * guess)
            updated = master[at] - (step_size * moment_one) * inverse
            new_master[at] = updated
            peaks.append(jnp.max(jnp.abs(updated), axis=0, keepdims=True))
        largest = jnp.max(jnp.concatenate(peaks, axis=0), axis=1, keepdims=True)
        scale = ((largest + scale_epsilon) * (1.0 / quant_limit)).astype(jnp.bfloat16)
        scale = jnp.broadcast_to(scale, (len(peaks), QB))
        return scale, 1.0 / scale.astype(jnp.float32)

    def quantize(chunk, scale, inverse_scale):
        n, i = chunk
        for block, start in enumerate(range(0, columns, QB)):
            at = (n, slice(i * QB, (i + 1) * QB), slice(start, start + QB))
            one = slice(block, block + 1)
            quantized = (buffers[4][at] * inverse_scale[one]).astype(jnp.bfloat16)
            buffers[7][at] = quantized * scale[one]
        for copy in copies(chunk, False):
            copy.start()

    for chunk in chunks:
        for copy in copies(chunk, True):
            copy.start()
    pending = None
    for chunk in chunks:
        for copy in copies(chunk, True):
            copy.wait()
        scales = update(chunk)
        if pending:
            quantize(*pending)
        pending = (chunk, *scales)
    quantize(*pending)
    for chunk in chunks:
        for copy in copies(chunk, False):
            copy.wait()


def adam_blocks(numbers, owner, arrays, carried, token, fenced):
    _, rows, columns = arrays[0].shape
    blocks = len(numbers)
    passed = len(carried) + len(token)
    made = [like(arrays[0]), like(arrays[2]), like(arrays[3])]
    made += [jax.ShapeDtypeStruct((rows, columns), jnp.bfloat16)] * blocks
    aliases = {5 + i: i for i in range(len(carried))}
    if token:
        aliases[5 + len(carried)] = len(made)
    made += [jax.ShapeDtypeStruct(TOKEN, jnp.float32)] * fenced
    kinds = [jnp.float32, jnp.bfloat16, jnp.bfloat16, jnp.bfloat16] * 2
    results = pl.pallas_call(
        functools.partial(adam_kernel, numbers, passed),
        in_specs=[pl.BlockSpec(memory_space=pltpu.SMEM)] + [WHOLE] * (4 + passed),
        out_specs=[WHOLE] * len(made),
        out_shape=made,
        scratch_shapes=[pltpu.VMEM((blocks, rows, columns), kind) for kind in kinds]
        + [pltpu.SemaphoreType.DMA((blocks, rows // QB, 8))],
        input_output_aliases=aliases,
        compiler_params=pltpu.CompilerParams(vmem_limit_bytes=VMEM_LIMIT),
        cost_estimate=SMALL_COST,
        name="adam_quantize",
    )(owner, *arrays, *carried, *token)
    return results[:3], results[3 : 3 + blocks], tuple(results[3 + blocks :])


def product_kernel(number, slabs, sources, places, left, *refs):
    out = refs[-1]
    rows = refs[0].shape[0]
    parts = [left[:, pl.ds(pl.multiple_of(places[i] * rows, QB), rows)] for i in range(slabs)]
    total = jnp.dot(
        jnp.concatenate(parts, axis=1),
        jnp.concatenate([right[...] for right in refs[:slabs]], axis=0),
        preferred_element_type=jnp.float32,
    )
    out[...] = total.astype(out.dtype)


def product(number, sources, places, token_rows, weights, breadth, carried, token):
    slabs = len(weights)
    tokens, units = token_rows.shape
    rows, columns = weights[0].shape
    passed = len(token) + len(carried)
    *token, out = pl.pallas_call(
        functools.partial(product_kernel, number, slabs),
        grid_spec=pltpu.PrefetchScalarGridSpec(
            num_scalar_prefetch=2,
            grid=(1,),
            in_specs=[pl.BlockSpec(memory_space=pltpu.VMEM)] * (1 + slabs) + [WHOLE] * passed,
            out_specs=[WHOLE] * len(token)
            + [pl.BlockSpec((tokens, columns), lambda i, sources, places: (0, sources[number]))],
        ),
        out_shape=[like(array) for array in token]
            + [jax.ShapeDtypeStruct((tokens, breadth), jnp.bfloat16)],
        input_output_aliases={3 + slabs + i: i for i in range(passed)},
        compiler_params=pltpu.CompilerParams(vmem_limit_bytes=PRODUCT_LIMIT),
        cost_estimate=SMALL_COST,
        name="expert_product",
    )(sources, places, token_rows, *weights, *token, *carried)
    return (out,), tuple(token)


def swap(value, axis, size, mask):
    return lax.ppermute(value, axis, [(i, i ^ mask) for i in range(size)])


def body(shards, replicas, *arguments):
    *arrays, hidden, owner_of_expert, slab_order = arguments
    shard = lax.axis_index("shard").astype(jnp.int32)
    replica = lax.axis_index("replica").astype(jnp.int32)
    token_rows = hidden.reshape(hidden.shape[2:])
    breadth = arrays[0].shape[2] * shards
    bits = [1 << i for i in range((replicas - 1).bit_length())]
    members = jnp.arange(replicas, dtype=jnp.int32)
    sources = shard ^ jnp.arange(shards, dtype=jnp.int32)
    places = jnp.sum(
        jnp.where((replica ^ members)[:, None] == members[None, :], slab_order[None, :], 0), axis=1
    ).astype(jnp.int32)

    pairs = shards // 2
    fenced = len(bits) == 2 and pairs > 1
    held = [{} for _ in range(shards)]
    made, due, ready = {}, collections.defaultdict(list), set()
    state = {"adam": (), "token": (), "out": ()}

    def adam(*numbers):
        state["adam"], sends, state["token"] = adam_blocks(
            numbers, owner_of_expert, arrays, tuple(state["adam"]), state["token"], fenced
        )
        made.update(zip(numbers, sends))

    def deliver(block):
        held[block][0] = swap(made[block], "shard", shards, block) if block else made[block]

    def send(block, member, bit):
        held[block][member ^ bit] = swap(held[block][member], "replica", replicas, bit)

    def arrived(keys, leaving):
        waiting = [held[b][m] for b, m in keys] + [made[b] for b in leaving]
        token, *passed = fence([*state["token"], *waiting])
        state["token"] = (token,)
        made.update(zip(leaving, passed[len(keys) :]))
        for (block, member), array in zip(keys, passed):
            held[block][member] = array
        ready.update(keys)

    def multiply(block):
        ordered = [held[block][member] for member in range(replicas)]
        state["out"], state["token"] = product(
            block, sources, places, token_rows, ordered, breadth, state["out"], state["token"]
        )

    waiting = list(range(shards))
    if fenced:
        fences = collections.defaultdict(lambda: ([], [], []))

        def plan(step, until, *keys):
            fences[step][1].extend(keys)
            fences[until][0].extend((block, member ^ bit) for block, member, bit in keys)

        plan(0, 2, (1, 0, 1), (1, 0, 2))
        plan(1, 3, (0, 1, 2))
        plan(2, 3, (1, 2, 1))
        plan(2.5, 4, (2, 0, 1), (3, 0, 2))
        plan(3, 5, (2, 0, 2), (3, 0, 1))
        plan(4, 6, (2, 1, 2), (3, 2, 1))
        for pair in range(2, pairs):
            even, odd, step = 2 * pair, 2 * pair + 1, 3 * pair
            if pair + 1 < pairs:
                plan(step - 1, step + 1, (even, 0, 1), (odd, 0, 2))
                plan(step, step + 2, (even, 0, 2), (odd, 0, 1))
                plan(step + 1, step + 3, (even, 1, 2), (odd, 2, 1))
            else:
                plan(step - 1, step + 1, (even, 0, 1), (even, 0, 2))
                plan(step, step + 2, (odd, 0, 1), (odd, 0, 2))
                plan(step + 1, step + 3, (even, 1, 2))
                plan(step + 2, step + 4, (odd, 2, 1))
        for block in range(4, shards):
            first = min(2 * block - 7, 3 * (block // 2) - 3)
            fences[first][2].append(block)
            fences[first + 2][0].append((block, 0))
        fences[0][0].append((1, 0))
        fences[1][0].extend([(0, 1), (0, 2)])
        fences[2.5][0].extend([(2, 0), (3, 0)])

        adam(0, 1)
        deliver(0)
        deliver(1)
        ready.add((0, 0))
        send(0, 0, 1)
        send(0, 0, 2)
        adam(2, 3)
        deliver(2)
        deliver(3)
        computed = 4
        for step in sorted(fences):
            keys, sending, leaving = fences[step]
            arrived(keys, leaving)
            for block in leaving:
                deliver(block)
            for key in sending:
                send(*key)
            if step not in (1, 2) and computed < shards:
                adam(computed, computed + 1)
                computed += 2
            for block in list(waiting):
                if all((block, member) in ready for member in range(replicas)):
                    multiply(block)
                    waiting.remove(block)
    else:
        for pair in range(pairs):
            adam(2 * pair, 2 * pair + 1)
        for block in range(shards):
            deliver(block)
            for number in range(len(bits)):
                bit = bits[(number + block) % len(bits)]
                for member in list(held[block]):
                    send(block, member, bit)
            multiply(block)
    out = state["out"][0]
    return (*state["adam"], out.reshape(hidden.shape[:2] + out.shape))


def solution(mesh):
    weights = P(None, "replica", "shard")
    tokens = P("replica", "shard", None, None)
    return jax.shard_map(
        functools.partial(body, mesh.shape["shard"], mesh.shape["replica"]),
        mesh=mesh,
        in_specs=(weights, weights, weights, weights, tokens, P(), P()),
        out_specs=(weights, weights, weights, tokens),
        check_vma=False,
    )
```

```python
import collections
import functools
import math

import jax
import jax.numpy as jnp
from jax import lax
from jax.experimental import pallas as pl
from jax.experimental.pallas import tpu as pltpu
from jax.sharding import PartitionSpec as P

QB = 128
GROUP = 32
VMEM_LIMIT = 60 * 1024 * 1024
PRODUCT_LIMIT = 16 * 1024 * 1024

beta_one = 0.9
beta_two = 0.95
learn_rate = 0.004
adam_epsilon = 1e-08
step_count = 10.0
quant_limit = 448.0
scale_epsilon = 1e-06
first_fix = 1.0 - beta_one**step_count
second_fix = 1.0 - beta_two**step_count
second_root = second_fix**0.5
step_size = learn_rate / first_fix * second_root
root_epsilon = adam_epsilon * second_root

TOKEN = (132 * 1024, 128)
WHOLE = pl.BlockSpec(memory_space=pl.ANY)
SMALL_COST = pl.CostEstimate(flops=0, bytes_accessed=65536, transcendentals=0)


def like(array):
    return jax.ShapeDtypeStruct(array.shape, array.dtype)


def fence_kernel(*refs):
    pass


def fence(arrays):
    return pl.pallas_call(
        fence_kernel,
        in_specs=[WHOLE] * len(arrays),
        out_specs=[WHOLE] * len(arrays),
        out_shape=[like(array) for array in arrays],
        input_output_aliases={i: i for i in range(len(arrays))},
        compiler_params=pltpu.CompilerParams(vmem_limit_bytes=1024 * 1024),
        cost_estimate=SMALL_COST,
        name="arrival_order",
    )(*arrays)


def adam_kernel(base, blocks, passed, owner, *refs):
    arrays, outs = refs[:4], refs[4 + passed : 7 + passed]
    sends = refs[7 + passed : 7 + passed + blocks]
    *buffers, semaphores = refs[-9:]
    master, gradient, first, second, new_master, new_first, new_second, sent = buffers
    experts, rows, columns = arrays[0].shape
    shard = lax.axis_index("shard")
    bands = rows // QB
    starts = range(0, columns, QB)

    def copies(chunk, inward):
        n, i = chunk // bands, chunk % bands
        expert = jnp.int32(0)
        for candidate in range(experts):
            expert = jnp.where(owner[candidate] == shard ^ (base + n), candidate, expert)
        span = pl.ds(pl.multiple_of(i * QB, QB), QB)
        for k, ref in enumerate(arrays if inward else outs):
            far, near = ref.at[expert, span], buffers[k if inward else 4 + k].at[n, span]
            pair = (far, near) if inward else (near, far)
            yield pltpu.make_async_copy(*pair, semaphores.at[chunk, k if inward else 4 + k])

    def send_copy(chunk, block):
        span = pl.ds(pl.multiple_of(chunk % bands * QB, QB), QB)
        return pltpu.make_async_copy(
            sent.at[block, span], sends[block].at[span], semaphores.at[chunk, 7]
        )

    def begin(chunk, carry):
        for copy in copies(chunk, True):
            copy.start()
        return carry

    def work(chunk, carry):
        for copy in copies(chunk, True):
            copy.wait()
        n, i = chunk // bands, chunk % bands

        def span(group):
            return pl.ds(pl.multiple_of(i * QB + group * GROUP, GROUP), GROUP)

        def update(group, peaks):
            found = []
            for start, peak in zip(starts, peaks):
                at = (n, span(group), slice(start, start + QB))
                grad = gradient[at].astype(jnp.float32)
                moment_one = beta_one * first[at].astype(jnp.float32) + (1.0 - beta_one) * grad
                moment_two = beta_two * second[at].astype(jnp.float32) + (
                    ((1.0 - beta_two) * grad) * grad
                )
                new_first[at] = moment_one.astype(jnp.bfloat16)
                new_second[at] = moment_two.astype(jnp.bfloat16)
                guess = lax.rsqrt(moment_two)
                root = moment_two * guess + root_epsilon
                inverse = guess * (2.0 - root * guess)
                updated = master[at] - (step_size * moment_one) * inverse
                new_master[at] = updated
                sizes = jnp.abs(updated).reshape(GROUP // 8, 8, QB)
                found.append(jnp.maximum(peak, jnp.max(sizes, axis=0)))
            return tuple(found)

        empty = tuple(jnp.zeros((8, QB), jnp.float32) for _ in starts)
        peaks = lax.fori_loop(0, QB // GROUP, update, empty)
        peaks = [jnp.max(peak, axis=0, keepdims=True) for peak in peaks]
        largest = jnp.max(jnp.concatenate(peaks, axis=0), axis=1, keepdims=True)
        scale = ((largest + scale_epsilon) * (1.0 / quant_limit)).astype(jnp.bfloat16)
        scale = jnp.broadcast_to(scale, (len(peaks), QB))
        inverse_scale = 1.0 / scale.astype(jnp.float32)

        def quantize(group, carry):
            for block, start in enumerate(starts):
                at = (n, span(group), slice(start, start + QB))
                one = slice(block, block + 1)
                quantized = (new_master[at] * inverse_scale[one]).astype(jnp.bfloat16)
                sent[at] = quantized * scale[one]
            return carry

        lax.fori_loop(0, QB // GROUP, quantize, 0)
        for copy in copies(chunk, False):
            copy.start()
        for block in range(blocks):

            @pl.when(n == block)
            def _():
                send_copy(chunk, block).start()

        return carry

    def finish(chunk, carry):
        for copy in copies(chunk, False):
            copy.wait()
        send_copy(chunk, 0).wait()
        return carry

    for part in (begin, work, finish):
        lax.fori_loop(0, blocks * bands, part, 0)


def adam_blocks(base, blocks, owner, arrays, carried, token, fenced):
    _, rows, columns = arrays[0].shape
    passed = len(carried) + len(token)
    made = [like(arrays[0]), like(arrays[2]), like(arrays[3])]
    made += [jax.ShapeDtypeStruct((rows, columns), jnp.bfloat16)] * blocks
    aliases = {5 + i: i for i in range(len(carried))}
    if token:
        aliases[5 + len(carried)] = len(made)
    made += [jax.ShapeDtypeStruct(TOKEN, jnp.float32)] * fenced
    kinds = [jnp.float32, jnp.bfloat16, jnp.bfloat16, jnp.bfloat16] * 2
    results = pl.pallas_call(
        functools.partial(adam_kernel, base, blocks, passed),
        in_specs=[pl.BlockSpec(memory_space=pltpu.SMEM)] + [WHOLE] * (4 + passed),
        out_specs=[WHOLE] * len(made),
        out_shape=made,
        scratch_shapes=[pltpu.VMEM((blocks, rows, columns), kind) for kind in kinds]
        + [pltpu.SemaphoreType.DMA((blocks * (rows // QB), 8))],
        input_output_aliases=aliases,
        compiler_params=pltpu.CompilerParams(vmem_limit_bytes=VMEM_LIMIT),
        cost_estimate=SMALL_COST,
        name="adam_quantize",
    )(owner, *arrays, *carried, *token)
    return results[:3], results[3 : 3 + blocks], tuple(results[3 + blocks :])


def product_kernel(slabs, sources, places, left, *refs):
    out = refs[-1]
    rows, breadth = refs[0].shape[0], out.shape[1]
    parts = [left[:, pl.ds(pl.multiple_of(places[i] * rows, QB), rows)] for i in range(slabs)]
    span = pl.ds(pl.multiple_of(pl.program_id(0) * breadth, QB), breadth)
    total = jnp.dot(
        jnp.concatenate(parts, axis=1),
        jnp.concatenate([right[:, span] for right in refs[:slabs]], axis=0),
        preferred_element_type=jnp.float32,
    )
    out[...] = total.astype(out.dtype)


def product(number, sources, places, token_rows, weights, breadth, carried, token):
    slabs = len(weights)
    tokens, units = token_rows.shape
    rows, columns = weights[0].shape
    passed = len(token) + len(carried)
    tile = math.gcd(columns, 2 * QB)

    def place(i, sources, places):
        return 0, sources[number] * (columns // tile) + i

    *token, out = pl.pallas_call(
        functools.partial(product_kernel, slabs),
        grid_spec=pltpu.PrefetchScalarGridSpec(
            num_scalar_prefetch=2,
            grid=(columns // tile,),
            in_specs=[pl.BlockSpec(memory_space=pltpu.VMEM)] * (1 + slabs) + [WHOLE] * passed,
            out_specs=[WHOLE] * len(token)
            + [pl.BlockSpec((tokens, tile), place)],
        ),
        out_shape=[like(array) for array in token]
            + [jax.ShapeDtypeStruct((tokens, breadth), jnp.bfloat16)],
        input_output_aliases={3 + slabs + i: i for i in range(passed)},
        compiler_params=pltpu.CompilerParams(vmem_limit_bytes=PRODUCT_LIMIT),
        cost_estimate=SMALL_COST,
        name="expert_product",
    )(sources, places, token_rows, *weights, *token, *carried)
    return (out,), tuple(token)


def swap(value, axis, size, mask):
    return lax.ppermute(value, axis, [(i, i ^ mask) for i in range(size)])


def body(shards, replicas, *arguments):
    *arrays, hidden, owner_of_expert, slab_order = arguments
    shard = lax.axis_index("shard").astype(jnp.int32)
    replica = lax.axis_index("replica").astype(jnp.int32)
    token_rows = hidden.reshape(hidden.shape[2:])
    breadth = arrays[0].shape[2] * shards
    bits = [1 << i for i in range((replicas - 1).bit_length())]
    members = jnp.arange(replicas, dtype=jnp.int32)
    sources = shard ^ jnp.arange(shards, dtype=jnp.int32)
    places = jnp.sum(
        jnp.where((replica ^ members)[:, None] == members[None, :], slab_order[None, :], 0), axis=1
    ).astype(jnp.int32)

    pairs = shards // 2
    fenced = len(bits) == 2 and pairs > 1
    held = [{} for _ in range(shards)]
    made, due, ready = {}, collections.defaultdict(list), set()
    state = {"adam": (), "token": (), "out": ()}

    def adam(base, blocks):
        state["adam"], sends, state["token"] = adam_blocks(
            base, blocks, owner_of_expert, arrays, tuple(state["adam"]), state["token"], fenced
        )
        made.update(zip(range(base, base + blocks), sends))

    def deliver(block):
        held[block][0] = swap(made[block], "shard", shards, block) if block else made[block]

    def send(block, member, bit):
        held[block][member ^ bit] = swap(held[block][member], "replica", replicas, bit)

    def arrived(keys, leaving):
        waiting = [held[b][m] for b, m in keys] + [made[b] for b in leaving]
        token, *passed = fence([*state["token"], *waiting])
        state["token"] = (token,)
        made.update(zip(leaving, passed[len(keys) :]))
        for (block, member), array in zip(keys, passed):
            held[block][member] = array
        ready.update(keys)

    def multiply(block):
        ordered = [held[block][member] for member in range(replicas)]
        state["out"], state["token"] = product(
            block, sources, places, token_rows, ordered, breadth, state["out"], state["token"]
        )

    waiting = list(range(shards))
    if fenced:
        fences = collections.defaultdict(lambda: ([], [], []))

        def plan(step, until, *keys):
            fences[step][1].extend(keys)
            fences[until][0].extend((block, member ^ bit) for block, member, bit in keys)

        plan(0, 2, (1, 0, 1), (1, 0, 2))
        plan(0, 3, (0, 1, 2))
        plan(2, 3, (1, 2, 1))
        plan(2.5, 4, (3, 0, 2), (2, 0, 1))
        plan(3, 5, (2, 0, 2), (3, 0, 1))
        plan(4, 6, (2, 1, 2), (3, 2, 1))
        for pair in range(2, pairs):
            even, odd, step = 2 * pair, 2 * pair + 1, 3 * pair
            if pair + 1 < pairs:
                plan(step - 1, step + 1, (even, 0, 1), (odd, 0, 2))
                plan(step, step + 2, (even, 0, 2), (odd, 0, 1))
                plan(step + 1, step + 3, (even, 1, 2), (odd, 2, 1))
            else:
                plan(step - 1, step + 1, (even, 0, 1), (even, 0, 2))
                plan(step, step + 2, (odd, 0, 1), (odd, 0, 2))
                plan(step + 1, step + 3, (even, 1, 2))
                plan(step + 2, step + 4, (odd, 2, 1))
        for block in range(4, shards):
            first = min(2 * block - 7, 3 * (block // 2) - 3)
            if first > 1:
                fences[first][2].append(block)
            fences[first + 2][0].append((block, 0))
        fences[0][0].extend([(1, 0), (0, 1), (0, 2)])
        fences[2.5][0].extend([(2, 0), (3, 0)])

        adam(0, 2)
        deliver(0)
        deliver(1)
        ready.add((0, 0))
        send(0, 0, 1)
        send(0, 0, 2)
        adam(2, 2)
        deliver(2)
        deliver(3)
        computed = 4
        for step in sorted(fences):
            keys, sending, leaving = fences[step]
            arrived(keys, leaving)
            for block in leaving:
                deliver(block)
            for key in sending:
                send(*key)
            if computed < shards:
                adam(computed, 2)
                if not step:
                    deliver(computed)
                computed += 2
            for block in list(waiting):
                if all((block, member) in ready for member in range(replicas)):
                    multiply(block)
                    waiting.remove(block)
    else:
        for pair in range(pairs):
            adam(2 * pair, 2)
        for block in range(shards):
            deliver(block)
            for number in range(len(bits)):
                bit = bits[(number + block) % len(bits)]
                for member in list(held[block]):
                    send(block, member, bit)
            multiply(block)
    out = state["out"][0]
    return (*state["adam"], out.reshape(hidden.shape[:2] + out.shape))


def solution(mesh):
    weights = P(None, "replica", "shard")
    tokens = P("replica", "shard", None, None)
    return jax.shard_map(
        functools.partial(body, mesh.shape["shard"], mesh.shape["replica"]),
        mesh=mesh,
        in_specs=(weights, weights, weights, weights, tokens, P(), P()),
        out_specs=(weights, weights, weights, tokens),
        check_vma=False,
    )
```

```python
import collections
import functools
import math

import jax
import jax.numpy as jnp
from jax import lax
from jax.experimental import pallas as pl
from jax.experimental.pallas import tpu as pltpu
from jax.sharding import PartitionSpec as P

QB = 128
GROUP = 32
VMEM_LIMIT = 60 * 1024 * 1024
LATER_LIMIT = 54 * 1024 * 1024
PRODUCT_LIMIT = 16 * 1024 * 1024

beta_one = 0.9
beta_two = 0.95
learn_rate = 0.004
adam_epsilon = 1e-08
step_count = 10.0
quant_limit = 448.0
scale_epsilon = 1e-06
first_fix = 1.0 - beta_one**step_count
second_fix = 1.0 - beta_two**step_count
second_root = second_fix**0.5
step_size = learn_rate / first_fix * second_root
root_epsilon = adam_epsilon * second_root

TOKEN = (132 * 1024, 128)
PLANNED = (4, 8)
WHOLE = pl.BlockSpec(memory_space=pl.ANY)
SMALL_COST = pl.CostEstimate(flops=0, bytes_accessed=65536, transcendentals=0)


def like(array):
    return jax.ShapeDtypeStruct(array.shape, array.dtype)


def fence_kernel(*refs):
    pass


def fence(arrays):
    return pl.pallas_call(
        fence_kernel,
        in_specs=[WHOLE] * len(arrays),
        out_specs=[WHOLE] * len(arrays),
        out_shape=[like(array) for array in arrays],
        input_output_aliases={i: i for i in range(len(arrays))},
        compiler_params=pltpu.CompilerParams(vmem_limit_bytes=1024 * 1024),
        cost_estimate=SMALL_COST,
        name="arrival_order",
    )(*arrays)


def adam_kernel(base, blocks, passed, owner, *refs):
    arrays, outs = refs[:4], refs[4 + passed : 7 + passed]
    sends = refs[7 + passed : 7 + passed + blocks]
    *buffers, semaphores = refs[-9:]
    master, gradient, first, second, new_master, new_first, new_second, sent = buffers
    experts, rows, columns = arrays[0].shape
    shard = lax.axis_index("shard")
    bands = rows // QB
    starts = range(0, columns, QB)

    def copies(chunk, inward):
        n, i = chunk // bands, chunk % bands
        expert = jnp.int32(0)
        for candidate in range(experts):
            expert = jnp.where(owner[candidate] == shard ^ (base + n), candidate, expert)
        span = pl.ds(pl.multiple_of(i * QB, QB), QB)
        for k, ref in enumerate(arrays if inward else outs):
            far, near = ref.at[expert, span], buffers[k if inward else 4 + k].at[n, span]
            pair = (far, near) if inward else (near, far)
            yield pltpu.make_async_copy(*pair, semaphores.at[chunk, k if inward else 4 + k])

    def send_copy(chunk, block):
        span = pl.ds(pl.multiple_of(chunk % bands * QB, QB), QB)
        return pltpu.make_async_copy(
            sent.at[block, span], sends[block].at[span], semaphores.at[chunk, 7]
        )

    def begin(chunk, carry):
        for copy in copies(chunk, True):
            copy.start()
        return carry

    def work(chunk, carry):
        for copy in copies(chunk, True):
            copy.wait()
        n, i = chunk // bands, chunk % bands

        def span(group):
            return pl.ds(pl.multiple_of(i * QB + group * GROUP, GROUP), GROUP)

        def update(group, peaks):
            found = []
            for start, peak in zip(starts, peaks):
                at = (n, span(group), slice(start, start + QB))
                grad = gradient[at].astype(jnp.float32)
                moment_one = beta_one * first[at].astype(jnp.float32) + (1.0 - beta_one) * grad
                moment_two = beta_two * second[at].astype(jnp.float32) + (
                    ((1.0 - beta_two) * grad) * grad
                )
                new_first[at] = moment_one.astype(jnp.bfloat16)
                new_second[at] = moment_two.astype(jnp.bfloat16)
                guess = lax.rsqrt(moment_two)
                root = moment_two * guess + root_epsilon
                inverse = guess * (2.0 - root * guess)
                updated = master[at] - (step_size * moment_one) * inverse
                new_master[at] = updated
                sizes = jnp.abs(updated).reshape(GROUP // 8, 8, QB)
                found.append(jnp.maximum(peak, jnp.max(sizes, axis=0)))
            return tuple(found)

        empty = tuple(jnp.zeros((8, QB), jnp.float32) for _ in starts)
        peaks = lax.fori_loop(0, QB // GROUP, update, empty)
        peaks = [jnp.max(peak, axis=0, keepdims=True) for peak in peaks]
        largest = jnp.max(jnp.concatenate(peaks, axis=0), axis=1, keepdims=True)
        scale = ((largest + scale_epsilon) * (1.0 / quant_limit)).astype(jnp.bfloat16)
        scale = jnp.broadcast_to(scale, (len(peaks), QB))
        inverse_scale = 1.0 / scale.astype(jnp.float32)

        def quantize(group, carry):
            for block, start in enumerate(starts):
                at = (n, span(group), slice(start, start + QB))
                one = slice(block, block + 1)
                quantized = (new_master[at] * inverse_scale[one]).astype(jnp.bfloat16)
                sent[at] = quantized * scale[one]
            return carry

        lax.fori_loop(0, QB // GROUP, quantize, 0)
        for copy in copies(chunk, False):
            copy.start()
        for block in range(blocks):

            @pl.when(n == block)
            def _():
                send_copy(chunk, block).start()

        return carry

    def finish(chunk, carry):
        for copy in copies(chunk, False):
            copy.wait()
        send_copy(chunk, 0).wait()
        return carry

    for part in (begin, work, finish):
        lax.fori_loop(0, blocks * bands, part, 0)


def adam_blocks(base, blocks, owner, arrays, carried, token, fenced, limit):
    _, rows, columns = arrays[0].shape
    passed = len(carried) + len(token)
    made = [like(arrays[0]), like(arrays[2]), like(arrays[3])]
    made += [jax.ShapeDtypeStruct((rows, columns), jnp.bfloat16)] * blocks
    aliases = {5 + i: i for i in range(len(carried))}
    if token:
        aliases[5 + len(carried)] = len(made)
    made += [jax.ShapeDtypeStruct(TOKEN, jnp.float32)] * fenced
    kinds = [jnp.float32, jnp.bfloat16, jnp.bfloat16, jnp.bfloat16] * 2
    results = pl.pallas_call(
        functools.partial(adam_kernel, base, blocks, passed),
        in_specs=[pl.BlockSpec(memory_space=pltpu.SMEM)] + [WHOLE] * (4 + passed),
        out_specs=[WHOLE] * len(made),
        out_shape=made,
        scratch_shapes=[pltpu.VMEM((blocks, rows, columns), kind) for kind in kinds]
        + [pltpu.SemaphoreType.DMA((blocks * (rows // QB), 8))],
        input_output_aliases=aliases,
        compiler_params=pltpu.CompilerParams(vmem_limit_bytes=limit),
        cost_estimate=SMALL_COST,
        name="adam_quantize",
    )(owner, *arrays, *carried, *token)
    return results[:3], results[3 : 3 + blocks], tuple(results[3 + blocks :])


def product_kernel(slabs, sources, places, left, *refs):
    out = refs[-1]
    rows, breadth = refs[0].shape[0], out.shape[1]
    parts = [left[:, pl.ds(pl.multiple_of(places[i] * rows, QB), rows)] for i in range(slabs)]
    span = pl.ds(pl.multiple_of(pl.program_id(0) * breadth, QB), breadth)
    total = jnp.dot(
        jnp.concatenate(parts, axis=1),
        jnp.concatenate([right[:, span] for right in refs[:slabs]], axis=0),
        preferred_element_type=jnp.float32,
    )
    out[...] = total.astype(out.dtype)


def product(number, sources, places, token_rows, weights, breadth, carried, token):
    slabs = len(weights)
    tokens, units = token_rows.shape
    rows, columns = weights[0].shape
    passed = len(token) + len(carried)
    tile = math.gcd(columns, 2 * QB)

    def place(i, sources, places):
        return 0, sources[number] * (columns // tile) + i

    *token, out = pl.pallas_call(
        functools.partial(product_kernel, slabs),
        grid_spec=pltpu.PrefetchScalarGridSpec(
            num_scalar_prefetch=2,
            grid=(columns // tile,),
            in_specs=[pl.BlockSpec(memory_space=pltpu.VMEM)] * (1 + slabs) + [WHOLE] * passed,
            out_specs=[WHOLE] * len(token)
            + [pl.BlockSpec((tokens, tile), place)],
        ),
        out_shape=[like(array) for array in token]
            + [jax.ShapeDtypeStruct((tokens, breadth), jnp.bfloat16)],
        input_output_aliases={3 + slabs + i: i for i in range(passed)},
        compiler_params=pltpu.CompilerParams(vmem_limit_bytes=PRODUCT_LIMIT),
        cost_estimate=SMALL_COST,
        name="expert_product",
    )(sources, places, token_rows, *weights, *token, *carried)
    return (out,), tuple(token)


def swap(value, axis, size, mask):
    return lax.ppermute(value, axis, [(i, i ^ mask) for i in range(size)])


def body(shards, replicas, *arguments):
    *arrays, hidden, owner_of_expert, slab_order = arguments
    shard = lax.axis_index("shard").astype(jnp.int32)
    replica = lax.axis_index("replica").astype(jnp.int32)
    token_rows = hidden.reshape(hidden.shape[2:])
    breadth = arrays[0].shape[2] * shards
    bits = [1 << i for i in range((replicas - 1).bit_length())]
    members = jnp.arange(replicas, dtype=jnp.int32)
    sources = shard ^ jnp.arange(shards, dtype=jnp.int32)
    places = jnp.sum(
        jnp.where((replica ^ members)[:, None] == members[None, :], slab_order[None, :], 0), axis=1
    ).astype(jnp.int32)

    pairs = shards // 2
    fenced = (replicas, shards) == PLANNED
    held = [{} for _ in range(shards)]
    made, due, ready = {}, collections.defaultdict(list), set()
    state = {"adam": (), "token": (), "out": ()}

    def adam(base, blocks, limit):
        state["adam"], sends, state["token"] = adam_blocks(
            base, blocks, owner_of_expert, arrays, tuple(state["adam"]), state["token"], fenced, limit
        )
        made.update(zip(range(base, base + blocks), sends))

    def deliver(block):
        held[block][0] = swap(made[block], "shard", shards, block) if block else made[block]

    def send(block, member, bit):
        held[block][member ^ bit] = swap(held[block][member], "replica", replicas, bit)

    def arrived(keys, leaving):
        waiting = [held[b][m] for b, m in keys] + [made[b] for b in leaving]
        token, *passed = fence([*state["token"], *waiting])
        state["token"] = (token,)
        made.update(zip(leaving, passed[len(keys) :]))
        for (block, member), array in zip(keys, passed):
            held[block][member] = array
        ready.update(keys)

    def multiply(block):
        ordered = [held[block][member] for member in range(replicas)]
        state["out"], state["token"] = product(
            block, sources, places, token_rows, ordered, breadth, state["out"], state["token"]
        )

    waiting = list(range(shards))
    if fenced:
        plan = [
            ([(1, 0), (0, 1), (0, 2)], [(1, 0, 1), (1, 0, 2)], []),
            ([(1, 1), (1, 2)], [(0, 1, 2), (1, 2, 1)], []),
            ([(2, 0), (3, 0), (4, 0)], [(3, 0, 2), (2, 0, 1)], []),
            ([(0, 3), (1, 3)], [(2, 0, 2), (3, 0, 1)], [5]),
            ([(2, 1), (3, 2)], [(2, 1, 2), (3, 2, 1)], []),
            ([(2, 2), (3, 1), (5, 0)], [(4, 0, 1), (4, 0, 2)], [6]),
            ([(2, 3), (3, 3)], [(5, 0, 1), (5, 0, 2)], []),
            ([(4, 1), (4, 2)], [(4, 1, 2)], []),
            ([(6, 0), (5, 1), (5, 2)], [(6, 0, 1), (6, 0, 2), (5, 2, 1)], [7]),
            ([(4, 3), (5, 3)], [], []),
            ([(6, 1), (6, 2)], [(6, 1, 2)], []),
            ([(7, 0)], [(7, 0, 1), (7, 0, 2)], []),
            ([(6, 3)], [], []),
            ([(7, 1), (7, 2)], [(7, 2, 1)], []),
            ([(7, 3)], [], []),
        ]
        adam(0, 2, VMEM_LIMIT)
        deliver(0)
        deliver(1)
        ready.add((0, 0))
        send(0, 0, 1)
        send(0, 0, 2)
        adam(2, 4, VMEM_LIMIT)
        for block in (4, 2, 3):
            deliver(block)
        for step, (keys, sending, leaving) in enumerate(plan):
            arrived(keys, leaving)
            for block in leaving:
                deliver(block)
            for key in sending:
                send(*key)
            if not step:
                adam(6, 2, LATER_LIMIT)
            for block in list(waiting):
                if all((block, member) in ready for member in range(replicas)):
                    multiply(block)
                    waiting.remove(block)
    else:
        for pair in range(pairs):
            adam(2 * pair, 2, VMEM_LIMIT)
        for block in range(shards):
            deliver(block)
            for number in range(len(bits)):
                bit = bits[(number + block) % len(bits)]
                for member in list(held[block]):
                    send(block, member, bit)
            multiply(block)
    out = state["out"][0]
    return (*state["adam"], out.reshape(hidden.shape[:2] + out.shape))


def solution(mesh):
    weights = P(None, "replica", "shard")
    tokens = P("replica", "shard", None, None)
    return jax.shard_map(
        functools.partial(body, mesh.shape["shard"], mesh.shape["replica"]),
        mesh=mesh,
        in_specs=(weights, weights, weights, weights, tokens, P(), P()),
        out_specs=(weights, weights, weights, tokens),
        check_vma=False,
    )
```

```python
import collections
import functools
import math

import jax
import jax.numpy as jnp
from jax import lax
from jax.experimental import pallas as pl
from jax.experimental.pallas import tpu as pltpu
from jax.sharding import PartitionSpec as P

QB = 128
GROUP = 32
VMEM_LIMIT = 60 * 1024 * 1024
PRODUCT_LIMIT = 16 * 1024 * 1024

beta_one = 0.9
beta_two = 0.95
learn_rate = 0.004
adam_epsilon = 1e-08
step_count = 10.0
quant_limit = 448.0
scale_epsilon = 1e-06
first_fix = 1.0 - beta_one**step_count
second_fix = 1.0 - beta_two**step_count
second_root = second_fix**0.5
step_size = learn_rate / first_fix * second_root
root_epsilon = adam_epsilon * second_root

TOKEN = (132 * 1024, 128)
PLANNED = (4, 8)
WHOLE = pl.BlockSpec(memory_space=pl.ANY)
SMALL_COST = pl.CostEstimate(flops=0, bytes_accessed=65536, transcendentals=0)


def like(array):
    return jax.ShapeDtypeStruct(array.shape, array.dtype)


def fence_kernel(*refs):
    pass


def fence(arrays):
    return pl.pallas_call(
        fence_kernel,
        in_specs=[WHOLE] * len(arrays),
        out_specs=[WHOLE] * len(arrays),
        out_shape=[like(array) for array in arrays],
        input_output_aliases={i: i for i in range(len(arrays))},
        compiler_params=pltpu.CompilerParams(vmem_limit_bytes=1024 * 1024),
        cost_estimate=SMALL_COST,
        name="arrival_order",
    )(*arrays)


def adam_kernel(groups, passed, owner, *refs):
    arrays, outs = refs[:4], refs[4 + passed : 7 + passed]
    sends = refs[7 + passed : 7 + passed + len(groups)]
    base, blocks = groups[0][0], sum(map(len, groups))
    *buffers, semaphores = refs[-9:]
    master, gradient, first, second, new_master, new_first, new_second, sent = buffers
    experts, rows, columns = arrays[0].shape
    shard = lax.axis_index("shard")
    bands = rows // QB
    starts = range(0, columns, QB)

    def copies(chunk, inward):
        n, i = chunk // bands, chunk % bands
        expert = jnp.int32(0)
        for candidate in range(experts):
            expert = jnp.where(owner[candidate] == shard ^ (base + n), candidate, expert)
        span = pl.ds(pl.multiple_of(i * QB, QB), QB)
        for k, ref in enumerate(arrays if inward else outs):
            far, near = ref.at[expert, span], buffers[k if inward else 4 + k].at[n, span]
            pair = (far, near) if inward else (near, far)
            yield pltpu.make_async_copy(*pair, semaphores.at[chunk, k if inward else 4 + k])

    def send_copy(chunk, group, member):
        span = pl.ds(pl.multiple_of(chunk % bands * QB, QB), QB)
        n = groups[group][member] - base
        far = sends[group].at[member, span]
        return pltpu.make_async_copy(sent.at[n, span], far, semaphores.at[chunk, 7])

    def begin(chunk, carry):
        for copy in copies(chunk, True):
            copy.start()
        return carry

    def work(chunk, carry):
        for copy in copies(chunk, True):
            copy.wait()
        n, i = chunk // bands, chunk % bands

        def span(group):
            return pl.ds(pl.multiple_of(i * QB + group * GROUP, GROUP), GROUP)

        def update(group, peaks):
            found = []
            for start, peak in zip(starts, peaks):
                at = (n, span(group), slice(start, start + QB))
                grad = gradient[at].astype(jnp.float32)
                moment_one = beta_one * first[at].astype(jnp.float32) + (1.0 - beta_one) * grad
                moment_two = beta_two * second[at].astype(jnp.float32) + (
                    ((1.0 - beta_two) * grad) * grad
                )
                new_first[at] = moment_one.astype(jnp.bfloat16)
                new_second[at] = moment_two.astype(jnp.bfloat16)
                guess = lax.rsqrt(moment_two)
                root = moment_two * guess + root_epsilon
                inverse = guess * (2.0 - root * guess)
                updated = master[at] - (step_size * moment_one) * inverse
                new_master[at] = updated
                sizes = jnp.abs(updated).reshape(GROUP // 8, 8, QB)
                found.append(jnp.maximum(peak, jnp.max(sizes, axis=0)))
            return tuple(found)

        empty = tuple(jnp.zeros((8, QB), jnp.float32) for _ in starts)
        peaks = lax.fori_loop(0, QB // GROUP, update, empty)
        peaks = [jnp.max(peak, axis=0, keepdims=True) for peak in peaks]
        largest = jnp.max(jnp.concatenate(peaks, axis=0), axis=1, keepdims=True)
        scale = ((largest + scale_epsilon) * (1.0 / quant_limit)).astype(jnp.bfloat16)
        scale = jnp.broadcast_to(scale, (len(peaks), QB))
        inverse_scale = 1.0 / scale.astype(jnp.float32)

        def quantize(group, carry):
            for block, start in enumerate(starts):
                at = (n, span(group), slice(start, start + QB))
                one = slice(block, block + 1)
                quantized = (new_master[at] * inverse_scale[one]).astype(jnp.bfloat16)
                sent[at] = quantized * scale[one]
            return carry

        lax.fori_loop(0, QB // GROUP, quantize, 0)
        for copy in copies(chunk, False):
            copy.start()
        for group, numbers in enumerate(groups):
            for member, number in enumerate(numbers):

                @pl.when(n == number - base)
                def _():
                    send_copy(chunk, group, member).start()

        return carry

    def finish(chunk, carry):
        for copy in copies(chunk, False):
            copy.wait()
        send_copy(chunk, 0, 0).wait()
        return carry

    for part in (begin, work, finish):
        lax.fori_loop(0, blocks * bands, part, 0)


def adam_blocks(groups, owner, arrays, carried, fenced):
    _, rows, columns = arrays[0].shape
    blocks, passed = sum(map(len, groups)), len(carried)
    made = [like(arrays[0]), like(arrays[2]), like(arrays[3])]
    made += [jax.ShapeDtypeStruct((len(group), rows, columns), jnp.bfloat16) for group in groups]
    made += [jax.ShapeDtypeStruct(TOKEN, jnp.float32)] * fenced
    kinds = [jnp.float32, jnp.bfloat16, jnp.bfloat16, jnp.bfloat16] * 2
    results = pl.pallas_call(
        functools.partial(adam_kernel, groups, passed),
        in_specs=[pl.BlockSpec(memory_space=pltpu.SMEM)] + [WHOLE] * (4 + passed),
        out_specs=[WHOLE] * len(made),
        out_shape=made,
        scratch_shapes=[pltpu.VMEM((blocks, rows, columns), kind) for kind in kinds]
        + [pltpu.SemaphoreType.DMA((blocks * (rows // QB), 8))],
        input_output_aliases={5 + i: i for i in range(passed)},
        compiler_params=pltpu.CompilerParams(vmem_limit_bytes=VMEM_LIMIT),
        cost_estimate=SMALL_COST,
        name="adam_quantize",
    )(owner, *arrays, *carried)
    return results[:3], results[3 : 3 + len(groups)], tuple(results[3 + len(groups) :])


def join_kernel(picks, *refs):
    out, semaphores = refs[-2:]
    pieces = [
        pltpu.make_async_copy(refs[1 + place].at[pick], out.at[place], semaphores.at[place])
        for place, pick in enumerate(picks)
    ]
    for piece in pieces:
        piece.start()
    for piece in pieces:
        piece.wait()


def join(token, arrays, picks):
    count = len(arrays)
    shape = jax.ShapeDtypeStruct((count, *arrays[0].shape[1:]), arrays[0].dtype)
    return pl.pallas_call(
        functools.partial(join_kernel, picks),
        in_specs=[WHOLE] * (1 + count),
        out_specs=[WHOLE] * 2,
        out_shape=[like(token), shape],
        scratch_shapes=[pltpu.SemaphoreType.DMA((count,))],
        input_output_aliases={0: 0},
        compiler_params=pltpu.CompilerParams(vmem_limit_bytes=1024 * 1024),
        cost_estimate=SMALL_COST,
        name="join_blocks",
    )(token, *arrays)


def product_kernel(slabs, sources, places, left, *refs):
    out = refs[-1]
    rows, breadth = refs[0].shape[1], out.shape[1]
    parts = [left[:, pl.ds(pl.multiple_of(places[i] * rows, QB), rows)] for i in range(slabs)]
    block = pl.program_id(0)
    span = pl.ds(pl.multiple_of(pl.program_id(1) * breadth, QB), breadth)
    total = jnp.dot(
        jnp.concatenate(parts, axis=1),
        jnp.concatenate([right[block, :, span] for right in refs[:slabs]], axis=0),
        preferred_element_type=jnp.float32,
    )
    out[...] = total.astype(out.dtype)


def product(number, sources, places, token_rows, weights, breadth, carried, token):
    slabs = len(weights)
    tokens, units = token_rows.shape
    blocks, rows, columns = weights[0].shape
    passed = len(token) + len(carried)
    tile = math.gcd(columns, 2 * QB)

    def place(block, i, sources, places):
        return 0, sources[number + block] * (columns // tile) + i

    *token, out = pl.pallas_call(
        functools.partial(product_kernel, slabs),
        grid_spec=pltpu.PrefetchScalarGridSpec(
            num_scalar_prefetch=2,
            grid=(blocks, columns // tile),
            in_specs=[pl.BlockSpec(memory_space=pltpu.VMEM)] * (1 + slabs) + [WHOLE] * passed,
            out_specs=[WHOLE] * len(token)
            + [pl.BlockSpec((tokens, tile), place)],
        ),
        out_shape=[like(array) for array in token]
            + [jax.ShapeDtypeStruct((tokens, breadth), jnp.bfloat16)],
        input_output_aliases={3 + slabs + i: i for i in range(passed)},
        compiler_params=pltpu.CompilerParams(vmem_limit_bytes=PRODUCT_LIMIT),
        cost_estimate=SMALL_COST,
        name="expert_product",
    )(sources, places, token_rows, *weights, *token, *carried)
    return (out,), tuple(token)


def swap(value, axis, size, mask):
    return lax.ppermute(value, axis, [(i, i ^ mask) for i in range(size)])


def body(shards, replicas, *arguments):
    *arrays, hidden, owner_of_expert, slab_order = arguments
    shard = lax.axis_index("shard").astype(jnp.int32)
    replica = lax.axis_index("replica").astype(jnp.int32)
    token_rows = hidden.reshape(hidden.shape[2:])
    breadth = arrays[0].shape[2] * shards
    bits = [1 << i for i in range((replicas - 1).bit_length())]
    members = jnp.arange(replicas, dtype=jnp.int32)
    sources = shard ^ jnp.arange(shards, dtype=jnp.int32)
    places = jnp.sum(
        jnp.where((replica ^ members)[:, None] == members[None, :], slab_order[None, :], 0), axis=1
    ).astype(jnp.int32)

    fenced = (replicas, shards) == PLANNED
    held, made, ready = collections.defaultdict(dict), {}, set()
    state = {"adam": (), "token": (), "out": ()}

    def adam(*groups):
        state["adam"], sends, state["token"] = adam_blocks(
            groups, owner_of_expert, arrays, tuple(state["adam"]), fenced
        )
        made.update({group[0]: send for group, send in zip(groups, sends)})

    def deliver(block):
        held[block][0] = swap(made[block], "shard", shards, block) if block else made[block]

    def send(block, member, bit):
        held[block][member ^ bit] = swap(held[block][member], "replica", replicas, bit)

    def arrived(keys, leaving=()):
        waiting = [held[b][m] for b, m in keys] + [made[b] for b in leaving]
        token, *passed = fence([*state["token"], *waiting])
        state["token"] = (token,)
        made.update(zip(leaving, passed[len(keys) :]))
        for (block, member), array in zip(keys, passed):
            held[block][member] = array
        ready.update(keys)

    def multiply(block):
        ordered = [held[block][member] for member in range(replicas)]
        number = int(block)
        state["out"], state["token"] = product(
            number, sources, places, token_rows, ordered, breadth, state["out"], state["token"]
        )

    if fenced:
        plan = [
            ([(0, 1), (0, 2), (1, 0)], [(1, 0, 1), (1, 0, 2), (0, 1, 2)], []),
            ([(4, 0)], [], [5]),
            (["pair", (1, 1), (1, 2)], [(1, 2, 1)], []),
            (["join", 2.0], [(2.0, 0, 1), (2.0, 0, 2)], []),
            ([(0, 3), (1, 3)], [], []),
            (["join", 4.0], [(4.0, 0, 1), (4.0, 0, 2)], [6]),
            ([(2.0, 1), (2.0, 2)], [(2.0, 1, 2)], []),
            ([(6, 0), (4.0, 1), (4.0, 2)], [(4.0, 2, 1), (6, 0, 1), (6, 0, 2)], [7]),
            ([(2.0, 3)], [], []),
            ([(7, 0)], [(7, 0, 1), (7, 0, 2)], []),
            ([(4.0, 3)], [], []),
            ([(6, 1), (6, 2)], [(6, 1, 2)], []),
            ([(7, 1), (7, 2)], [(7, 2, 1)], []),
            ([(6, 3)], [], []),
            ([(7, 3)], [], []),
        ]
        waiting = [0, 1, 2.0, 4.0, 6, 7]
        adam((0,), (1,), (2, 3), (4,), (5,), (6,), (7,))
        for block in (0, 1, 2, 4):
            deliver(block)
        ready.add((0, 0))
        send(0, 0, 1)
        send(0, 0, 2)
        for keys, sending, leaving in plan:
            if keys[0] == "pair":
                arrived([(2, 0), *keys[1:]], leaving)
                held[2.5][0] = swap(held[2][0], "shard", shards, 1)
            elif keys[0] == "join":
                pair = keys[1]
                one, two = ((2, 2.5) if pair == 2 else (4, 5))
                picks = (0, 1) if pair == 2 else (0, 0)
                token, held[pair][0] = join(
                    state["token"][0], [held[one][0], held[two][0]], picks
                )
                state["token"] = (token,)
                ready.add((pair, 0))
            else:
                arrived(keys, leaving)
            for block in leaving:
                deliver(block)
            for key in sending:
                send(*key)
            for block in list(waiting):
                if all((block, member) in ready for member in range(replicas)):
                    multiply(block)
                    waiting.remove(block)
    else:
        for pair in range(0, shards, 2):
            adam((pair,), (pair + 1,))
        for block in range(shards):
            deliver(block)
            for number in range(len(bits)):
                bit = bits[(number + block) % len(bits)]
                for member in list(held[block]):
                    send(block, member, bit)
            multiply(block)
    out = state["out"][0]
    return (*state["adam"], out.reshape(hidden.shape[:2] + out.shape))


def solution(mesh):
    weights = P(None, "replica", "shard")
    tokens = P("replica", "shard", None, None)
    return jax.shard_map(
        functools.partial(body, mesh.shape["shard"], mesh.shape["replica"]),
        mesh=mesh,
        in_specs=(weights, weights, weights, weights, tokens, P(), P()),
        out_specs=(weights, weights, weights, tokens),
        check_vma=False,
    )
```

```python
import collections
import functools
import math

import jax
import jax.numpy as jnp
from jax import lax
from jax.experimental import pallas as pl
from jax.experimental.pallas import tpu as pltpu
from jax.sharding import PartitionSpec as P

QB = 128
GROUP = 32
VMEM_LIMIT = 60 * 1024 * 1024
PRODUCT_LIMIT = 16 * 1024 * 1024

beta_one = 0.9
beta_two = 0.95
learn_rate = 0.004
adam_epsilon = 1e-08
step_count = 10.0
quant_limit = 448.0
scale_epsilon = 1e-06
first_fix = 1.0 - beta_one**step_count
second_fix = 1.0 - beta_two**step_count
second_root = second_fix**0.5
step_size = learn_rate / first_fix * second_root
root_epsilon = adam_epsilon * second_root

TOKEN = (132 * 1024, 128)
PLANNED = (4, 8)
WHOLE = pl.BlockSpec(memory_space=pl.ANY)
SMALL_COST = pl.CostEstimate(flops=0, bytes_accessed=65536, transcendentals=0)


def like(array):
    return jax.ShapeDtypeStruct(array.shape, array.dtype)


def fence_kernel(*refs):
    pass


def fence(arrays):
    return pl.pallas_call(
        fence_kernel,
        in_specs=[WHOLE] * len(arrays),
        out_specs=[WHOLE] * len(arrays),
        out_shape=[like(array) for array in arrays],
        input_output_aliases={i: i for i in range(len(arrays))},
        compiler_params=pltpu.CompilerParams(vmem_limit_bytes=1024 * 1024),
        cost_estimate=SMALL_COST,
        name="arrival_order",
    )(*arrays)


def adam_kernel(groups, passed, owner, *refs):
    arrays, outs = refs[:4], refs[4 + passed : 7 + passed]
    sends = refs[7 + passed : 7 + passed + len(groups)]
    base, blocks = groups[0][0], sum(map(len, groups))
    *buffers, semaphores = refs[-9:]
    master, gradient, first, second, new_master, new_first, new_second, sent = buffers
    experts, rows, columns = arrays[0].shape
    shard = lax.axis_index("shard")
    bands = rows // QB
    starts = range(0, columns, QB)

    def copies(chunk, inward):
        n, i = chunk // bands, chunk % bands
        expert = jnp.int32(0)
        for candidate in range(experts):
            expert = jnp.where(owner[candidate] == shard ^ (base + n), candidate, expert)
        span = pl.ds(pl.multiple_of(i * QB, QB), QB)
        for k, ref in enumerate(arrays if inward else outs):
            far, near = ref.at[expert, span], buffers[k if inward else 4 + k].at[n, span]
            pair = (far, near) if inward else (near, far)
            yield pltpu.make_async_copy(*pair, semaphores.at[chunk, k if inward else 4 + k])

    def send_copy(chunk, group, member):
        span = pl.ds(pl.multiple_of(chunk % bands * QB, QB), QB)
        n = groups[group][member] - base
        far = sends[group].at[member, span]
        return pltpu.make_async_copy(sent.at[n, span], far, semaphores.at[chunk, 7])

    def begin(chunk, carry):
        for copy in copies(chunk, True):
            copy.start()
        return carry

    def work(chunk, carry):
        for copy in copies(chunk, True):
            copy.wait()
        n, i = chunk // bands, chunk % bands

        def span(group):
            return pl.ds(pl.multiple_of(i * QB + group * GROUP, GROUP), GROUP)

        def update(group, peaks):
            found = []
            for start, peak in zip(starts, peaks):
                at = (n, span(group), slice(start, start + QB))
                grad = gradient[at].astype(jnp.float32)
                moment_one = beta_one * first[at].astype(jnp.float32) + (1.0 - beta_one) * grad
                moment_two = beta_two * second[at].astype(jnp.float32) + (
                    ((1.0 - beta_two) * grad) * grad
                )
                new_first[at] = moment_one.astype(jnp.bfloat16)
                new_second[at] = moment_two.astype(jnp.bfloat16)
                guess = lax.rsqrt(moment_two)
                root = moment_two * guess + root_epsilon
                inverse = guess * (2.0 - root * guess)
                updated = master[at] - (step_size * moment_one) * inverse
                new_master[at] = updated
                sizes = jnp.abs(updated).reshape(GROUP // 8, 8, QB)
                found.append(jnp.maximum(peak, jnp.max(sizes, axis=0)))
            return tuple(found)

        empty = tuple(jnp.zeros((8, QB), jnp.float32) for _ in starts)
        peaks = lax.fori_loop(0, QB // GROUP, update, empty)
        peaks = [jnp.max(peak, axis=0, keepdims=True) for peak in peaks]
        largest = jnp.max(jnp.concatenate(peaks, axis=0), axis=1, keepdims=True)
        scale = ((largest + scale_epsilon) * (1.0 / quant_limit)).astype(jnp.bfloat16)
        scale = jnp.broadcast_to(scale, (len(peaks), QB))
        inverse_scale = 1.0 / scale.astype(jnp.float32)

        def quantize(group, carry):
            for block, start in enumerate(starts):
                at = (n, span(group), slice(start, start + QB))
                one = slice(block, block + 1)
                quantized = (new_master[at] * inverse_scale[one]).astype(jnp.bfloat16)
                sent[at] = quantized * scale[one]
            return carry

        lax.fori_loop(0, QB // GROUP, quantize, 0)
        for copy in copies(chunk, False):
            copy.start()
        for group, numbers in enumerate(groups):
            for member, number in enumerate(numbers):

                @pl.when(n == number - base)
                def _():
                    send_copy(chunk, group, member).start()

        return carry

    def finish(chunk, carry):
        for copy in copies(chunk, False):
            copy.wait()
        send_copy(chunk, 0, 0).wait()
        return carry

    for part in (begin, work, finish):
        lax.fori_loop(0, blocks * bands, part, 0)


def adam_blocks(groups, owner, arrays, carried, fenced):
    _, rows, columns = arrays[0].shape
    blocks, passed = sum(map(len, groups)), len(carried)
    made = [like(arrays[0]), like(arrays[2]), like(arrays[3])]
    made += [jax.ShapeDtypeStruct((len(group), rows, columns), jnp.bfloat16) for group in groups]
    made += [jax.ShapeDtypeStruct(TOKEN, jnp.float32)] * fenced
    kinds = [jnp.float32, jnp.bfloat16, jnp.bfloat16, jnp.bfloat16] * 2
    results = pl.pallas_call(
        functools.partial(adam_kernel, groups, passed),
        in_specs=[pl.BlockSpec(memory_space=pltpu.SMEM)] + [WHOLE] * (4 + passed),
        out_specs=[WHOLE] * len(made),
        out_shape=made,
        scratch_shapes=[pltpu.VMEM((blocks, rows, columns), kind) for kind in kinds]
        + [pltpu.SemaphoreType.DMA((blocks * (rows // QB), 8))],
        input_output_aliases={5 + i: i for i in range(passed)},
        compiler_params=pltpu.CompilerParams(vmem_limit_bytes=VMEM_LIMIT),
        cost_estimate=SMALL_COST,
        name="adam_quantize",
    )(owner, *arrays, *carried)
    return results[:3], results[3 : 3 + len(groups)], tuple(results[3 + len(groups) :])


def join_kernel(picks, *refs):
    out, semaphores = refs[-2:]
    pieces = [
        pltpu.make_async_copy(refs[1 + place].at[pick], out.at[place], semaphores.at[place])
        for place, pick in enumerate(picks)
    ]
    for piece in pieces:
        piece.start()
    for piece in pieces:
        piece.wait()


def join(token, arrays, picks):
    count = len(arrays)
    shape = jax.ShapeDtypeStruct((count, *arrays[0].shape[1:]), arrays[0].dtype)
    return pl.pallas_call(
        functools.partial(join_kernel, picks),
        in_specs=[WHOLE] * (1 + count),
        out_specs=[WHOLE] * 2,
        out_shape=[like(token), shape],
        scratch_shapes=[pltpu.SemaphoreType.DMA((count,))],
        input_output_aliases={0: 0},
        compiler_params=pltpu.CompilerParams(vmem_limit_bytes=1024 * 1024),
        cost_estimate=SMALL_COST,
        name="join_blocks",
    )(token, *arrays)


def product_kernel(slabs, sources, places, left, *refs):
    out = refs[-1]
    rows, breadth = refs[0].shape[1], out.shape[1]
    parts = [left[:, pl.ds(pl.multiple_of(places[i] * rows, QB), rows)] for i in range(slabs)]
    block = pl.program_id(0)
    span = pl.ds(pl.multiple_of(pl.program_id(1) * breadth, QB), breadth)
    total = jnp.dot(
        jnp.concatenate(parts, axis=1),
        jnp.concatenate([right[block, :, span] for right in refs[:slabs]], axis=0),
        preferred_element_type=jnp.float32,
    )
    out[...] = total.astype(out.dtype)


def product(numbers, sources, places, token_rows, weights, breadth, carried, token):
    slabs = len(weights)
    tokens, units = token_rows.shape
    blocks, rows, columns = weights[0].shape
    passed = len(token) + len(carried)
    tile = math.gcd(columns, 2 * QB)

    def place(block, i, sources, places):
        number = numbers[0] + block * (numbers[-1] - numbers[0])
        return 0, sources[number] * (columns // tile) + i

    *token, out = pl.pallas_call(
        functools.partial(product_kernel, slabs),
        grid_spec=pltpu.PrefetchScalarGridSpec(
            num_scalar_prefetch=2,
            grid=(blocks, columns // tile),
            in_specs=[pl.BlockSpec(memory_space=pltpu.VMEM)] * (1 + slabs) + [WHOLE] * passed,
            out_specs=[WHOLE] * len(token)
            + [pl.BlockSpec((tokens, tile), place)],
        ),
        out_shape=[like(array) for array in token]
            + [jax.ShapeDtypeStruct((tokens, breadth), jnp.bfloat16)],
        input_output_aliases={3 + slabs + i: i for i in range(passed)},
        compiler_params=pltpu.CompilerParams(vmem_limit_bytes=PRODUCT_LIMIT),
        cost_estimate=SMALL_COST,
        name="expert_product",
    )(sources, places, token_rows, *weights, *token, *carried)
    return (out,), tuple(token)


def swap(value, axis, size, mask):
    return lax.ppermute(value, axis, [(i, i ^ mask) for i in range(size)])


def body(shards, replicas, *arguments):
    *arrays, hidden, owner_of_expert, slab_order = arguments
    shard = lax.axis_index("shard").astype(jnp.int32)
    replica = lax.axis_index("replica").astype(jnp.int32)
    token_rows = hidden.reshape(hidden.shape[2:])
    breadth = arrays[0].shape[2] * shards
    bits = [1 << i for i in range((replicas - 1).bit_length())]
    members = jnp.arange(replicas, dtype=jnp.int32)
    sources = shard ^ jnp.arange(shards, dtype=jnp.int32)
    places = jnp.sum(
        jnp.where((replica ^ members)[:, None] == members[None, :], slab_order[None, :], 0), axis=1
    ).astype(jnp.int32)

    fenced = (replicas, shards) == PLANNED
    held, made, ready = collections.defaultdict(dict), {}, set()
    state = {"adam": (), "token": (), "out": ()}

    def adam(*groups):
        state["adam"], sends, state["token"] = adam_blocks(
            groups, owner_of_expert, arrays, tuple(state["adam"]), fenced
        )
        made.update({group[0]: send for group, send in zip(groups, sends)})

    def deliver(block):
        held[block][0] = swap(made[block], "shard", shards, block) if block else made[block]

    def send(block, member, bit):
        held[block][member ^ bit] = swap(held[block][member], "replica", replicas, bit)

    def arrived(keys, leaving=()):
        waiting = [held[b][m] for b, m in keys] + [made[b] for b in leaving]
        token, *passed = fence([*state["token"], *waiting])
        state["token"] = (token,)
        made.update(zip(leaving, passed[len(keys) :]))
        for (block, member), array in zip(keys, passed):
            held[block][member] = array
        ready.update(keys)

    def multiply(block):
        ordered = [held[block][member] for member in range(replicas)]
        numbers = block if isinstance(block, tuple) else (block,)
        state["out"], state["token"] = product(
            numbers, sources, places, token_rows, ordered, breadth, state["out"], state["token"]
        )

    if fenced:
        one, two = (2, 4), (3, 5)
        plan = [
            ([(0, 1), (0, 2), (1, 0)], [(1, 0, 1), (1, 0, 2)], []),
            ([(2, 0), (4, 0)], [], [5]),
            ([(1, 1), (1, 2)], [(1, 2, 1), (0, 1, 2)], []),
            (one, [(one, 0, 1), (one, 0, 2)], []),
            ([(0, 3), (1, 3)], [], [3]),
            (two, [(two, 0, 1), (two, 0, 2)], [6]),
            ([(one, 1), (one, 2)], [(one, 1, 2)], []),
            ([(6, 0), (two, 1), (two, 2)], [(two, 2, 1), (6, 0, 1), (6, 0, 2)], [7]),
            ([(one, 3)], [], []),
            ([(7, 0)], [(7, 0, 1), (7, 0, 2)], []),
            ([(two, 3)], [], []),
            ([(6, 1), (6, 2)], [(6, 1, 2)], []),
            ([(7, 1), (7, 2)], [(7, 2, 1)], []),
            ([(6, 3)], [], []),
            ([(7, 3)], [], []),
        ]
        waiting = [0, 1, one, two, 6, 7]
        adam(*[(block,) for block in range(shards)])
        for block in (0, 1, 2, 4):
            deliver(block)
        ready.add((0, 0))
        send(0, 0, 1)
        send(0, 0, 2)
        for keys, sending, leaving in plan:
            if isinstance(keys, tuple):
                pieces = [held[block][0] for block in keys]
                token, held[keys][0] = join(state["token"][0], pieces, (0, 0))
                state["token"] = (token,)
                ready.add((keys, 0))
            else:
                arrived(keys, leaving)
            for block in leaving:
                deliver(block)
            for key in sending:
                send(*key)
            for block in list(waiting):
                if all((block, member) in ready for member in range(replicas)):
                    multiply(block)
                    waiting.remove(block)
    else:
        for pair in range(0, shards, 2):
            adam((pair,), (pair + 1,))
        for block in range(shards):
            deliver(block)
            for number in range(len(bits)):
                bit = bits[(number + block) % len(bits)]
                for member in list(held[block]):
                    send(block, member, bit)
            multiply(block)
    out = state["out"][0]
    return (*state["adam"], out.reshape(hidden.shape[:2] + out.shape))


def solution(mesh):
    weights = P(None, "replica", "shard")
    tokens = P("replica", "shard", None, None)
    return jax.shard_map(
        functools.partial(body, mesh.shape["shard"], mesh.shape["replica"]),
        mesh=mesh,
        in_specs=(weights, weights, weights, weights, tokens, P(), P()),
        out_specs=(weights, weights, weights, tokens),
        check_vma=False,
    )
```

```python
import collections
import functools
import math

import jax
import jax.numpy as jnp
from jax import lax
from jax.experimental import pallas as pl
from jax.experimental.pallas import tpu as pltpu
from jax.sharding import PartitionSpec as P

QB = 128
GROUP = 32
VMEM_LIMIT = 60 * 1024 * 1024
LATER_LIMIT = 56 * 1024 * 1024
PRODUCT_LIMIT = 16 * 1024 * 1024

beta_one = 0.9
beta_two = 0.95
learn_rate = 0.004
adam_epsilon = 1e-08
step_count = 10.0
quant_limit = 448.0
scale_epsilon = 1e-06
first_fix = 1.0 - beta_one**step_count
second_fix = 1.0 - beta_two**step_count
second_root = second_fix**0.5
step_size = learn_rate / first_fix * second_root
root_epsilon = adam_epsilon * second_root

TOKEN = (132 * 1024, 128)
PLANNED = (4, 8)
WHOLE = pl.BlockSpec(memory_space=pl.ANY)
SMALL_COST = pl.CostEstimate(flops=0, bytes_accessed=65536, transcendentals=0)


PAIR_COST = pl.CostEstimate(flops=0, bytes_accessed=16 * 1024 * 1024, transcendentals=0)


def like(array):
    return jax.ShapeDtypeStruct(array.shape, array.dtype)


def fence_kernel(*refs):
    pass


def fence(arrays):
    return pl.pallas_call(
        fence_kernel,
        in_specs=[WHOLE] * len(arrays),
        out_specs=[WHOLE] * len(arrays),
        out_shape=[like(array) for array in arrays],
        input_output_aliases={i: i for i in range(len(arrays))},
        compiler_params=pltpu.CompilerParams(vmem_limit_bytes=1024 * 1024),
        cost_estimate=SMALL_COST,
        name="arrival_order",
    )(*arrays)


def adam_kernel(groups, passed, owner, *refs):
    arrays, outs = refs[:4], refs[4 + passed : 7 + passed]
    sends = refs[7 + passed : 7 + passed + len(groups)]
    order = [number for group in groups for number in group]
    blocks = len(order)
    *buffers, semaphores = refs[-9:]
    master, gradient, first, second, new_master, new_first, new_second, sent = buffers
    experts, rows, columns = arrays[0].shape
    shard = lax.axis_index("shard")
    bands = rows // QB
    starts = range(0, columns, QB)

    def copies(chunk, inward):
        n, i = chunk // bands, chunk % bands
        number, expert = jnp.int32(order[0]), jnp.int32(0)
        for position in range(1, blocks):
            number = jnp.where(n == position, order[position], number)
        for candidate in range(experts):
            expert = jnp.where(owner[candidate] == shard ^ number, candidate, expert)
        span = pl.ds(pl.multiple_of(i * QB, QB), QB)
        for k, ref in enumerate(arrays if inward else outs):
            far, near = ref.at[expert, span], buffers[k if inward else 4 + k].at[n, span]
            pair = (far, near) if inward else (near, far)
            yield pltpu.make_async_copy(*pair, semaphores.at[chunk, k if inward else 4 + k])

    def send_copy(chunk, group, member):
        span = pl.ds(pl.multiple_of(chunk % bands * QB, QB), QB)
        n = order.index(groups[group][member])
        far = sends[group].at[member, span]
        return pltpu.make_async_copy(sent.at[n, span], far, semaphores.at[chunk, 7])

    def begin(chunk, carry):
        for copy in copies(chunk, True):
            copy.start()
        return carry

    def work(chunk, carry):
        for copy in copies(chunk, True):
            copy.wait()
        n, i = chunk // bands, chunk % bands

        def span(group):
            return pl.ds(pl.multiple_of(i * QB + group * GROUP, GROUP), GROUP)

        def update(group, peaks):
            found = []
            for start, peak in zip(starts, peaks):
                at = (n, span(group), slice(start, start + QB))
                grad = gradient[at].astype(jnp.float32)
                moment_one = beta_one * first[at].astype(jnp.float32) + (1.0 - beta_one) * grad
                moment_two = beta_two * second[at].astype(jnp.float32) + (
                    ((1.0 - beta_two) * grad) * grad
                )
                new_first[at] = moment_one.astype(jnp.bfloat16)
                new_second[at] = moment_two.astype(jnp.bfloat16)
                guess = lax.rsqrt(moment_two)
                root = moment_two * guess + root_epsilon
                inverse = guess * (2.0 - root * guess)
                updated = master[at] - (step_size * moment_one) * inverse
                new_master[at] = updated
                sizes = jnp.abs(updated).reshape(GROUP // 8, 8, QB)
                found.append(jnp.maximum(peak, jnp.max(sizes, axis=0)))
            return tuple(found)

        empty = tuple(jnp.zeros((8, QB), jnp.float32) for _ in starts)
        peaks = lax.fori_loop(0, QB // GROUP, update, empty)
        peaks = [jnp.max(peak, axis=0, keepdims=True) for peak in peaks]
        largest = jnp.max(jnp.concatenate(peaks, axis=0), axis=1, keepdims=True)
        scale = ((largest + scale_epsilon) * (1.0 / quant_limit)).astype(jnp.bfloat16)
        scale = jnp.broadcast_to(scale, (len(peaks), QB))
        inverse_scale = 1.0 / scale.astype(jnp.float32)

        def quantize(group, carry):
            for block, start in enumerate(starts):
                at = (n, span(group), slice(start, start + QB))
                one = slice(block, block + 1)
                quantized = (new_master[at] * inverse_scale[one]).astype(jnp.bfloat16)
                sent[at] = quantized * scale[one]
            return carry

        lax.fori_loop(0, QB // GROUP, quantize, 0)
        for copy in copies(chunk, False):
            copy.start()
        for group, numbers in enumerate(groups):
            for member, number in enumerate(numbers):

                @pl.when(n == order.index(number))
                def _():
                    send_copy(chunk, group, member).start()

        return carry

    def finish(chunk, carry):
        for copy in copies(chunk, False):
            copy.wait()
        send_copy(chunk, 0, 0).wait()
        return carry

    for part in (begin, work, finish):
        lax.fori_loop(0, blocks * bands, part, 0)


def adam_blocks(groups, owner, arrays, carried, token, fenced, limit):
    _, rows, columns = arrays[0].shape
    blocks, passed = sum(map(len, groups)), len(carried) + len(token)
    made = [like(arrays[0]), like(arrays[2]), like(arrays[3])]
    made += [jax.ShapeDtypeStruct((len(group), rows, columns), jnp.bfloat16) for group in groups]
    aliases = {5 + i: i for i in range(len(carried))}
    if token:
        aliases[5 + len(carried)] = len(made)
    made += [jax.ShapeDtypeStruct(TOKEN, jnp.float32)] * fenced
    kinds = [jnp.float32, jnp.bfloat16, jnp.bfloat16, jnp.bfloat16] * 2
    results = pl.pallas_call(
        functools.partial(adam_kernel, groups, passed),
        in_specs=[pl.BlockSpec(memory_space=pltpu.SMEM)] + [WHOLE] * (4 + passed),
        out_specs=[WHOLE] * len(made),
        out_shape=made,
        scratch_shapes=[pltpu.VMEM((blocks, rows, columns), kind) for kind in kinds]
        + [pltpu.SemaphoreType.DMA((blocks * (rows // QB), 8))],
        input_output_aliases=aliases,
        compiler_params=pltpu.CompilerParams(vmem_limit_bytes=limit),
        cost_estimate=SMALL_COST,
        name="adam_quantize",
    )(owner, *arrays, *carried, *token)
    return results[:3], results[3 : 3 + len(groups)], tuple(results[3 + len(groups) :])


def join_kernel(picks, *refs):
    out, semaphores = refs[-2:]
    pieces = [
        pltpu.make_async_copy(refs[1 + place].at[pick], out.at[place], semaphores.at[place])
        for place, pick in enumerate(picks)
    ]
    for piece in pieces:
        piece.start()
    for piece in pieces:
        piece.wait()


def join(token, arrays, picks):
    count = len(arrays)
    shape = jax.ShapeDtypeStruct((count, *arrays[0].shape[1:]), arrays[0].dtype)
    return pl.pallas_call(
        functools.partial(join_kernel, picks),
        in_specs=[WHOLE] * (1 + count),
        out_specs=[WHOLE] * 2,
        out_shape=[like(token), shape],
        scratch_shapes=[pltpu.SemaphoreType.DMA((count,))],
        input_output_aliases={0: 0},
        compiler_params=pltpu.CompilerParams(vmem_limit_bytes=1024 * 1024),
        cost_estimate=SMALL_COST,
        name="join_blocks",
    )(token, *arrays)


def product_kernel(slabs, sources, places, left, *refs):
    out = refs[-1]
    rows, breadth = refs[0].shape[1], out.shape[1]
    parts = [left[:, pl.ds(pl.multiple_of(places[i] * rows, QB), rows)] for i in range(slabs)]
    block = pl.program_id(0)
    span = pl.ds(pl.multiple_of(pl.program_id(1) * breadth, QB), breadth)
    total = jnp.dot(
        jnp.concatenate(parts, axis=1),
        jnp.concatenate([right[block, :, span] for right in refs[:slabs]], axis=0),
        preferred_element_type=jnp.float32,
    )
    out[...] = total.astype(out.dtype)


def product(numbers, sources, places, token_rows, weights, breadth, carried, token):
    slabs = len(weights)
    tokens, units = token_rows.shape
    blocks, rows, columns = weights[0].shape
    passed = len(token) + len(carried)
    tile = math.gcd(columns, 2 * QB)

    def place(block, i, sources, places):
        number = numbers[0] + block * (numbers[-1] - numbers[0])
        return 0, sources[number] * (columns // tile) + i

    *token, out = pl.pallas_call(
        functools.partial(product_kernel, slabs),
        grid_spec=pltpu.PrefetchScalarGridSpec(
            num_scalar_prefetch=2,
            grid=(blocks, columns // tile),
            in_specs=[pl.BlockSpec(memory_space=pltpu.VMEM)] * (1 + slabs) + [WHOLE] * passed,
            out_specs=[WHOLE] * len(token)
            + [pl.BlockSpec((tokens, tile), place)],
        ),
        out_shape=[like(array) for array in token]
            + [jax.ShapeDtypeStruct((tokens, breadth), jnp.bfloat16)],
        input_output_aliases={3 + slabs + i: i for i in range(passed)},
        compiler_params=pltpu.CompilerParams(vmem_limit_bytes=PRODUCT_LIMIT),
        cost_estimate=SMALL_COST if blocks == 1 else PAIR_COST,
        name="expert_product",
    )(sources, places, token_rows, *weights, *token, *carried)
    return (out,), tuple(token)


def swap(value, axis, size, mask):
    return lax.ppermute(value, axis, [(i, i ^ mask) for i in range(size)])


def body(shards, replicas, *arguments):
    *arrays, hidden, owner_of_expert, slab_order = arguments
    shard = lax.axis_index("shard").astype(jnp.int32)
    replica = lax.axis_index("replica").astype(jnp.int32)
    token_rows = hidden.reshape(hidden.shape[2:])
    breadth = arrays[0].shape[2] * shards
    bits = [1 << i for i in range((replicas - 1).bit_length())]
    members = jnp.arange(replicas, dtype=jnp.int32)
    sources = shard ^ jnp.arange(shards, dtype=jnp.int32)
    places = jnp.sum(
        jnp.where((replica ^ members)[:, None] == members[None, :], slab_order[None, :], 0), axis=1
    ).astype(jnp.int32)

    fenced = (replicas, shards) == PLANNED
    held, made, ready = collections.defaultdict(dict), {}, set()
    state = {"adam": (), "token": (), "out": ()}

    def adam(groups, limit=VMEM_LIMIT):
        state["adam"], sends, state["token"] = adam_blocks(
            groups, owner_of_expert, arrays, tuple(state["adam"]), state["token"], fenced, limit
        )
        made.update({group[0]: send for group, send in zip(groups, sends)})

    def deliver(block):
        held[block][0] = swap(made[block], "shard", shards, block) if block else made[block]

    def send(block, member, bit):
        held[block][member ^ bit] = swap(held[block][member], "replica", replicas, bit)

    def arrived(keys, leaving=()):
        waiting = [held[b][m] for b, m in keys] + [made[b] for b in leaving]
        token, *passed = fence([*state["token"], *waiting])
        state["token"] = (token,)
        made.update(zip(leaving, passed[len(keys) :]))
        for (block, member), array in zip(keys, passed):
            held[block][member] = array
        ready.update(keys)

    def multiply(block):
        ordered = [held[block][member] for member in range(replicas)]
        numbers = block if isinstance(block, tuple) else (block,)
        state["out"], state["token"] = product(
            numbers, sources, places, token_rows, ordered, breadth, state["out"], state["token"]
        )

    if fenced:
        one, two = (2, 4), (3, 5)
        plan = [
            ([(0, 1), (0, 2), (1, 0)], [(1, 0, 1), (1, 0, 2), (0, 1, 2)], []),
            ([(2, 0), (4, 0)], [], [3, 5]),
            ([(1, 1), (1, 2), (0, 3)], [(1, 2, 1)], []),
            (one, [(one, 0, 1), (one, 0, 2)], []),
            ([(1, 3)], [], []),
            (two, [(two, 0, 1), (two, 0, 2)], [6]),
            ([(one, 1), (one, 2)], [(one, 1, 2)], []),
            ([(6, 0)], [], [7]),
            ([(two, 1), (two, 2)], [(two, 2, 1), (6, 0, 1), (6, 0, 2)], []),
            ([(7, 0)], [(7, 0, 1), (7, 0, 2)], []),
            ([(one, 3)], [], []),
            ([(two, 3)], [], []),
            ([(6, 1), (6, 2)], [(6, 1, 2)], []),
            ([(7, 1), (7, 2)], [(7, 2, 1)], []),
            ([(6, 3)], [], []),
            ([(7, 3)], [], []),
        ]
        waiting = [0, 1, one, two, 6, 7]
        adam(((0,), (1,), (2,), (4,)))
        for block in (0, 1, 2, 4):
            deliver(block)
        ready.add((0, 0))
        send(0, 0, 1)
        send(0, 0, 2)
        adam(((3,), (5,), (6,), (7,)), LATER_LIMIT)
        for keys, sending, leaving in plan:
            if isinstance(keys, tuple):
                pieces = [held[block][0] for block in keys]
                token, held[keys][0] = join(state["token"][0], pieces, (0, 0))
                state["token"] = (token,)
                ready.add((keys, 0))
            else:
                arrived(keys, leaving)
            for block in leaving:
                deliver(block)
            for key in sending:
                send(*key)
            for block in [] if sending or leaving else list(waiting):
                if all((block, member) in ready for member in range(replicas)):
                    multiply(block)
                    waiting.remove(block)
    else:
        for pair in range(0, shards, 2):
            adam(((pair,), (pair + 1,)))
        for block in range(shards):
            deliver(block)
            for number in range(len(bits)):
                bit = bits[(number + block) % len(bits)]
                for member in list(held[block]):
                    send(block, member, bit)
            multiply(block)
    out = state["out"][0]
    return (*state["adam"], out.reshape(hidden.shape[:2] + out.shape))


def solution(mesh):
    weights = P(None, "replica", "shard")
    tokens = P("replica", "shard", None, None)
    return jax.shard_map(
        functools.partial(body, mesh.shape["shard"], mesh.shape["replica"]),
        mesh=mesh,
        in_specs=(weights, weights, weights, weights, tokens, P(), P()),
        out_specs=(weights, weights, weights, tokens),
        check_vma=False,
    )
```

```python
import collections
import functools
import math

import jax
import jax.numpy as jnp
from jax import lax
from jax.experimental import pallas as pl
from jax.experimental.pallas import tpu as pltpu
from jax.sharding import PartitionSpec as P

QB = 128
GROUP = 32
VMEM_LIMIT = 60 * 1024 * 1024
LATER_LIMIT = 56 * 1024 * 1024
PRODUCT_LIMIT = 16 * 1024 * 1024

beta_one = 0.9
beta_two = 0.95
learn_rate = 0.004
adam_epsilon = 1e-08
step_count = 10.0
quant_limit = 448.0
scale_epsilon = 1e-06
first_fix = 1.0 - beta_one**step_count
second_fix = 1.0 - beta_two**step_count
second_root = second_fix**0.5
step_size = learn_rate / first_fix * second_root
root_epsilon = adam_epsilon * second_root

TOKEN = (132 * 1024, 128)
PLANNED = (4, 8)
WHOLE = pl.BlockSpec(memory_space=pl.ANY)
SMALL_COST = pl.CostEstimate(flops=0, bytes_accessed=65536, transcendentals=0)


def like(array):
    return jax.ShapeDtypeStruct(array.shape, array.dtype)


def fence_kernel(*refs):
    pass


def fence(arrays):
    return pl.pallas_call(
        fence_kernel,
        in_specs=[WHOLE] * len(arrays),
        out_specs=[WHOLE] * len(arrays),
        out_shape=[like(array) for array in arrays],
        input_output_aliases={i: i for i in range(len(arrays))},
        compiler_params=pltpu.CompilerParams(vmem_limit_bytes=1024 * 1024),
        cost_estimate=SMALL_COST,
        name="arrival_order",
    )(*arrays)


def adam_kernel(groups, passed, owner, *refs):
    arrays, outs = refs[:4], refs[4 + passed : 7 + passed]
    sends = refs[7 + passed : 7 + passed + len(groups)]
    order = [number for group in groups for number in group]
    blocks = len(order)
    *buffers, semaphores = refs[-9:]
    master, gradient, first, second, new_master, new_first, new_second, sent = buffers
    experts, rows, columns = arrays[0].shape
    shard = lax.axis_index("shard")
    bands = rows // QB
    starts = range(0, columns, QB)

    def copies(chunk, inward):
        n, i = chunk // bands, chunk % bands
        number, expert = jnp.int32(order[0]), jnp.int32(0)
        for position in range(1, blocks):
            number = jnp.where(n == position, order[position], number)
        for candidate in range(experts):
            expert = jnp.where(owner[candidate] == shard ^ number, candidate, expert)
        span = pl.ds(pl.multiple_of(i * QB, QB), QB)
        for k, ref in enumerate(arrays if inward else outs):
            far, near = ref.at[expert, span], buffers[k if inward else 4 + k].at[n, span]
            pair = (far, near) if inward else (near, far)
            yield pltpu.make_async_copy(*pair, semaphores.at[chunk, k if inward else 4 + k])

    def send_copy(chunk, group, member):
        span = pl.ds(pl.multiple_of(chunk % bands * QB, QB), QB)
        n = order.index(groups[group][member])
        far = sends[group].at[member, span]
        return pltpu.make_async_copy(sent.at[n, span], far, semaphores.at[chunk, 7])

    def begin(chunk, carry):
        for copy in copies(chunk, True):
            copy.start()
        return carry

    def work(chunk, carry):
        for copy in copies(chunk, True):
            copy.wait()
        n, i = chunk // bands, chunk % bands

        def span(group):
            return pl.ds(pl.multiple_of(i * QB + group * GROUP, GROUP), GROUP)

        def update(group, peaks):
            found = []
            for start, peak in zip(starts, peaks):
                at = (n, span(group), slice(start, start + QB))
                grad = gradient[at].astype(jnp.float32)
                moment_one = beta_one * first[at].astype(jnp.float32) + (1.0 - beta_one) * grad
                moment_two = beta_two * second[at].astype(jnp.float32) + (
                    ((1.0 - beta_two) * grad) * grad
                )
                new_first[at] = moment_one.astype(jnp.bfloat16)
                new_second[at] = moment_two.astype(jnp.bfloat16)
                guess = lax.rsqrt(moment_two)
                root = moment_two * guess + root_epsilon
                inverse = guess * (2.0 - root * guess)
                updated = master[at] - (step_size * moment_one) * inverse
                new_master[at] = updated
                sizes = jnp.abs(updated).reshape(GROUP // 8, 8, QB)
                found.append(jnp.maximum(peak, jnp.max(sizes, axis=0)))
            return tuple(found)

        empty = tuple(jnp.zeros((8, QB), jnp.float32) for _ in starts)
        peaks = lax.fori_loop(0, QB // GROUP, update, empty)
        peaks = [jnp.max(peak, axis=0, keepdims=True) for peak in peaks]
        largest = jnp.max(jnp.concatenate(peaks, axis=0), axis=1, keepdims=True)
        scale = ((largest + scale_epsilon) * (1.0 / quant_limit)).astype(jnp.bfloat16)
        scale = jnp.broadcast_to(scale, (len(peaks), QB))
        inverse_scale = 1.0 / scale.astype(jnp.float32)

        def quantize(group, carry):
            for block, start in enumerate(starts):
                at = (n, span(group), slice(start, start + QB))
                one = slice(block, block + 1)
                quantized = (new_master[at] * inverse_scale[one]).astype(jnp.bfloat16)
                sent[at] = quantized * scale[one]
            return carry

        lax.fori_loop(0, QB // GROUP, quantize, 0)
        for copy in copies(chunk, False):
            copy.start()
        for group, numbers in enumerate(groups):
            for member, number in enumerate(numbers):

                @pl.when(n == order.index(number))
                def _():
                    send_copy(chunk, group, member).start()

        return carry

    def finish(chunk, carry):
        for copy in copies(chunk, False):
            copy.wait()
        send_copy(chunk, 0, 0).wait()
        return carry

    for part in (begin, work, finish):
        lax.fori_loop(0, blocks * bands, part, 0)


def adam_blocks(groups, owner, arrays, carried, token, fenced, limit):
    _, rows, columns = arrays[0].shape
    blocks, passed = sum(map(len, groups)), len(carried) + len(token)
    made = [like(arrays[0]), like(arrays[2]), like(arrays[3])]
    made += [jax.ShapeDtypeStruct((len(group), rows, columns), jnp.bfloat16) for group in groups]
    aliases = {5 + i: i for i in range(len(carried))}
    if token:
        aliases[5 + len(carried)] = len(made)
    made += [jax.ShapeDtypeStruct(TOKEN, jnp.float32)] * fenced
    kinds = [jnp.float32, jnp.bfloat16, jnp.bfloat16, jnp.bfloat16] * 2
    results = pl.pallas_call(
        functools.partial(adam_kernel, groups, passed),
        in_specs=[pl.BlockSpec(memory_space=pltpu.SMEM)] + [WHOLE] * (4 + passed),
        out_specs=[WHOLE] * len(made),
        out_shape=made,
        scratch_shapes=[pltpu.VMEM((blocks, rows, columns), kind) for kind in kinds]
        + [pltpu.SemaphoreType.DMA((blocks * (rows // QB), 8))],
        input_output_aliases=aliases,
        compiler_params=pltpu.CompilerParams(vmem_limit_bytes=limit),
        cost_estimate=SMALL_COST,
        name="adam_quantize",
    )(owner, *arrays, *carried, *token)
    return results[:3], results[3 : 3 + len(groups)], tuple(results[3 + len(groups) :])


def join_kernel(picks, *refs):
    out, semaphores = refs[-2:]
    pieces = [
        pltpu.make_async_copy(refs[1 + place].at[pick], out.at[place], semaphores.at[place])
        for place, pick in enumerate(picks)
    ]
    for piece in pieces:
        piece.start()
    for piece in pieces:
        piece.wait()


def join(token, arrays, picks):
    count = len(arrays)
    shape = jax.ShapeDtypeStruct((count, *arrays[0].shape[1:]), arrays[0].dtype)
    return pl.pallas_call(
        functools.partial(join_kernel, picks),
        in_specs=[WHOLE] * (1 + count),
        out_specs=[WHOLE] * 2,
        out_shape=[like(token), shape],
        scratch_shapes=[pltpu.SemaphoreType.DMA((count,))],
        input_output_aliases={0: 0},
        compiler_params=pltpu.CompilerParams(vmem_limit_bytes=1024 * 1024),
        cost_estimate=SMALL_COST,
        name="join_blocks",
    )(token, *arrays)


def product_kernel(slabs, sources, places, left, *refs):
    out = refs[-1]
    rows, breadth = refs[0].shape[1], out.shape[1]
    parts = [left[:, pl.ds(pl.multiple_of(places[i] * rows, QB), rows)] for i in range(slabs)]
    block = pl.program_id(0)
    span = pl.ds(pl.multiple_of(pl.program_id(1) * breadth, QB), breadth)
    total = jnp.dot(
        jnp.concatenate(parts, axis=1),
        jnp.concatenate([right[block, :, span] for right in refs[:slabs]], axis=0),
        preferred_element_type=jnp.float32,
    )
    out[...] = total.astype(out.dtype)


def product(numbers, sources, places, token_rows, weights, breadth, carried, token):
    slabs = len(weights)
    tokens, units = token_rows.shape
    blocks, rows, columns = weights[0].shape
    passed = len(token) + len(carried)
    tile = math.gcd(columns, 2 * QB)

    def place(block, i, sources, places):
        number = numbers[0] + block * (numbers[-1] - numbers[0])
        return 0, sources[number] * (columns // tile) + i

    *token, out = pl.pallas_call(
        functools.partial(product_kernel, slabs),
        grid_spec=pltpu.PrefetchScalarGridSpec(
            num_scalar_prefetch=2,
            grid=(blocks, columns // tile),
            in_specs=[pl.BlockSpec(memory_space=pltpu.VMEM)] * (1 + slabs) + [WHOLE] * passed,
            out_specs=[WHOLE] * len(token)
            + [pl.BlockSpec((tokens, tile), place)],
        ),
        out_shape=[like(array) for array in token]
            + [jax.ShapeDtypeStruct((tokens, breadth), jnp.bfloat16)],
        input_output_aliases={3 + slabs + i: i for i in range(passed)},
        compiler_params=pltpu.CompilerParams(vmem_limit_bytes=PRODUCT_LIMIT),
        cost_estimate=SMALL_COST,
        name="expert_product",
    )(sources, places, token_rows, *weights, *token, *carried)
    return (out,), tuple(token)


def swap(value, axis, size, mask):
    return lax.ppermute(value, axis, [(i, i ^ mask) for i in range(size)])


def body(shards, replicas, *arguments):
    *arrays, hidden, owner_of_expert, slab_order = arguments
    shard = lax.axis_index("shard").astype(jnp.int32)
    replica = lax.axis_index("replica").astype(jnp.int32)
    token_rows = hidden.reshape(hidden.shape[2:])
    breadth = arrays[0].shape[2] * shards
    bits = [1 << i for i in range((replicas - 1).bit_length())]
    members = jnp.arange(replicas, dtype=jnp.int32)
    sources = shard ^ jnp.arange(shards, dtype=jnp.int32)
    places = jnp.sum(
        jnp.where((replica ^ members)[:, None] == members[None, :], slab_order[None, :], 0), axis=1
    ).astype(jnp.int32)

    fenced = (replicas, shards) == PLANNED
    held, made, ready = collections.defaultdict(dict), {}, set()
    state = {"adam": (), "token": (), "out": ()}

    def adam(groups, limit=VMEM_LIMIT):
        state["adam"], sends, state["token"] = adam_blocks(
            groups, owner_of_expert, arrays, tuple(state["adam"]), state["token"], fenced, limit
        )
        made.update({group[0]: send for group, send in zip(groups, sends)})

    def deliver(block):
        held[block][0] = swap(made[block], "shard", shards, block) if block else made[block]

    def send(block, member, bit):
        held[block][member ^ bit] = swap(held[block][member], "replica", replicas, bit)

    def arrived(keys, leaving=()):
        waiting = [held[b][m] for b, m in keys] + [made[b] for b in leaving]
        token, *passed = fence([*state["token"], *waiting])
        state["token"] = (token,)
        made.update(zip(leaving, passed[len(keys) :]))
        for (block, member), array in zip(keys, passed):
            held[block][member] = array
        ready.update(keys)

    def multiply(block):
        ordered = [held[block][member] for member in range(replicas)]
        numbers = block if isinstance(block, tuple) else (block,)
        state["out"], state["token"] = product(
            numbers, sources, places, token_rows, ordered, breadth, state["out"], state["token"]
        )

    if fenced:
        one, two = (2, 4), (3, 5)
        plan = [
            ([(0, 1), (0, 2), (1, 0)], [(1, 0, 1), (1, 0, 2)], []),
            ([(2, 0), (4, 0)], [], [5]),
            ([(1, 1), (1, 2)], [(1, 2, 1), (0, 1, 2)], []),
            (one, [(one, 0, 1), (one, 0, 2)], []),
            ([(0, 3), (1, 3)], [], [3]),
            (two, [(two, 0, 1), (two, 0, 2)], [6]),
            ([(one, 1), (one, 2)], [(one, 1, 2)], []),
            ([(6, 0), (two, 1), (two, 2)], [(two, 2, 1), (6, 0, 1), (6, 0, 2)], [7]),
            ([(one, 3)], [], []),
            ([(7, 0)], [(7, 0, 1), (7, 0, 2)], []),
            ([(two, 3)], [], []),
            ([(6, 1), (6, 2)], [(6, 1, 2)], []),
            ([(7, 1), (7, 2)], [(7, 2, 1)], []),
            ([(6, 3)], [], []),
            ([(7, 3)], [], []),
        ]
        waiting = [0, 1, one, two, 6, 7]
        adam(((0,), (1,), (2,), (4,)))
        for block in (0, 1, 2, 4):
            deliver(block)
        ready.add((0, 0))
        send(0, 0, 1)
        send(0, 0, 2)
        adam(((3,), (5,), (6,), (7,)), LATER_LIMIT)
        for keys, sending, leaving in plan:
            if isinstance(keys, tuple):
                pieces = [held[block][0] for block in keys]
                token, held[keys][0] = join(state["token"][0], pieces, (0, 0))
                state["token"] = (token,)
                ready.add((keys, 0))
            else:
                arrived(keys, leaving)
            for block in leaving:
                deliver(block)
            for key in sending:
                send(*key)
            for block in list(waiting):
                if all((block, member) in ready for member in range(replicas)):
                    multiply(block)
                    waiting.remove(block)
    else:
        for pair in range(0, shards, 2):
            adam(((pair,), (pair + 1,)))
        for block in range(shards):
            deliver(block)
            for number in range(len(bits)):
                bit = bits[(number + block) % len(bits)]
                for member in list(held[block]):
                    send(block, member, bit)
            multiply(block)
    out = state["out"][0]
    return (*state["adam"], out.reshape(hidden.shape[:2] + out.shape))


def solution(mesh):
    weights = P(None, "replica", "shard")
    tokens = P("replica", "shard", None, None)
    return jax.shard_map(
        functools.partial(body, mesh.shape["shard"], mesh.shape["replica"]),
        mesh=mesh,
        in_specs=(weights, weights, weights, weights, tokens, P(), P()),
        out_specs=(weights, weights, weights, tokens),
        check_vma=False,
    )
```

```python
import collections
import functools
import math

import jax
import jax.numpy as jnp
from jax import lax
from jax.experimental import pallas as pl
from jax.experimental.pallas import tpu as pltpu
from jax.sharding import PartitionSpec as P

QB = 128
GROUP = 32
VMEM_LIMIT = 60 * 1024 * 1024
LATER_LIMIT = 52 * 1024 * 1024
PRODUCT_LIMIT = 16 * 1024 * 1024

beta_one = 0.9
beta_two = 0.95
learn_rate = 0.004
adam_epsilon = 1e-08
step_count = 10.0
quant_limit = 448.0
scale_epsilon = 1e-06
first_fix = 1.0 - beta_one**step_count
second_fix = 1.0 - beta_two**step_count
second_root = second_fix**0.5
step_size = learn_rate / first_fix * second_root
root_epsilon = adam_epsilon * second_root

TOKEN = (132 * 1024, 128)
PLANNED = (4, 8)
WHOLE = pl.BlockSpec(memory_space=pl.ANY)
SMALL_COST = pl.CostEstimate(flops=0, bytes_accessed=65536, transcendentals=0)


def like(array):
    return jax.ShapeDtypeStruct(array.shape, array.dtype)


def fence_kernel(*refs):
    pass


def fence(arrays):
    return pl.pallas_call(
        fence_kernel,
        in_specs=[WHOLE] * len(arrays),
        out_specs=[WHOLE] * len(arrays),
        out_shape=[like(array) for array in arrays],
        input_output_aliases={i: i for i in range(len(arrays))},
        compiler_params=pltpu.CompilerParams(vmem_limit_bytes=1024 * 1024),
        cost_estimate=SMALL_COST,
        name="arrival_order",
    )(*arrays)


def adam_kernel(groups, passed, owner, *refs):
    arrays, outs = refs[:4], refs[4 + passed : 7 + passed]
    sends = refs[7 + passed : 7 + passed + len(groups)]
    order = [number for group in groups for number in group]
    blocks = len(order)
    *buffers, semaphores = refs[-9:]
    master, gradient, first, second, new_master, new_first, new_second, sent = buffers
    experts, rows, columns = arrays[0].shape
    shard = lax.axis_index("shard")
    bands = rows // QB
    starts = range(0, columns, QB)

    def copies(chunk, inward):
        n, i = chunk // bands, chunk % bands
        number, expert = jnp.int32(order[0]), jnp.int32(0)
        for position in range(1, blocks):
            number = jnp.where(n == position, order[position], number)
        for candidate in range(experts):
            expert = jnp.where(owner[candidate] == shard ^ number, candidate, expert)
        span = pl.ds(pl.multiple_of(i * QB, QB), QB)
        for k, ref in enumerate(arrays if inward else outs):
            far, near = ref.at[expert, span], buffers[k if inward else 4 + k].at[n, span]
            pair = (far, near) if inward else (near, far)
            yield pltpu.make_async_copy(*pair, semaphores.at[chunk, k if inward else 4 + k])

    def send_copy(chunk, group, member):
        span = pl.ds(pl.multiple_of(chunk % bands * QB, QB), QB)
        n = order.index(groups[group][member])
        far = sends[group].at[member, span]
        return pltpu.make_async_copy(sent.at[n, span], far, semaphores.at[chunk, 7])

    def begin(chunk, carry):
        for copy in copies(chunk, True):
            copy.start()
        return carry

    def work(chunk, carry):
        for copy in copies(chunk, True):
            copy.wait()
        n, i = chunk // bands, chunk % bands

        def span(group):
            return pl.ds(pl.multiple_of(i * QB + group * GROUP, GROUP), GROUP)

        def update(group, peaks):
            found = []
            for start, peak in zip(starts, peaks):
                at = (n, span(group), slice(start, start + QB))
                grad = gradient[at].astype(jnp.float32)
                moment_one = beta_one * first[at].astype(jnp.float32) + (1.0 - beta_one) * grad
                moment_two = beta_two * second[at].astype(jnp.float32) + (
                    ((1.0 - beta_two) * grad) * grad
                )
                new_first[at] = moment_one.astype(jnp.bfloat16)
                new_second[at] = moment_two.astype(jnp.bfloat16)
                guess = lax.rsqrt(moment_two)
                root = moment_two * guess + root_epsilon
                inverse = guess * (2.0 - root * guess)
                updated = master[at] - (step_size * moment_one) * inverse
                new_master[at] = updated
                sizes = jnp.abs(updated).reshape(GROUP // 8, 8, QB)
                found.append(jnp.maximum(peak, jnp.max(sizes, axis=0)))
            return tuple(found)

        empty = tuple(jnp.zeros((8, QB), jnp.float32) for _ in starts)
        peaks = lax.fori_loop(0, QB // GROUP, update, empty)
        peaks = [jnp.max(peak, axis=0, keepdims=True) for peak in peaks]
        largest = jnp.max(jnp.concatenate(peaks, axis=0), axis=1, keepdims=True)
        scale = ((largest + scale_epsilon) * (1.0 / quant_limit)).astype(jnp.bfloat16)
        scale = jnp.broadcast_to(scale, (len(peaks), QB))
        inverse_scale = 1.0 / scale.astype(jnp.float32)

        def quantize(group, carry):
            for block, start in enumerate(starts):
                at = (n, span(group), slice(start, start + QB))
                one = slice(block, block + 1)
                quantized = (new_master[at] * inverse_scale[one]).astype(jnp.bfloat16)
                sent[at] = quantized * scale[one]
            return carry

        lax.fori_loop(0, QB // GROUP, quantize, 0)
        for copy in copies(chunk, False):
            copy.start()
        for group, numbers in enumerate(groups):
            for member, number in enumerate(numbers):

                @pl.when(n == order.index(number))
                def _():
                    send_copy(chunk, group, member).start()

        return carry

    def finish(chunk, carry):
        for copy in copies(chunk, False):
            copy.wait()
        send_copy(chunk, 0, 0).wait()
        return carry

    for part in (begin, work, finish):
        lax.fori_loop(0, blocks * bands, part, 0)


def adam_blocks(groups, owner, arrays, carried, token, fenced, limit):
    _, rows, columns = arrays[0].shape
    blocks, passed = sum(map(len, groups)), len(carried) + len(token)
    made = [like(arrays[0]), like(arrays[2]), like(arrays[3])]
    made += [jax.ShapeDtypeStruct((len(group), rows, columns), jnp.bfloat16) for group in groups]
    aliases = {5 + i: i for i in range(len(carried))}
    if token:
        aliases[5 + len(carried)] = len(made)
    made += [jax.ShapeDtypeStruct(TOKEN, jnp.float32)] * fenced
    kinds = [jnp.float32, jnp.bfloat16, jnp.bfloat16, jnp.bfloat16] * 2
    results = pl.pallas_call(
        functools.partial(adam_kernel, groups, passed),
        in_specs=[pl.BlockSpec(memory_space=pltpu.SMEM)] + [WHOLE] * (4 + passed),
        out_specs=[WHOLE] * len(made),
        out_shape=made,
        scratch_shapes=[pltpu.VMEM((blocks, rows, columns), kind) for kind in kinds]
        + [pltpu.SemaphoreType.DMA((blocks * (rows // QB), 8))],
        input_output_aliases=aliases,
        compiler_params=pltpu.CompilerParams(vmem_limit_bytes=limit),
        cost_estimate=SMALL_COST,
        name="adam_quantize",
    )(owner, *arrays, *carried, *token)
    return results[:3], results[3 : 3 + len(groups)], tuple(results[3 + len(groups) :])


def join_kernel(picks, *refs):
    out, semaphores = refs[-2:]
    pieces = [
        pltpu.make_async_copy(refs[1 + place].at[pick], out.at[place], semaphores.at[place])
        for place, pick in enumerate(picks)
    ]
    for piece in pieces:
        piece.start()
    for piece in pieces:
        piece.wait()


def join(token, arrays, picks):
    count = len(arrays)
    shape = jax.ShapeDtypeStruct((count, *arrays[0].shape[1:]), arrays[0].dtype)
    return pl.pallas_call(
        functools.partial(join_kernel, picks),
        in_specs=[WHOLE] * (1 + count),
        out_specs=[WHOLE] * 2,
        out_shape=[like(token), shape],
        scratch_shapes=[pltpu.SemaphoreType.DMA((count,))],
        input_output_aliases={0: 0},
        compiler_params=pltpu.CompilerParams(vmem_limit_bytes=1024 * 1024),
        cost_estimate=SMALL_COST,
        name="join_blocks",
    )(token, *arrays)


def product_kernel(slabs, sources, places, left, *refs):
    out = refs[-1]
    rows, breadth = refs[0].shape[1], out.shape[1]
    parts = [left[:, pl.ds(pl.multiple_of(places[i] * rows, QB), rows)] for i in range(slabs)]
    block = pl.program_id(0)
    span = pl.ds(pl.multiple_of(pl.program_id(1) * breadth, QB), breadth)
    total = jnp.dot(
        jnp.concatenate(parts, axis=1),
        jnp.concatenate([right[block, :, span] for right in refs[:slabs]], axis=0),
        preferred_element_type=jnp.float32,
    )
    out[...] = total.astype(out.dtype)


def product(numbers, sources, places, token_rows, weights, breadth, carried, token):
    slabs = len(weights)
    tokens, units = token_rows.shape
    blocks, rows, columns = weights[0].shape
    passed = len(token) + len(carried)
    tile = math.gcd(columns, 2 * QB)

    def place(block, i, sources, places):
        number = numbers[0] + block * (numbers[-1] - numbers[0])
        return 0, sources[number] * (columns // tile) + i

    *token, out = pl.pallas_call(
        functools.partial(product_kernel, slabs),
        grid_spec=pltpu.PrefetchScalarGridSpec(
            num_scalar_prefetch=2,
            grid=(blocks, columns // tile),
            in_specs=[pl.BlockSpec(memory_space=pltpu.VMEM)] * (1 + slabs) + [WHOLE] * passed,
            out_specs=[WHOLE] * len(token)
            + [pl.BlockSpec((tokens, tile), place)],
        ),
        out_shape=[like(array) for array in token]
            + [jax.ShapeDtypeStruct((tokens, breadth), jnp.bfloat16)],
        input_output_aliases={3 + slabs + i: i for i in range(passed)},
        compiler_params=pltpu.CompilerParams(vmem_limit_bytes=PRODUCT_LIMIT),
        cost_estimate=SMALL_COST,
        name="expert_product",
    )(sources, places, token_rows, *weights, *token, *carried)
    return (out,), tuple(token)


def swap(value, axis, size, mask):
    return lax.ppermute(value, axis, [(i, i ^ mask) for i in range(size)])


def body(shards, replicas, *arguments):
    *arrays, hidden, owner_of_expert, slab_order = arguments
    shard = lax.axis_index("shard").astype(jnp.int32)
    replica = lax.axis_index("replica").astype(jnp.int32)
    token_rows = hidden.reshape(hidden.shape[2:])
    breadth = arrays[0].shape[2] * shards
    bits = [1 << i for i in range((replicas - 1).bit_length())]
    members = jnp.arange(replicas, dtype=jnp.int32)
    sources = shard ^ jnp.arange(shards, dtype=jnp.int32)
    places = jnp.sum(
        jnp.where((replica ^ members)[:, None] == members[None, :], slab_order[None, :], 0), axis=1
    ).astype(jnp.int32)

    fenced = (replicas, shards) == PLANNED
    held, made, ready = collections.defaultdict(dict), {}, set()
    state = {"adam": (), "token": (), "out": ()}

    def adam(groups, limit=VMEM_LIMIT):
        state["adam"], sends, state["token"] = adam_blocks(
            groups, owner_of_expert, arrays, tuple(state["adam"]), state["token"], fenced, limit
        )
        made.update({group[0]: send for group, send in zip(groups, sends)})

    def deliver(block):
        held[block][0] = swap(made[block], "shard", shards, block) if block else made[block]

    def send(block, member, bit):
        held[block][member ^ bit] = swap(held[block][member], "replica", replicas, bit)

    def arrived(keys, leaving=()):
        waiting = [held[b][m] for b, m in keys] + [made[b] for b in leaving]
        token, *passed = fence([*state["token"], *waiting])
        state["token"] = (token,)
        made.update(zip(leaving, passed[len(keys) :]))
        for (block, member), array in zip(keys, passed):
            held[block][member] = array
        ready.update(keys)

    def multiply(block):
        ordered = [held[block][member] for member in range(replicas)]
        numbers = block if isinstance(block, tuple) else (block,)
        state["out"], state["token"] = product(
            numbers, sources, places, token_rows, ordered, breadth, state["out"], state["token"]
        )

    if fenced:
        one, two = (2, 4), (3, 5)
        plan = [
            ([(0, 1), (0, 2), (1, 0)], [(1, 0, 1), (1, 0, 2), (0, 1, 2)], []),
            ([(2, 0), (4, 0)], [], []),
            ([(1, 1), (1, 2)], [(1, 2, 1)], []),
            ([(1, 3)], [], []),
            (one, [(one, 0, 1), (one, 0, 2)], []),
            ([(0, 3)], [], [6]),
            (two, [(two, 0, 1), (two, 0, 2)], []),
            ([(6, 0), (one, 1), (one, 2)], [(one, 1, 2)], [7]),
            ([(two, 1), (two, 2)], [(two, 2, 1), (6, 0, 1), (6, 0, 2)], []),
            ([(one, 3), (7, 0)], [(7, 0, 1), (7, 0, 2)], []),
            ([(two, 3)], [], []),
            ([(6, 1), (6, 2)], [(6, 1, 2)], []),
            ([(7, 1), (7, 2)], [(7, 2, 1)], []),
            ([(6, 3)], [], []),
            ([(7, 3)], [], []),
        ]
        waiting = [0, 1, one, two, 6, 7]
        adam(((0,), (1,), (2,), (4,)))
        for block in (0, 1, 2, 4):
            deliver(block)
        ready.add((0, 0))
        send(0, 0, 1)
        send(0, 0, 2)
        for step, (keys, sending, leaving) in enumerate(plan):
            if isinstance(keys, tuple):
                pieces = [held[block][0] for block in keys]
                token, held[keys][0] = join(state["token"][0], pieces, (0, 0))
                state["token"] = (token,)
                ready.add((keys, 0))
            else:
                arrived(keys, leaving)
            for block in leaving:
                deliver(block)
            for key in sending:
                send(*key)
            if not step:
                adam(((3,), (5,), (6,), (7,)), LATER_LIMIT)
                deliver(5)
                deliver(3)
            for block in list(waiting) if step > 3 else []:
                if all((block, member) in ready for member in range(replicas)):
                    multiply(block)
                    waiting.remove(block)
    else:
        for pair in range(0, shards, 2):
            adam(((pair,), (pair + 1,)))
        for block in range(shards):
            deliver(block)
            for number in range(len(bits)):
                bit = bits[(number + block) % len(bits)]
                for member in list(held[block]):
                    send(block, member, bit)
            multiply(block)
    out = state["out"][0]
    return (*state["adam"], out.reshape(hidden.shape[:2] + out.shape))


def solution(mesh):
    weights = P(None, "replica", "shard")
    tokens = P("replica", "shard", None, None)
    return jax.shard_map(
        functools.partial(body, mesh.shape["shard"], mesh.shape["replica"]),
        mesh=mesh,
        in_specs=(weights, weights, weights, weights, tokens, P(), P()),
        out_specs=(weights, weights, weights, tokens),
        check_vma=False,
    )
```

```python
import collections
import functools
import math

import jax
import jax.numpy as jnp
from jax import lax
from jax.experimental import pallas as pl
from jax.experimental.pallas import tpu as pltpu
from jax.sharding import PartitionSpec as P

QB = 128
GROUP = 32
VMEM_LIMIT = 60 * 1024 * 1024
LATER_LIMIT = 52 * 1024 * 1024
PRODUCT_LIMIT = 16 * 1024 * 1024

beta_one = 0.9
beta_two = 0.95
learn_rate = 0.004
adam_epsilon = 1e-08
step_count = 10.0
quant_limit = 448.0
scale_epsilon = 1e-06
first_fix = 1.0 - beta_one**step_count
second_fix = 1.0 - beta_two**step_count
second_root = second_fix**0.5
step_size = learn_rate / first_fix * second_root
root_epsilon = adam_epsilon * second_root

TOKEN = (132 * 1024, 128)
PLANNED = (4, 8)
WHOLE = pl.BlockSpec(memory_space=pl.ANY)
SMALL_COST = pl.CostEstimate(flops=0, bytes_accessed=65536, transcendentals=0)


def like(array):
    return jax.ShapeDtypeStruct(array.shape, array.dtype)


def fence_kernel(*refs):
    pass


def fence(arrays):
    return pl.pallas_call(
        fence_kernel,
        in_specs=[WHOLE] * len(arrays),
        out_specs=[WHOLE] * len(arrays),
        out_shape=[like(array) for array in arrays],
        input_output_aliases={i: i for i in range(len(arrays))},
        compiler_params=pltpu.CompilerParams(vmem_limit_bytes=1024 * 1024),
        cost_estimate=SMALL_COST,
        name="arrival_order",
    )(*arrays)


def adam_kernel(groups, passed, owner, *refs):
    arrays, outs = refs[:4], refs[4 + passed : 7 + passed]
    sends = refs[7 + passed : 7 + passed + len(groups)]
    order = [number for group in groups for number in group]
    blocks = len(order)
    *buffers, semaphores = refs[-9:]
    master, gradient, first, second, new_master, new_first, new_second, sent = buffers
    experts, rows, columns = arrays[0].shape
    shard = lax.axis_index("shard")
    bands = rows // QB
    starts = range(0, columns, QB)

    def copies(chunk, inward):
        n, i = chunk // bands, chunk % bands
        number, expert = jnp.int32(order[0]), jnp.int32(0)
        for position in range(1, blocks):
            number = jnp.where(n == position, order[position], number)
        for candidate in range(experts):
            expert = jnp.where(owner[candidate] == shard ^ number, candidate, expert)
        span = pl.ds(pl.multiple_of(i * QB, QB), QB)
        for k, ref in enumerate(arrays if inward else outs):
            far, near = ref.at[expert, span], buffers[k if inward else 4 + k].at[n, span]
            pair = (far, near) if inward else (near, far)
            yield pltpu.make_async_copy(*pair, semaphores.at[chunk, k if inward else 4 + k])

    def send_copy(chunk, group, member):
        span = pl.ds(pl.multiple_of(chunk % bands * QB, QB), QB)
        n = order.index(groups[group][member])
        far = sends[group].at[member, span]
        return pltpu.make_async_copy(sent.at[n, span], far, semaphores.at[chunk, 7])

    def begin(chunk, carry):
        for copy in copies(chunk, True):
            copy.start()
        return carry

    def work(chunk, carry):
        for copy in copies(chunk, True):
            copy.wait()
        n, i = chunk // bands, chunk % bands

        def span(group):
            return pl.ds(pl.multiple_of(i * QB + group * GROUP, GROUP), GROUP)

        def update(group, peaks):
            found = []
            for start, peak in zip(starts, peaks):
                at = (n, span(group), slice(start, start + QB))
                grad = gradient[at].astype(jnp.float32)
                moment_one = beta_one * first[at].astype(jnp.float32) + (1.0 - beta_one) * grad
                moment_two = beta_two * second[at].astype(jnp.float32) + (
                    ((1.0 - beta_two) * grad) * grad
                )
                new_first[at] = moment_one.astype(jnp.bfloat16)
                new_second[at] = moment_two.astype(jnp.bfloat16)
                guess = lax.rsqrt(moment_two)
                root = moment_two * guess + root_epsilon
                inverse = guess * (2.0 - root * guess)
                updated = master[at] - (step_size * moment_one) * inverse
                new_master[at] = updated
                sizes = jnp.abs(updated).reshape(GROUP // 8, 8, QB)
                found.append(jnp.maximum(peak, jnp.max(sizes, axis=0)))
            return tuple(found)

        empty = tuple(jnp.zeros((8, QB), jnp.float32) for _ in starts)
        peaks = lax.fori_loop(0, QB // GROUP, update, empty)
        peaks = [jnp.max(peak, axis=0, keepdims=True) for peak in peaks]
        largest = jnp.max(jnp.concatenate(peaks, axis=0), axis=1, keepdims=True)
        scale = ((largest + scale_epsilon) * (1.0 / quant_limit)).astype(jnp.bfloat16)
        scale = jnp.broadcast_to(scale, (len(peaks), QB))
        inverse_scale = 1.0 / scale.astype(jnp.float32)

        def quantize(group, carry):
            for block, start in enumerate(starts):
                at = (n, span(group), slice(start, start + QB))
                one = slice(block, block + 1)
                quantized = (new_master[at] * inverse_scale[one]).astype(jnp.bfloat16)
                sent[at] = quantized * scale[one]
            return carry

        lax.fori_loop(0, QB // GROUP, quantize, 0)
        for copy in copies(chunk, False):
            copy.start()
        for group, numbers in enumerate(groups):
            for member, number in enumerate(numbers):

                @pl.when(n == order.index(number))
                def _():
                    send_copy(chunk, group, member).start()

        return carry

    def finish(chunk, carry):
        for copy in copies(chunk, False):
            copy.wait()
        send_copy(chunk, 0, 0).wait()
        return carry

    for part in (begin, work, finish):
        lax.fori_loop(0, blocks * bands, part, 0)


def adam_blocks(groups, owner, arrays, carried, token, fenced, limit):
    _, rows, columns = arrays[0].shape
    blocks, passed = sum(map(len, groups)), len(carried) + len(token)
    made = [like(arrays[0]), like(arrays[2]), like(arrays[3])]
    made += [jax.ShapeDtypeStruct((len(group), rows, columns), jnp.bfloat16) for group in groups]
    aliases = {5 + i: i for i in range(len(carried))}
    if token:
        aliases[5 + len(carried)] = len(made)
    made += [jax.ShapeDtypeStruct(TOKEN, jnp.float32)] * fenced
    kinds = [jnp.float32, jnp.bfloat16, jnp.bfloat16, jnp.bfloat16] * 2
    results = pl.pallas_call(
        functools.partial(adam_kernel, groups, passed),
        in_specs=[pl.BlockSpec(memory_space=pltpu.SMEM)] + [WHOLE] * (4 + passed),
        out_specs=[WHOLE] * len(made),
        out_shape=made,
        scratch_shapes=[pltpu.VMEM((blocks, rows, columns), kind) for kind in kinds]
        + [pltpu.SemaphoreType.DMA((blocks * (rows // QB), 8))],
        input_output_aliases=aliases,
        compiler_params=pltpu.CompilerParams(vmem_limit_bytes=limit),
        cost_estimate=SMALL_COST,
        name="adam_quantize",
    )(owner, *arrays, *carried, *token)
    return results[:3], results[3 : 3 + len(groups)], tuple(results[3 + len(groups) :])


def join_kernel(picks, *refs):
    out, semaphores = refs[-2:]
    pieces = [
        pltpu.make_async_copy(refs[1 + place].at[pick], out.at[place], semaphores.at[place])
        for place, pick in enumerate(picks)
    ]
    for piece in pieces:
        piece.start()
    for piece in pieces:
        piece.wait()


def join(token, arrays, picks):
    count = len(arrays)
    shape = jax.ShapeDtypeStruct((count, *arrays[0].shape[1:]), arrays[0].dtype)
    return pl.pallas_call(
        functools.partial(join_kernel, picks),
        in_specs=[WHOLE] * (1 + count),
        out_specs=[WHOLE] * 2,
        out_shape=[like(token), shape],
        scratch_shapes=[pltpu.SemaphoreType.DMA((count,))],
        input_output_aliases={0: 0},
        compiler_params=pltpu.CompilerParams(vmem_limit_bytes=1024 * 1024),
        cost_estimate=SMALL_COST,
        name="join_blocks",
    )(token, *arrays)


def product_kernel(slabs, sources, places, left, *refs):
    out = refs[-1]
    rows, breadth = refs[0].shape[1], out.shape[1]
    parts = [left[:, pl.ds(pl.multiple_of(places[i] * rows, QB), rows)] for i in range(slabs)]
    block = pl.program_id(0)
    span = pl.ds(pl.multiple_of(pl.program_id(1) * breadth, QB), breadth)
    total = jnp.dot(
        jnp.concatenate(parts, axis=1),
        jnp.concatenate([right[block, :, span] for right in refs[:slabs]], axis=0),
        preferred_element_type=jnp.float32,
    )
    out[...] = total.astype(out.dtype)


def product(numbers, sources, places, token_rows, weights, breadth, carried, token):
    slabs = len(weights)
    tokens, units = token_rows.shape
    blocks, rows, columns = weights[0].shape
    passed = len(token) + len(carried)
    tile = math.gcd(columns, 2 * QB)

    def place(block, i, sources, places):
        number = numbers[0] + block * (numbers[-1] - numbers[0])
        return 0, sources[number] * (columns // tile) + i

    *token, out = pl.pallas_call(
        functools.partial(product_kernel, slabs),
        grid_spec=pltpu.PrefetchScalarGridSpec(
            num_scalar_prefetch=2,
            grid=(blocks, columns // tile),
            in_specs=[pl.BlockSpec(memory_space=pltpu.VMEM)] * (1 + slabs) + [WHOLE] * passed,
            out_specs=[WHOLE] * len(token)
            + [pl.BlockSpec((tokens, tile), place)],
        ),
        out_shape=[like(array) for array in token]
            + [jax.ShapeDtypeStruct((tokens, breadth), jnp.bfloat16)],
        input_output_aliases={3 + slabs + i: i for i in range(passed)},
        compiler_params=pltpu.CompilerParams(vmem_limit_bytes=PRODUCT_LIMIT),
        cost_estimate=SMALL_COST,
        name="expert_product",
    )(sources, places, token_rows, *weights, *token, *carried)
    return (out,), tuple(token)


def swap(value, axis, size, mask):
    return lax.ppermute(value, axis, [(i, i ^ mask) for i in range(size)])


def body(shards, replicas, *arguments):
    *arrays, hidden, owner_of_expert, slab_order = arguments
    shard = lax.axis_index("shard").astype(jnp.int32)
    replica = lax.axis_index("replica").astype(jnp.int32)
    token_rows = hidden.reshape(hidden.shape[2:])
    breadth = arrays[0].shape[2] * shards
    bits = [1 << i for i in range((replicas - 1).bit_length())]
    members = jnp.arange(replicas, dtype=jnp.int32)
    sources = shard ^ jnp.arange(shards, dtype=jnp.int32)
    places = jnp.sum(
        jnp.where((replica ^ members)[:, None] == members[None, :], slab_order[None, :], 0), axis=1
    ).astype(jnp.int32)

    fenced = (replicas, shards) == PLANNED
    held, made = collections.defaultdict(dict), {}
    state = {"adam": (), "token": (), "out": ()}

    def adam(groups, limit=VMEM_LIMIT):
        state["adam"], sends, state["token"] = adam_blocks(
            groups, owner_of_expert, arrays, tuple(state["adam"]), state["token"], fenced, limit
        )
        made.update({group[0]: send for group, send in zip(groups, sends)})

    def deliver(block):
        held[block][0] = swap(made[block], "shard", shards, block) if block else made[block]

    def send(block, member, bit):
        held[block][member ^ bit] = swap(held[block][member], "replica", replicas, bit)

    def arrived(keys, leaving=()):
        waiting = [held[b][m] for b, m in keys] + [made[b] for b in leaving]
        token, *passed = fence([*state["token"], *waiting])
        state["token"] = (token,)
        made.update(zip(leaving, passed[len(keys) :]))
        for (block, member), array in zip(keys, passed):
            held[block][member] = array

    def multiply(block):
        ordered = [held[block][member] for member in range(replicas)]
        numbers = block if isinstance(block, tuple) else (block,)
        state["out"], state["token"] = product(
            numbers, sources, places, token_rows, ordered, breadth, state["out"], state["token"]
        )

    if fenced:
        one, two = (2, 4), (3, 5)
        plan = [
            ([(0, 1), (0, 2), (1, 0)], [(1, 0, 1), (1, 0, 2), (0, 1, 2)], [], []),
            ([(2, 0), (4, 0)], [], [], []),
            ([(1, 1), (1, 2)], [(1, 2, 1)], [], []),
            ([(1, 3)], [], [], []),
            (one, [(one, 0, 1), (one, 0, 2)], [], [1]),
            ([(0, 3)], [], [6], [0]),
            (two, [(two, 0, 1), (two, 0, 2)], [], []),
            ([(6, 0), (one, 1), (one, 2)], [(one, 1, 2)], [7], []),
            ([(two, 1), (two, 2)], [(two, 2, 1), (6, 0, 1), (6, 0, 2)], [], []),
            ([(one, 3), (7, 0)], [(7, 0, 1), (7, 0, 2)], [], []),
            ([(two, 3)], [], [], []),
            ([(6, 1), (6, 2)], [(6, 1, 2)], [], [one]),
            ([(7, 1), (7, 2)], [(7, 2, 1)], [], [two]),
            ([(6, 3)], [], [], [6]),
            ([(7, 3)], [], [], [7]),
        ]
        adam(((0,), (1,), (2,), (4,)))
        for block in (0, 1, 2, 4):
            deliver(block)
        send(0, 0, 1)
        send(0, 0, 2)
        for step, (keys, sending, leaving, finished) in enumerate(plan):
            if isinstance(keys, tuple):
                pieces = [held[block][0] for block in keys]
                token, held[keys][0] = join(state["token"][0], pieces, (0, 0))
                state["token"] = (token,)
            else:
                arrived(keys, leaving)
            for block in leaving:
                deliver(block)
            for key in sending:
                send(*key)
            if not step:
                adam(((3,), (5,), (6,), (7,)), LATER_LIMIT)
                deliver(5)
                deliver(3)
            for block in finished:
                multiply(block)
    else:
        for pair in range(0, shards, 2):
            adam(((pair,), (pair + 1,)))
        for block in range(shards):
            deliver(block)
            for number in range(len(bits)):
                bit = bits[(number + block) % len(bits)]
                for member in list(held[block]):
                    send(block, member, bit)
            multiply(block)
    out = state["out"][0]
    return (*state["adam"], out.reshape(hidden.shape[:2] + out.shape))


def solution(mesh):
    weights = P(None, "replica", "shard")
    tokens = P("replica", "shard", None, None)
    return jax.shard_map(
        functools.partial(body, mesh.shape["shard"], mesh.shape["replica"]),
        mesh=mesh,
        in_specs=(weights, weights, weights, weights, tokens, P(), P()),
        out_specs=(weights, weights, weights, tokens),
        check_vma=False,
    )
```

```python
import collections
import functools
import math

import jax
import jax.numpy as jnp
from jax import lax
from jax.experimental import pallas as pl
from jax.experimental.pallas import tpu as pltpu
from jax.sharding import PartitionSpec as P

QB = 128
GROUP = 32
VMEM_LIMIT = 60 * 1024 * 1024
LATER_LIMIT = 52 * 1024 * 1024
PRODUCT_LIMIT = 16 * 1024 * 1024

beta_one = 0.9
beta_two = 0.95
learn_rate = 0.004
adam_epsilon = 1e-08
step_count = 10.0
quant_limit = 448.0
scale_epsilon = 1e-06
first_fix = 1.0 - beta_one**step_count
second_fix = 1.0 - beta_two**step_count
second_root = second_fix**0.5
step_size = learn_rate / first_fix * second_root
root_epsilon = adam_epsilon * second_root

TOKEN = (132 * 1024, 128)
PLANNED = (4, 8)
WHOLE = pl.BlockSpec(memory_space=pl.ANY)
SMALL_COST = pl.CostEstimate(flops=0, bytes_accessed=65536, transcendentals=0)


def like(array):
    return jax.ShapeDtypeStruct(array.shape, array.dtype)


def fence_kernel(*refs):
    pass


def fence(arrays):
    return pl.pallas_call(
        fence_kernel,
        in_specs=[WHOLE] * len(arrays),
        out_specs=[WHOLE] * len(arrays),
        out_shape=[like(array) for array in arrays],
        input_output_aliases={i: i for i in range(len(arrays))},
        compiler_params=pltpu.CompilerParams(vmem_limit_bytes=1024 * 1024),
        cost_estimate=SMALL_COST,
        name="arrival_order",
    )(*arrays)


def adam_kernel(groups, passed, owner, *refs):
    arrays, outs = refs[:4], refs[4 + passed : 7 + passed]
    sends = refs[7 + passed : 7 + passed + len(groups)]
    order = [number for group in groups for number in group]
    blocks = len(order)
    *buffers, semaphores = refs[-9:]
    master, gradient, first, second, new_master, new_first, new_second, sent = buffers
    experts, rows, columns = arrays[0].shape
    shard = lax.axis_index("shard")
    bands = rows // QB
    starts = range(0, columns, QB)

    def copies(chunk, inward):
        n, i = chunk // bands, chunk % bands
        number, expert = jnp.int32(order[0]), jnp.int32(0)
        for position in range(1, blocks):
            number = jnp.where(n == position, order[position], number)
        for candidate in range(experts):
            expert = jnp.where(owner[candidate] == shard ^ number, candidate, expert)
        span = pl.ds(pl.multiple_of(i * QB, QB), QB)
        for k, ref in enumerate(arrays if inward else outs):
            far, near = ref.at[expert, span], buffers[k if inward else 4 + k].at[n, span]
            pair = (far, near) if inward else (near, far)
            yield pltpu.make_async_copy(*pair, semaphores.at[chunk, k if inward else 4 + k])

    def send_copy(chunk, group, member):
        span = pl.ds(pl.multiple_of(chunk % bands * QB, QB), QB)
        n = order.index(groups[group][member])
        far = sends[group].at[member, span]
        return pltpu.make_async_copy(sent.at[n, span], far, semaphores.at[chunk, 7])

    def begin(chunk, carry):
        for copy in copies(chunk, True):
            copy.start()
        return carry

    def work(chunk, carry):
        for copy in copies(chunk, True):
            copy.wait()
        n, i = chunk // bands, chunk % bands

        def span(group):
            return pl.ds(pl.multiple_of(i * QB + group * GROUP, GROUP), GROUP)

        def update(group, peaks):
            found = []
            for start, peak in zip(starts, peaks):
                at = (n, span(group), slice(start, start + QB))
                grad = gradient[at].astype(jnp.float32)
                moment_one = beta_one * first[at].astype(jnp.float32) + (1.0 - beta_one) * grad
                moment_two = beta_two * second[at].astype(jnp.float32) + (
                    ((1.0 - beta_two) * grad) * grad
                )
                new_first[at] = moment_one.astype(jnp.bfloat16)
                new_second[at] = moment_two.astype(jnp.bfloat16)
                guess = lax.rsqrt(moment_two)
                root = moment_two * guess + root_epsilon
                inverse = guess * (2.0 - root * guess)
                updated = master[at] - (step_size * moment_one) * inverse
                new_master[at] = updated
                sizes = jnp.abs(updated).reshape(GROUP // 8, 8, QB)
                found.append(jnp.maximum(peak, jnp.max(sizes, axis=0)))
            return tuple(found)

        empty = tuple(jnp.zeros((8, QB), jnp.float32) for _ in starts)
        peaks = lax.fori_loop(0, QB // GROUP, update, empty)
        peaks = [jnp.max(peak, axis=0, keepdims=True) for peak in peaks]
        largest = jnp.max(jnp.concatenate(peaks, axis=0), axis=1, keepdims=True)
        scale = ((largest + scale_epsilon) * (1.0 / quant_limit)).astype(jnp.bfloat16)
        scale = jnp.broadcast_to(scale, (len(peaks), QB))
        inverse_scale = 1.0 / scale.astype(jnp.float32)

        def quantize(group, carry):
            for block, start in enumerate(starts):
                at = (n, span(group), slice(start, start + QB))
                one = slice(block, block + 1)
                quantized = (new_master[at] * inverse_scale[one]).astype(jnp.bfloat16)
                sent[at] = quantized * scale[one]
            return carry

        lax.fori_loop(0, QB // GROUP, quantize, 0)
        for copy in copies(chunk, False):
            copy.start()
        for group, numbers in enumerate(groups):
            for member, number in enumerate(numbers):

                @pl.when(n == order.index(number))
                def _():
                    send_copy(chunk, group, member).start()

        return carry

    def finish(chunk, carry):
        for copy in copies(chunk, False):
            copy.wait()
        send_copy(chunk, 0, 0).wait()
        return carry

    for part in (begin, work, finish):
        lax.fori_loop(0, blocks * bands, part, 0)


def adam_blocks(groups, owner, arrays, carried, token, fenced, limit):
    _, rows, columns = arrays[0].shape
    blocks, passed = sum(map(len, groups)), len(carried) + len(token)
    made = [like(arrays[0]), like(arrays[2]), like(arrays[3])]
    made += [jax.ShapeDtypeStruct((len(group), rows, columns), jnp.bfloat16) for group in groups]
    aliases = {5 + i: i for i in range(len(carried))}
    if token:
        aliases[5 + len(carried)] = len(made)
    made += [jax.ShapeDtypeStruct(TOKEN, jnp.float32)] * fenced
    kinds = [jnp.float32, jnp.bfloat16, jnp.bfloat16, jnp.bfloat16] * 2
    results = pl.pallas_call(
        functools.partial(adam_kernel, groups, passed),
        in_specs=[pl.BlockSpec(memory_space=pltpu.SMEM)] + [WHOLE] * (4 + passed),
        out_specs=[WHOLE] * len(made),
        out_shape=made,
        scratch_shapes=[pltpu.VMEM((blocks, rows, columns), kind) for kind in kinds]
        + [pltpu.SemaphoreType.DMA((blocks * (rows // QB), 8))],
        input_output_aliases=aliases,
        compiler_params=pltpu.CompilerParams(vmem_limit_bytes=limit),
        cost_estimate=SMALL_COST,
        name="adam_quantize",
    )(owner, *arrays, *carried, *token)
    return results[:3], results[3 : 3 + len(groups)], tuple(results[3 + len(groups) :])


def join_kernel(picks, *refs):
    out, semaphores = refs[-2:]
    pieces = [
        pltpu.make_async_copy(refs[1 + place].at[pick], out.at[place], semaphores.at[place])
        for place, pick in enumerate(picks)
    ]
    for piece in pieces:
        piece.start()
    for piece in pieces:
        piece.wait()


def join(token, arrays, picks):
    count = len(arrays)
    shape = jax.ShapeDtypeStruct((count, *arrays[0].shape[1:]), arrays[0].dtype)
    return pl.pallas_call(
        functools.partial(join_kernel, picks),
        in_specs=[WHOLE] * (1 + count),
        out_specs=[WHOLE] * 2,
        out_shape=[like(token), shape],
        scratch_shapes=[pltpu.SemaphoreType.DMA((count,))],
        input_output_aliases={0: 0},
        compiler_params=pltpu.CompilerParams(vmem_limit_bytes=1024 * 1024),
        cost_estimate=SMALL_COST,
        name="join_blocks",
    )(token, *arrays)


def product_kernel(slabs, sources, places, left, *refs):
    out = refs[-1]
    rows, breadth = refs[0].shape[1], out.shape[1]
    parts = [left[:, pl.ds(pl.multiple_of(places[i] * rows, QB), rows)] for i in range(slabs)]
    block = pl.program_id(0)
    span = pl.ds(pl.multiple_of(pl.program_id(1) * breadth, QB), breadth)
    total = jnp.dot(
        jnp.concatenate(parts, axis=1),
        jnp.concatenate([right[block, :, span] for right in refs[:slabs]], axis=0),
        preferred_element_type=jnp.float32,
    )
    out[...] = total.astype(out.dtype)


def product(numbers, sources, places, token_rows, weights, breadth, carried, token):
    slabs = len(weights)
    tokens, units = token_rows.shape
    blocks, rows, columns = weights[0].shape
    passed = len(token) + len(carried)
    tile = math.gcd(columns, 2 * QB)

    def place(block, i, sources, places):
        number = numbers[0] + block * (numbers[-1] - numbers[0])
        return 0, sources[number] * (columns // tile) + i

    *token, out = pl.pallas_call(
        functools.partial(product_kernel, slabs),
        grid_spec=pltpu.PrefetchScalarGridSpec(
            num_scalar_prefetch=2,
            grid=(blocks, columns // tile),
            in_specs=[pl.BlockSpec(memory_space=pltpu.VMEM)] * (1 + slabs) + [WHOLE] * passed,
            out_specs=[WHOLE] * len(token)
            + [pl.BlockSpec((tokens, tile), place)],
        ),
        out_shape=[like(array) for array in token]
            + [jax.ShapeDtypeStruct((tokens, breadth), jnp.bfloat16)],
        input_output_aliases={3 + slabs + i: i for i in range(passed)},
        compiler_params=pltpu.CompilerParams(vmem_limit_bytes=PRODUCT_LIMIT),
        cost_estimate=SMALL_COST,
        name="expert_product",
    )(sources, places, token_rows, *weights, *token, *carried)
    return (out,), tuple(token)


def swap(value, axis, size, mask):
    return lax.ppermute(value, axis, [(i, i ^ mask) for i in range(size)])


def body(shards, replicas, *arguments):
    *arrays, hidden, owner_of_expert, slab_order = arguments
    shard = lax.axis_index("shard").astype(jnp.int32)
    replica = lax.axis_index("replica").astype(jnp.int32)
    token_rows = hidden.reshape(hidden.shape[2:])
    breadth = arrays[0].shape[2] * shards
    bits = [1 << i for i in range((replicas - 1).bit_length())]
    members = jnp.arange(replicas, dtype=jnp.int32)
    sources = shard ^ jnp.arange(shards, dtype=jnp.int32)
    places = jnp.sum(
        jnp.where((replica ^ members)[:, None] == members[None, :], slab_order[None, :], 0), axis=1
    ).astype(jnp.int32)

    fenced = (replicas, shards) == PLANNED
    held, made = collections.defaultdict(dict), {}
    state = {"adam": (), "token": (), "out": ()}

    def adam(groups, limit=VMEM_LIMIT):
        state["adam"], sends, state["token"] = adam_blocks(
            groups, owner_of_expert, arrays, tuple(state["adam"]), state["token"], fenced, limit
        )
        made.update({group[0]: send for group, send in zip(groups, sends)})

    def deliver(block):
        held[block][0] = swap(made[block], "shard", shards, block) if block else made[block]

    def send(block, member, bit):
        held[block][member ^ bit] = swap(held[block][member], "replica", replicas, bit)

    def arrived(keys, leaving=()):
        waiting = [held[b][m] for b, m in keys] + [made[b] for b in leaving]
        token, *passed = fence([*state["token"], *waiting])
        state["token"] = (token,)
        made.update(zip(leaving, passed[len(keys) :]))
        for (block, member), array in zip(keys, passed):
            held[block][member] = array

    def multiply(block):
        ordered = [held[block][member] for member in range(replicas)]
        numbers = block if isinstance(block, tuple) else (block,)
        state["out"], state["token"] = product(
            numbers, sources, places, token_rows, ordered, breadth, state["out"], state["token"]
        )

    if fenced:
        one, two = (2, 4), (3, 5)
        plan = [
            ([(0, 1), (0, 2), (1, 0)], [(1, 0, 1), (1, 0, 2), (0, 1, 2)], [], []),
            ([(2, 0), (4, 0)], [], [], []),
            ([(1, 1), (1, 2)], [(1, 2, 1)], [], []),
            ([(1, 3)], [], [], []),
            (one, [(one, 0, 1), (one, 0, 2)], [], [1]),
            ([(0, 3)], [], [6], [0]),
            (two, [(two, 0, 1), (two, 0, 2)], [], []),
            ([(6, 0), (one, 1), (one, 2)], [(one, 1, 2)], [7], []),
            ([(two, 1), (two, 2)], [(two, 2, 1), (6, 0, 1), (6, 0, 2)], [], []),
            ([(7, 0)], [(7, 0, 1), (7, 0, 2)], [], []),
            ([(one, 3), (6, 1), (6, 2)], [(6, 1, 2)], [], [one]),
            ([(7, 1), (7, 2)], [(7, 2, 1)], [], []),
            ([(two, 3)], [], [], [two]),
            ([(6, 3)], [], [], [6]),
            ([(7, 3)], [], [], [7]),
        ]
        adam(((0,), (1,), (2,), (4,)))
        for block in (0, 1, 2, 4):
            deliver(block)
        send(0, 0, 1)
        send(0, 0, 2)
        for step, (keys, sending, leaving, finished) in enumerate(plan):
            if isinstance(keys, tuple):
                pieces = [held[block][0] for block in keys]
                token, held[keys][0] = join(state["token"][0], pieces, (0, 0))
                state["token"] = (token,)
            else:
                arrived(keys, leaving)
            for block in leaving:
                deliver(block)
            for key in sending:
                send(*key)
            if not step:
                adam(((3,), (5,), (6,), (7,)), LATER_LIMIT)
                deliver(5)
                deliver(3)
            for block in finished:
                multiply(block)
    else:
        for pair in range(0, shards, 2):
            adam(((pair,), (pair + 1,)))
        for block in range(shards):
            deliver(block)
            for number in range(len(bits)):
                bit = bits[(number + block) % len(bits)]
                for member in list(held[block]):
                    send(block, member, bit)
            multiply(block)
    out = state["out"][0]
    return (*state["adam"], out.reshape(hidden.shape[:2] + out.shape))


def solution(mesh):
    weights = P(None, "replica", "shard")
    tokens = P("replica", "shard", None, None)
    return jax.shard_map(
        functools.partial(body, mesh.shape["shard"], mesh.shape["replica"]),
        mesh=mesh,
        in_specs=(weights, weights, weights, weights, tokens, P(), P()),
        out_specs=(weights, weights, weights, tokens),
        check_vma=False,
    )
```

```python
import collections
import functools
import math

import jax
import jax.numpy as jnp
from jax import lax
from jax.experimental import pallas as pl
from jax.experimental.pallas import tpu as pltpu
from jax.sharding import PartitionSpec as P

QB = 128
GROUP = 32
VMEM_LIMIT = 60 * 1024 * 1024
LATER_LIMIT = 52 * 1024 * 1024
PRODUCT_LIMIT = 16 * 1024 * 1024

beta_one = 0.9
beta_two = 0.95
learn_rate = 0.004
adam_epsilon = 1e-08
step_count = 10.0
quant_limit = 448.0
scale_epsilon = 1e-06
first_fix = 1.0 - beta_one**step_count
second_fix = 1.0 - beta_two**step_count
second_root = second_fix**0.5
step_size = learn_rate / first_fix * second_root
root_epsilon = adam_epsilon * second_root

TOKEN = (132 * 1024, 128)
PLANNED = (4, 8)
WHOLE = pl.BlockSpec(memory_space=pl.ANY)
SMALL_COST = pl.CostEstimate(flops=0, bytes_accessed=65536, transcendentals=0)


def like(array):
    return jax.ShapeDtypeStruct(array.shape, array.dtype)


def fence_kernel(*refs):
    pass


def fence(arrays):
    return pl.pallas_call(
        fence_kernel,
        in_specs=[WHOLE] * len(arrays),
        out_specs=[WHOLE] * len(arrays),
        out_shape=[like(array) for array in arrays],
        input_output_aliases={i: i for i in range(len(arrays))},
        compiler_params=pltpu.CompilerParams(vmem_limit_bytes=1024 * 1024),
        cost_estimate=SMALL_COST,
        name="arrival_order",
    )(*arrays)


def adam_kernel(groups, passed, owner, *refs):
    arrays, outs = refs[:4], refs[4 + passed : 7 + passed]
    sends = refs[7 + passed : 7 + passed + len(groups)]
    order = [number for group in groups for number in group]
    blocks = len(order)
    *buffers, semaphores = refs[-9:]
    master, gradient, first, second, new_master, new_first, new_second, sent = buffers
    experts, rows, columns = arrays[0].shape
    shard = lax.axis_index("shard")
    bands = rows // QB
    starts = range(0, columns, QB)

    def copies(chunk, inward):
        n, i = chunk // bands, chunk % bands
        number, expert = jnp.int32(order[0]), jnp.int32(0)
        for position in range(1, blocks):
            number = jnp.where(n == position, order[position], number)
        for candidate in range(experts):
            expert = jnp.where(owner[candidate] == shard ^ number, candidate, expert)
        span = pl.ds(pl.multiple_of(i * QB, QB), QB)
        for k, ref in enumerate(arrays if inward else outs):
            far, near = ref.at[expert, span], buffers[k if inward else 4 + k].at[n, span]
            pair = (far, near) if inward else (near, far)
            yield pltpu.make_async_copy(*pair, semaphores.at[chunk, k if inward else 4 + k])

    def send_copy(chunk, group, member):
        span = pl.ds(pl.multiple_of(chunk % bands * QB, QB), QB)
        n = order.index(groups[group][member])
        far = sends[group].at[member, span]
        return pltpu.make_async_copy(sent.at[n, span], far, semaphores.at[chunk, 7])

    def begin(chunk, carry):
        for copy in copies(chunk, True):
            copy.start()
        return carry

    def work(chunk, carry):
        for copy in copies(chunk, True):
            copy.wait()
        n, i = chunk // bands, chunk % bands

        def span(group):
            return pl.ds(pl.multiple_of(i * QB + group * GROUP, GROUP), GROUP)

        def update(group, peaks):
            found = []
            for start, peak in zip(starts, peaks):
                at = (n, span(group), slice(start, start + QB))
                grad = gradient[at].astype(jnp.float32)
                moment_one = beta_one * first[at].astype(jnp.float32) + (1.0 - beta_one) * grad
                moment_two = beta_two * second[at].astype(jnp.float32) + (
                    ((1.0 - beta_two) * grad) * grad
                )
                new_first[at] = moment_one.astype(jnp.bfloat16)
                new_second[at] = moment_two.astype(jnp.bfloat16)
                guess = lax.rsqrt(moment_two)
                root = moment_two * guess + root_epsilon
                inverse = guess * (2.0 - root * guess)
                updated = master[at] - (step_size * moment_one) * inverse
                new_master[at] = updated
                sizes = jnp.abs(updated).reshape(GROUP // 8, 8, QB)
                found.append(jnp.maximum(peak, jnp.max(sizes, axis=0)))
            return tuple(found)

        empty = tuple(jnp.zeros((8, QB), jnp.float32) for _ in starts)
        peaks = lax.fori_loop(0, QB // GROUP, update, empty)
        peaks = [jnp.max(peak, axis=0, keepdims=True) for peak in peaks]
        largest = jnp.max(jnp.concatenate(peaks, axis=0), axis=1, keepdims=True)
        scale = ((largest + scale_epsilon) * (1.0 / quant_limit)).astype(jnp.bfloat16)
        scale = jnp.broadcast_to(scale, (len(peaks), QB))
        inverse_scale = 1.0 / scale.astype(jnp.float32)

        def quantize(group, carry):
            for block, start in enumerate(starts):
                at = (n, span(group), slice(start, start + QB))
                one = slice(block, block + 1)
                quantized = (new_master[at] * inverse_scale[one]).astype(jnp.bfloat16)
                sent[at] = quantized * scale[one]
            return carry

        lax.fori_loop(0, QB // GROUP, quantize, 0)
        for copy in copies(chunk, False):
            copy.start()
        for group, numbers in enumerate(groups):
            for member, number in enumerate(numbers):

                @pl.when(n == order.index(number))
                def _():
                    send_copy(chunk, group, member).start()

        return carry

    def finish(chunk, carry):
        for copy in copies(chunk, False):
            copy.wait()
        send_copy(chunk, 0, 0).wait()
        return carry

    for part in (begin, work, finish):
        lax.fori_loop(0, blocks * bands, part, 0)


def adam_blocks(groups, owner, arrays, carried, token, fenced, limit):
    _, rows, columns = arrays[0].shape
    blocks, passed = sum(map(len, groups)), len(carried) + len(token)
    made = [like(arrays[0]), like(arrays[2]), like(arrays[3])]
    made += [jax.ShapeDtypeStruct((len(group), rows, columns), jnp.bfloat16) for group in groups]
    aliases = {5 + i: i for i in range(len(carried))}
    if token:
        aliases[5 + len(carried)] = len(made)
    made += [jax.ShapeDtypeStruct(TOKEN, jnp.float32)] * fenced
    kinds = [jnp.float32, jnp.bfloat16, jnp.bfloat16, jnp.bfloat16] * 2
    results = pl.pallas_call(
        functools.partial(adam_kernel, groups, passed),
        in_specs=[pl.BlockSpec(memory_space=pltpu.SMEM)] + [WHOLE] * (4 + passed),
        out_specs=[WHOLE] * len(made),
        out_shape=made,
        scratch_shapes=[pltpu.VMEM((blocks, rows, columns), kind) for kind in kinds]
        + [pltpu.SemaphoreType.DMA((blocks * (rows // QB), 8))],
        input_output_aliases=aliases,
        compiler_params=pltpu.CompilerParams(vmem_limit_bytes=limit),
        cost_estimate=SMALL_COST,
        name="adam_quantize",
    )(owner, *arrays, *carried, *token)
    return results[:3], results[3 : 3 + len(groups)], tuple(results[3 + len(groups) :])


def join_kernel(picks, *refs):
    out, semaphores = refs[-2:]
    pieces = [
        pltpu.make_async_copy(refs[1 + place].at[pick], out.at[place], semaphores.at[place])
        for place, pick in enumerate(picks)
    ]
    for piece in pieces:
        piece.start()
    for piece in pieces:
        piece.wait()


def join(token, arrays, picks):
    count = len(arrays)
    shape = jax.ShapeDtypeStruct((count, *arrays[0].shape[1:]), arrays[0].dtype)
    return pl.pallas_call(
        functools.partial(join_kernel, picks),
        in_specs=[WHOLE] * (1 + count),
        out_specs=[WHOLE] * 2,
        out_shape=[like(token), shape],
        scratch_shapes=[pltpu.SemaphoreType.DMA((count,))],
        input_output_aliases={0: 0},
        compiler_params=pltpu.CompilerParams(vmem_limit_bytes=1024 * 1024),
        cost_estimate=SMALL_COST,
        name="join_blocks",
    )(token, *arrays)


def product_kernel(slabs, sources, places, left, *refs):
    out = refs[-1]
    rows, breadth = refs[0].shape[1], out.shape[1]
    parts = [left[:, pl.ds(pl.multiple_of(places[i] * rows, QB), rows)] for i in range(slabs)]
    block = pl.program_id(0)
    span = pl.ds(pl.multiple_of(pl.program_id(1) * breadth, QB), breadth)
    total = jnp.dot(
        jnp.concatenate(parts, axis=1),
        jnp.concatenate([right[block, :, span] for right in refs[:slabs]], axis=0),
        preferred_element_type=jnp.float32,
    )
    out[...] = total.astype(out.dtype)


def product(numbers, sources, places, token_rows, weights, breadth, carried, token):
    slabs = len(weights)
    tokens, units = token_rows.shape
    blocks, rows, columns = weights[0].shape
    passed = len(token) + len(carried)
    tile = math.gcd(columns, 2 * QB)

    def place(block, i, sources, places):
        number = numbers[0] + block * (numbers[-1] - numbers[0])
        return 0, sources[number] * (columns // tile) + i

    *token, out = pl.pallas_call(
        functools.partial(product_kernel, slabs),
        grid_spec=pltpu.PrefetchScalarGridSpec(
            num_scalar_prefetch=2,
            grid=(blocks, columns // tile),
            in_specs=[pl.BlockSpec(memory_space=pltpu.VMEM)] * (1 + slabs) + [WHOLE] * passed,
            out_specs=[WHOLE] * len(token)
            + [pl.BlockSpec((tokens, tile), place)],
        ),
        out_shape=[like(array) for array in token]
            + [jax.ShapeDtypeStruct((tokens, breadth), jnp.bfloat16)],
        input_output_aliases={3 + slabs + i: i for i in range(passed)},
        compiler_params=pltpu.CompilerParams(vmem_limit_bytes=PRODUCT_LIMIT),
        cost_estimate=SMALL_COST,
        name="expert_product",
    )(sources, places, token_rows, *weights, *token, *carried)
    return (out,), tuple(token)


def swap(value, axis, size, mask):
    return lax.ppermute(value, axis, [(i, i ^ mask) for i in range(size)])


def body(shards, replicas, *arguments):
    *arrays, hidden, owner_of_expert, slab_order = arguments
    shard = lax.axis_index("shard").astype(jnp.int32)
    replica = lax.axis_index("replica").astype(jnp.int32)
    token_rows = hidden.reshape(hidden.shape[2:])
    breadth = arrays[0].shape[2] * shards
    bits = [1 << i for i in range((replicas - 1).bit_length())]
    members = jnp.arange(replicas, dtype=jnp.int32)
    sources = shard ^ jnp.arange(shards, dtype=jnp.int32)
    places = jnp.sum(
        jnp.where((replica ^ members)[:, None] == members[None, :], slab_order[None, :], 0), axis=1
    ).astype(jnp.int32)

    fenced = (replicas, shards) == PLANNED
    held, made = collections.defaultdict(dict), {}
    state = {"adam": (), "token": (), "out": ()}

    def adam(groups, limit=VMEM_LIMIT):
        state["adam"], sends, state["token"] = adam_blocks(
            groups, owner_of_expert, arrays, tuple(state["adam"]), state["token"], fenced, limit
        )
        made.update({group[0]: send for group, send in zip(groups, sends)})

    def deliver(block):
        held[block][0] = swap(made[block], "shard", shards, block) if block else made[block]

    def send(block, member, bit):
        held[block][member ^ bit] = swap(held[block][member], "replica", replicas, bit)

    def arrived(keys, leaving=()):
        waiting = [held[b][m] for b, m in keys] + [made[b] for b in leaving]
        token, *passed = fence([*state["token"], *waiting])
        state["token"] = (token,)
        made.update(zip(leaving, passed[len(keys) :]))
        for (block, member), array in zip(keys, passed):
            held[block][member] = array

    def multiply(block):
        ordered = [held[block][member] for member in range(replicas)]
        numbers = block if isinstance(block, tuple) else (block,)
        state["out"], state["token"] = product(
            numbers, sources, places, token_rows, ordered, breadth, state["out"], state["token"]
        )

    if fenced:
        one, two = (2, 4), (3, 5)
        plan = [
            ([(0, 1), (0, 2), (1, 0)], [(1, 0, 1), (1, 0, 2), (0, 1, 2)], [], []),
            ([(2, 0), (4, 0)], [], [], []),
            ([(1, 1), (1, 2)], [(1, 2, 1)], [], []),
            ([(1, 3)], [], [], []),
            (one, [(one, 0, 1), (one, 0, 2)], [], [1]),
            ([(0, 3)], [], [], [0]),
            ([(3, 0), (5, 0)], [], [6], []),
            (two, [(two, 0, 1), (two, 0, 2)], [], []),
            ([(6, 0), (one, 1), (one, 2)], [(one, 1, 2)], [7], []),
            ([(two, 1), (two, 2)], [(two, 2, 1), (6, 0, 1), (6, 0, 2)], [], []),
            ([(7, 0)], [(7, 0, 1), (7, 0, 2)], [], []),
            ([(one, 3), (6, 1), (6, 2)], [(6, 1, 2)], [], []),
            ([(7, 1), (7, 2)], [(7, 2, 1)], [], [one]),
            ([(two, 3)], [], [], [two]),
            ([(6, 3)], [], [], [6]),
            ([(7, 3)], [], [], [7]),
        ]
        adam(((0,), (1,), (2,), (4,)))
        for block in (0, 1, 2, 4):
            deliver(block)
        send(0, 0, 1)
        send(0, 0, 2)
        for step, (keys, sending, leaving, finished) in enumerate(plan):
            if isinstance(keys, tuple):
                pieces = [held[block][0] for block in keys]
                token, held[keys][0] = join(state["token"][0], pieces, (0, 0))
                state["token"] = (token,)
            else:
                arrived(keys, leaving)
            for block in leaving:
                deliver(block)
            for key in sending:
                send(*key)
            if not step:
                adam(((3,), (5,), (6,), (7,)), LATER_LIMIT)
                deliver(5)
                deliver(3)
            for block in finished:
                multiply(block)
    else:
        for pair in range(0, shards, 2):
            adam(((pair,), (pair + 1,)))
        for block in range(shards):
            deliver(block)
            for number in range(len(bits)):
                bit = bits[(number + block) % len(bits)]
                for member in list(held[block]):
                    send(block, member, bit)
            multiply(block)
    out = state["out"][0]
    return (*state["adam"], out.reshape(hidden.shape[:2] + out.shape))


def solution(mesh):
    weights = P(None, "replica", "shard")
    tokens = P("replica", "shard", None, None)
    return jax.shard_map(
        functools.partial(body, mesh.shape["shard"], mesh.shape["replica"]),
        mesh=mesh,
        in_specs=(weights, weights, weights, weights, tokens, P(), P()),
        out_specs=(weights, weights, weights, tokens),
        check_vma=False,
    )
```
